32 devices in a mesh: dp: 8 (over y, x, core), mp: 4 (over z).
Axes of the slice: x: 2, y: 2, z: 4, core: 2. Of those that a mesh axis runs over, the one named last changes fastest.
Arguments:
- block_input: float32 [8, 8192, 512], P('dp', 'mp'), may hold values from -6 to 6
- ln_gain: float32 [512], replicated, may hold values from 0.1 to 1.9
- ln_bias: float32 [512], replicated, may hold values from -3 to 3
- nu_log: float32 [256], P('mp'), may hold values from -9 to -2.5
- theta_log: float32 [256], P('mp'), may hold values from -4.6 to 1
- gamma_log: float32 [256], P('mp'), may hold values from -4.9 to -0.2
- in_weight: bfloat16 [512, 2, 256], P(None, None, 'mp'), may hold values from -0.25 to 0.25
- out_weight: bfloat16 [2, 256, 512], P(None, 'mp'), may hold values from -0.25 to 0.25
- skip: float32 [512], replicated, may hold values from -4 to 4
- glu_weight: bfloat16 [512, 2, 512], P(None, None, 'mp'), may hold values from -0.25 to 0.25
- glu_bias: bfloat16 [2, 512], P(None, 'mp'), may hold values from -3 to 3
- out_cotangent: float32 [8, 8192, 512], P('dp', 'mp'), may hold values from -6 to 6
Outputs:
- block_output: float32 [8, 8192, 512], P('dp', 'mp')
- grad_input: float32 [8, 8192, 512], P('dp', 'mp')
- grad_ln_gain: float32 [512], replicated
- grad_ln_bias: float32 [512], replicated
- grad_nu_log: float32 [256], P('mp')
- grad_theta_log: float32 [256], P('mp')
- grad_gamma_log: float32 [256], P('mp')
- grad_in_weight: float32 [512, 2, 256], P(None, None, 'mp')
- grad_out_weight: float32 [2, 256, 512], P(None, 'mp')
- grad_skip: float32 [512], replicated
- grad_glu_weight: float32 [512, 2, 512], P(None, None, 'mp')
- grad_glu_bias: float32 [2, 512], P(None, 'mp')
The draws below stay inside these ranges and needn't reach their ends.
All inputs are finite; a program needn't handle non-finite values.
Results may differ from the reference program's by a relative error of at most 0.011.
Values may be sent and summed in bfloat16 or wider, within the bound.
No kernel may reach another device: no remote copies, remote signals or barrier semaphores. Data moves between devices by JAX's collectives and lax.ppermute only.
A program may use at most 192 MiB of HBM per device.

```python
import jax
import jax.numpy as jnp
from jax import lax

D = 512
N = 256
LEN = 8192
SEQS = 8


def decay_logs(key, upper):
    return jax.random.uniform(key, (N,), jnp.float32, -9.0, upper)


def draw_nu_log(key, part):
    upper = -2.5
    return decay_logs(key, upper)


def draw_gamma_log(key, part):
    upper = -2.5
    nu_values = decay_logs(key, upper)
    key = jax.random.fold_in(key, 7)
    radius = jnp.exp(-jnp.exp(nu_values))
    jitter = jax.random.uniform(key, (N,), jnp.float32, -0.7, 0.7)
    return 0.5 * jnp.log(1.0 - radius * radius) + jitter


def steps_of(stream_key, dims, cuts, low, top_value):
    def one(axis_at, blocks):
        steps = jax.random.uniform(jax.random.fold_in(jax.random.fold_in(stream_key, 6), axis_at), (blocks,), jnp.float32, low / len(cuts), top_value / len(cuts))
        return jnp.repeat(jnp.exp(steps), dims[axis_at] // blocks).reshape((-1,) + (1,) * (len(dims) - axis_at - 1))

    loudness = one(*cuts[0])
    for cut in cuts[1:]:
        loudness = loudness * one(*cut)
    return loudness


def noise(rng, dims, scale, reach, split=(), kind=jnp.bfloat16):
    array = jax.random.normal(rng, dims, jnp.float32) * scale
    if len(split) > 0:
        array = steps_of(rng, dims, split, -0.22, 0.18) * array
    return jnp.clip(array, min=-reach, max=reach).astype(kind)


def setup_inputs(seed: int = 0) -> dict:
    streams_of = jax.random.split(jax.random.key(seed), 13)
    return {
        "block_input": noise(streams_of[0], (SEQS, LEN, D), 1.0, 6.0, ((0, 8), (1, 4)), jnp.float32),
        "ln_gain": jnp.clip(1.0 + 0.18 * jax.random.normal(streams_of[1], (D,), jnp.float32), 0.1, 1.9),
        "ln_bias": noise(streams_of[2], (D,), 0.5, 3.0, (), jnp.float32),
        "nu_log": draw_nu_log(jax.random.fold_in(streams_of[12], 71), 0),
        "theta_log": jnp.clip(-4.6 + 5.6 * jax.random.uniform(streams_of[4], (N,), jnp.float32) ** steps_of(streams_of[4], (N,), ((0, 4),), -0.2, 0.2), -4.6, 1.0),
        "gamma_log": draw_gamma_log(jax.random.fold_in(streams_of[12], 71), 0),
        "in_weight": noise(streams_of[6], (D, 2, N), D ** -0.5, 0.25, ((2, 4),)),
        "out_weight": noise(streams_of[7], (2, N, D), (2 * N) ** -0.5, 0.25, ((1, 4),)),
        "skip": noise(streams_of[8], (D,), 1.0, 4.0, (), jnp.float32),
        "glu_weight": noise(streams_of[9], (D, 2, D), D ** -0.5, 0.25, ((2, 4),)),
        "glu_bias": noise(streams_of[10], (2, D), 0.5, 3.0, ((1, 4),)),
        "out_cotangent": noise(streams_of[11], (SEQS, LEN, D), 1.0, 6.0, ((0, 8), (1, 4)), jnp.float32),
    }


@jax.custom_vjp
def low(v):
    return lax.optimization_barrier(v.astype(jnp.bfloat16)).astype(jnp.float32)

@jax.custom_vjp
def low_back(v):
    return v

def low_keep(v):
    return (low(v), None)

def low_pass(kept, grad):
    return (grad,)

def back_keep(v):
    return (v, None)

def back_low(kept, grad):
    return (low(grad),)
low.defvjp(low_keep, low_pass)
low_back.defvjp(back_keep, back_low)
EPS = 1e-05
HIGH = lax.Precision.HIGHEST

def combine_pair(earlier, later):
    ar1, ai1, br1, bi1 = earlier
    ar2, ai2, br2, bi2 = later
    return (ar2 * ar1 - ai2 * ai1, ar2 * ai1 + ai2 * ar1, ar2 * br1 - ai2 * bi1 + br2, ar2 * bi1 + ai2 * br1 + bi2)

def recurrence(lam_re, lam_im, src_re, src_im):
    power_re = jnp.broadcast_to(lam_re, src_re.shape)
    power_im = jnp.broadcast_to(lam_im, src_re.shape)
    result = lax.associative_scan(combine_pair, (power_re, power_im, src_re, src_im), axis=0)
    return (result[2], result[3])

def normalize(rows, gain, bias):
    mean = lax.optimization_barrier(jnp.mean(rows, -1, keepdims=True))
    centred = rows - mean
    var = lax.optimization_barrier(jnp.mean(centred * centred, -1, keepdims=True))
    return centred * lax.rsqrt(var + EPS) * gain + bias

def decay(nu_log, theta_log):
    radius = jnp.exp(-jnp.exp(nu_log))
    turn = jnp.exp(theta_log)
    return (radius * jnp.cos(turn), radius * jnp.sin(turn))

def forward_sequence(rows, ln_gain, ln_bias, nu_log, theta_log, gamma_log, in_weight, out_weight, skip, glu_weight, glu_bias):
    width = rows.shape[1]
    states = nu_log.shape[0]
    normed = normalize(rows, ln_gain, ln_bias)
    normed_low = low(normed)
    drive = low_back(jnp.dot(normed_low, in_weight.reshape(width, 2 * states), precision=HIGH, preferred_element_type=jnp.float32))
    gamma = jnp.exp(gamma_log)
    lam_re, lam_im = decay(nu_log, theta_log)
    state_re, state_im = recurrence(lam_re, lam_im, drive[:, :states] * gamma, drive[:, states:] * gamma)
    state_low = low(jnp.concatenate([state_re, state_im], 1))
    c_stack = jnp.concatenate([out_weight[0], -out_weight[1]], 0)
    mixed = low_back(jnp.dot(state_low, c_stack, precision=HIGH, preferred_element_type=jnp.float32))
    lru_out = mixed + skip * normed
    act_low = low(jax.nn.gelu(lru_out, approximate=False))
    pre = low_back(jnp.dot(act_low, glu_weight.reshape(width, 2 * width), precision=HIGH, preferred_element_type=jnp.float32) + glu_bias.reshape(2 * width))
    branch = pre[:, :width] * jax.nn.sigmoid(pre[:, width:])
    return rows + low(low_back(branch))

def reference(block_input, ln_gain, ln_bias, nu_log, theta_log, gamma_log, in_weight, out_weight, skip, glu_weight, glu_bias, out_cotangent):
    params = (ln_gain, ln_bias, nu_log, theta_log, gamma_log, in_weight.astype(jnp.float32), out_weight.astype(jnp.float32), skip, glu_weight.astype(jnp.float32), glu_bias.astype(jnp.float32))

    def one_sequence(carry, item):
        rows, cot = item
        output, back_fn = jax.vjp(forward_sequence, rows, *params)
        grads = back_fn(cot)
        carry = tuple((total + piece for total, piece in zip(carry, grads[1:])))
        return (carry, (output, grads[0]))
    init = tuple((jnp.zeros(p.shape, jnp.float32) for p in params))
    totals, (block_output, grad_input) = lax.scan(one_sequence, init, (block_input, out_cotangent))
    return (block_output, grad_input, totals[0], totals[1], totals[2], totals[3], totals[4], totals[5], totals[6], totals[7], totals[8], totals[9])
```

```python
from functools import partial

import jax
import jax.numpy as jnp
from jax import lax
from jax.experimental import pallas as pl
from jax.experimental.pallas import tpu as pltpu
from jax.sharding import PartitionSpec as P

EPS = 1e-05
F32 = jnp.float32
BF16 = jnp.bfloat16
CHUNKS = 16
STEP_ROWS = 256
PARAM_ROWS = 16
VMEM_LIMIT = 56 * 1024 * 1024
INV_SQRT2 = 0.7071067811865476
INV_SQRT_2PI = 0.3989422804014327


def nt(a, b):
    return lax.dot_general(a, b, (((1,), (1,)), ((), ())), preferred_element_type=F32)


def nn(a, b):
    return lax.dot_general(a, b, (((1,), (0,)), ((), ())), preferred_element_type=F32)


def tn(a, b):
    return lax.dot_general(a, b, (((0,), (0,)), ((), ())), preferred_element_type=F32)


def cmul(ar, ai, br, bi):
    return ar * br - ai * bi, ar * bi + ai * br


def cpower(re, im, log2):
    for _ in range(log2):
        re, im = cmul(re, im, re, im)
    return re, im


def log2_of(n):
    return n.bit_length() - 1


def assemble(dst, dst_row, own, other, src_row, rows, me, core, slots, negate_second):
    for slot in range(slots):
        for part in range(2):
            place = pl.ds(dst_row + (part * slots + slot) * rows, rows)
            mine = own[me ^ slot, pl.ds(src_row, rows), :]
            theirs = other[me ^ slot, pl.ds(src_row, rows), :]
            value = jnp.where(core == part, mine, theirs)
            dst[place, :] = -value if negate_second and part == 1 else value


def forward_first(
    chunk, mp, idx, x_ref, gain_ref, bias_ref, own_ref, other_ref,
    xhat_ref, rstd_ref, src_ref, wt_ref, par_ref, ends_ref, last_ref, h_ref, norm_ref, drive_ref,
):
    step = pl.program_id(0)
    width = x_ref.shape[2]
    states = width // 2
    per = x_ref.shape[1]
    ns = states // mp

    @pl.when(step == 0)
    def _():
        me, core = idx[0], idx[1]
        assemble(wt_ref, 0, own_ref, other_ref, 0, ns, me, core, mp, False)
        total = own_ref[0, 2 * 0 + ns : ns + PARAM_ROWS, :].astype(F32)
        for s in range(1, mp):
            total = total + own_ref[s, ns : ns + PARAM_ROWS, :].astype(F32)
        lam = total[0:1] + total[1:2] + total[2:3]
        gam = total[3:4] + total[4:5] + total[5:6]
        re, im = lam[:, :states], lam[:, states:]
        lre, lim = cpower(re, im, log2_of(chunk))
        tre, tim = cpower(lre, lim, log2_of(CHUNKS))
        par_ref[0:1, :] = lam
        par_ref[1:2, :] = gam
        par_ref[2:3, :] = jnp.concatenate([lre, lim], 1)
        par_ref[3:5, :] = total[6:8]
        pre, pim = jnp.ones_like(tre), jnp.zeros_like(tim)
        for s in range(mp):
            par_ref[8 + s : 9 + s, :] = jnp.concatenate([pre, pim], 1)
            pre, pim = cmul(pre, pim, tre, tim)
        h_ref[...] = jnp.zeros_like(h_ref)

    x = jnp.swapaxes(x_ref[...], 0, 1).reshape(per * CHUNKS, width)
    gain, bias = gain_ref[...], bias_ref[...]
    for r in range(0, per * CHUNKS, 16):
        rows = x[r : r + 16]
        mean = jnp.mean(rows, -1, keepdims=True)
        cen = rows - mean
        var = jnp.mean(cen * cen, -1, keepdims=True)
        rstd = lax.rsqrt(var + EPS)
        xhat = cen * rstd
        xhat_ref[r : r + 16, :] = xhat
        rstd_ref[r : r + 16, :] = jnp.broadcast_to(rstd, (16, 128))
        norm_ref[r : r + 16, :] = (xhat * gain + bias).astype(BF16)
    drive_ref[...] = nt(norm_ref[...], wt_ref[...])
    gam = par_ref[1:2, :]
    lre, lim = par_ref[0:1, :states], par_ref[0:1, states:]
    hre, him = h_ref[:, :states], h_ref[:, states:]
    for k in range(per):
        rows = pl.ds(k * CHUNKS, CHUNKS)
        src = drive_ref[rows, :] * gam
        src_ref[rows, :] = src
        hre, him = (
            src[:, :states] + lre * hre - lim * him,
            src[:, states:] + lre * him + lim * hre,
        )
    h_ref[:, :states] = hre
    h_ref[:, states:] = him

    @pl.when(step == pl.num_programs(0) - 1)
    def _():
        ends_ref[...] = h_ref[...]
        pre, pim = par_ref[2:3, :states], par_ref[2:3, states:]
        re, im = h_ref[0:1, :states], h_ref[0:1, states:]
        for c in range(1, CHUNKS):
            mre, mim = cmul(pre, pim, re, im)
            re, im = mre + h_ref[c : c + 1, :states], mim + h_ref[c : c + 1, states:]
        last_ref[...] = jnp.broadcast_to(jnp.concatenate([re, im], 1), last_ref.shape)


def gelu_parts(v):
    cdf = 0.5 * (1.0 + lax.erf(v * INV_SQRT2))
    pdf = jnp.exp(-0.5 * v * v) * INV_SQRT_2PI
    return v * cdf, cdf + v * pdf


def middle(
    mp, idx, x_ref, cot_ref, xhat_ref, src_ref, par_ref, ends_ref, gain_ref, bias_ref, skip_ref, own_ref, other_ref,
    *rest,
):
    others = rest[: mp - 1]
    (
        y_ref, state_ref, glru_ref, gs_ref, gglu_ref, gout_ref, adj_ref, first_ref, vec_ref,
        w_ref, h_ref, p_ref, mix_ref, act_ref, slope_ref, pre_ref, gpre_ref, gmix_ref, br_ref,
    ) = rest[mp - 1 :]
    step = pl.program_id(0)
    width = x_ref.shape[2]
    states = width // 2
    per = x_ref.shape[1]
    rows_all = per * CHUNKS
    ns = states // mp
    hid = width // mp
    me, core = idx[0], idx[1]

    @pl.when(step == 0)
    def _():
        assemble(w_ref, 0, own_ref, other_ref, 0, ns, me, core, mp, True)
        assemble(w_ref, width, own_ref, other_ref, ns, hid, me, core, mp, False)
        re = jnp.zeros((1, states), F32)
        im = jnp.zeros((1, states), F32)
        for s in range(1, mp):
            j = me ^ s
            power = jnp.maximum(me - 1 - j, 0)
            row = par_ref[pl.ds(8 + power, 1), :]
            sre, sim = cmul(row[:, :states], row[:, states:], others[s - 1][0:1, :states], others[s - 1][0:1, states:])
            keep = (j < me).astype(F32)
            re, im = re + keep * sre, im + keep * sim
        lre, lim = par_ref[2:3, :states], par_ref[2:3, states:]
        for c in range(CHUNKS):
            h_ref[c : c + 1, :states] = re
            h_ref[c : c + 1, states:] = im
            mre, mim = cmul(lre, lim, re, im)
            re, im = mre + ends_ref[c : c + 1, :states], mim + ends_ref[c : c + 1, states:]
        p_ref[:, :states] = jnp.ones((8, states), F32)
        p_ref[:, states:] = jnp.zeros((8, states), F32)
        adj_ref[...] = jnp.zeros_like(adj_ref)
        gglu_ref[...] = jnp.zeros_like(gglu_ref)
        gout_ref[...] = jnp.zeros_like(gout_ref)
        vec_ref[...] = jnp.zeros_like(vec_ref)

    lre, lim = par_ref[0:1, :states], par_ref[0:1, states:]
    hre, him = h_ref[:, :states], h_ref[:, states:]
    for k in range(per):
        rows = pl.ds(k * CHUNKS, CHUNKS)
        hre, him = (
            src_ref[rows, :states] + lre * hre - lim * him,
            src_ref[rows, states:] + lre * him + lim * hre,
        )
        state_ref[rows, :states] = hre.astype(BF16)
        state_ref[rows, states:] = him.astype(BF16)
    h_ref[:, :states] = hre
    h_ref[:, states:] = him

    mix_ref[...] = nn(state_ref[...], w_ref[0:width, :])
    for r in range(0, rows_all, 16):
        for c in range(0, width, 128):
            cols = slice(c, c + 128)
            normed = xhat_ref[r : r + 16, cols] * gain_ref[:, cols] + bias_ref[:, cols]
            lru = mix_ref[r : r + 16, cols] + skip_ref[:, cols] * normed
            act, slope = gelu_parts(lru)
            act_ref[r : r + 16, cols] = act.astype(BF16)
            slope_ref[r : r + 16, cols] = slope
    pre_ref[...] = nt(act_ref[...], w_ref[width:, :])
    cot = jnp.swapaxes(cot_ref[...], 0, 1).reshape(rows_all, width)
    for c in range(0, width, 128):
        cols = slice(c, c + 128)
        gate_cols = slice(width + c, width + c + 128)
        sum_value = jnp.zeros((16, 128), F32)
        sum_gate = jnp.zeros((16, 128), F32)
        for r in range(0, rows_all, 16):
            value = pre_ref[r : r + 16, cols] + par_ref[3:4, cols]
            gate = pre_ref[r : r + 16, gate_cols] + par_ref[4:5, cols]
            sig = 0.5 * jnp.tanh(0.5 * gate) + 0.5
            branch = value * sig
            br_ref[r : r + 16, cols] = branch.astype(BF16).astype(F32)
            g = cot[r : r + 16, cols].astype(BF16).astype(F32)
            g_value = (g * sig).astype(BF16)
            g_gate = (g * branch * (1.0 - sig)).astype(BF16)
            gpre_ref[r : r + 16, cols] = g_value
            gpre_ref[r : r + 16, gate_cols] = g_gate
            sum_value = sum_value + g_value.astype(F32)
            sum_gate = sum_gate + g_gate.astype(F32)
        vec_ref[1:2, cols] += jnp.sum(sum_value, 0, keepdims=True)
        vec_ref[2:3, cols] += jnp.sum(sum_gate, 0, keepdims=True)
    y_ref[...] = x_ref[...] + jnp.swapaxes(br_ref[...].reshape(per, CHUNKS, width), 0, 1)
    gglu_ref[...] += tn(gpre_ref[...], act_ref[...])
    mix_ref[...] = nn(gpre_ref[...], w_ref[width:, :])
    for c in range(0, width, 128):
        cols = slice(c, c + 128)
        total = jnp.zeros((16, 128), F32)
        for r in range(0, rows_all, 16):
            normed = xhat_ref[r : r + 16, cols] * gain_ref[:, cols] + bias_ref[:, cols]
            g_lru = mix_ref[r : r + 16, cols] * slope_ref[r : r + 16, cols]
            glru_ref[r : r + 16, cols] = g_lru
            gmix_ref[r : r + 16, cols] = g_lru.astype(BF16)
            total = total + g_lru * normed
        vec_ref[0:1, cols] += jnp.sum(total, 0, keepdims=True)
    gout_ref[...] += tn(state_ref[...], gmix_ref[...])
    gs_ref[...] = nt(gmix_ref[...], w_ref[0:width, :])
    pre, pim = p_ref[:, :states], p_ref[:, states:]
    are = [adj_ref[c : c + 8, :states] for c in range(0, CHUNKS, 8)]
    aim = [adj_ref[c : c + 8, states:] for c in range(0, CHUNKS, 8)]
    for k in range(per):
        for n, c in enumerate(range(0, CHUNKS, 8)):
            rows = pl.ds(k * CHUNKS + c, 8)
            gre, gim = gs_ref[rows, :states], gs_ref[rows, states:]
            mre, mim = cmul(pre, pim, gre, gim)
            are[n], aim[n] = are[n] + mre, aim[n] + mim
        pre, pim = pre * lre + pim * lim, pim * lre - pre * lim
    for n, c in enumerate(range(0, CHUNKS, 8)):
        adj_ref[c : c + 8, :states] = are[n]
        adj_ref[c : c + 8, states:] = aim[n]
    p_ref[:, :states] = pre
    p_ref[:, states:] = pim

    @pl.when(step == pl.num_programs(0) - 1)
    def _():
        lre, lim = par_ref[2:3, :states], -par_ref[2:3, states:]
        last = CHUNKS - 1
        re, im = adj_ref[last : last + 1, :states], adj_ref[last : last + 1, states:]
        for c in range(CHUNKS - 2, -1, -1):
            mre, mim = cmul(lre, lim, re, im)
            re, im = mre + adj_ref[c : c + 1, :states], mim + adj_ref[c : c + 1, states:]
        first_ref[...] = jnp.broadcast_to(jnp.concatenate([re, im], 1), first_ref.shape)


def backward_last(
    mp, idx, cot_ref, xhat_ref, rstd_ref, src_ref, state_ref, glru_ref, gs_ref, par_ref, adj_ref,
    gain_ref, bias_ref, skip_ref, wt_ref, *rest,
):
    others = rest[: mp - 1]
    (gx_ref, gin_ref, vec_ref, h_ref, norm_ref, gdrive_ref, gn_ref, dx_ref, lam_ref) = rest[mp - 1 :]
    step = pl.program_id(0)
    width = cot_ref.shape[2]
    states = width // 2
    per = cot_ref.shape[1]
    rows_all = per * CHUNKS
    me = idx[0]

    @pl.when(step == 0)
    def _():
        re = jnp.zeros((1, states), F32)
        im = jnp.zeros((1, states), F32)
        for s in range(1, mp):
            j = me ^ s
            power = jnp.maximum(j - me - 1, 0)
            row = par_ref[pl.ds(8 + power, 1), :]
            sre, sim = cmul(row[:, :states], -row[:, states:], others[s - 1][0:1, :states], others[s - 1][0:1, states:])
            keep = (j > me).astype(F32)
            re, im = re + keep * sre, im + keep * sim
        lre, lim = par_ref[2:3, :states], -par_ref[2:3, states:]
        for c in range(CHUNKS - 1, -1, -1):
            h_ref[c : c + 1, :states] = re
            h_ref[c : c + 1, states:] = im
            mre, mim = cmul(lre, lim, re, im)
            re, im = mre + adj_ref[c : c + 1, :states], mim + adj_ref[c : c + 1, states:]
        gin_ref[...] = jnp.zeros_like(gin_ref)
        vec_ref[...] = jnp.zeros_like(vec_ref)
        lam_ref[...] = jnp.zeros_like(lam_ref)

    lre, lim = par_ref[0:1, :states], par_ref[0:1, states:]
    gam = par_ref[1:2, :states]
    hre, him = h_ref[:, :states], h_ref[:, states:]
    sre, sim = lam_ref[:, :states], lam_ref[:, states : 2 * states]
    sgam = lam_ref[:, 2 * states :]
    for k in range(per - 1, -1, -1):
        rows = pl.ds(k * CHUNKS, CHUNKS)
        tre, tim = state_ref[rows, :states].astype(F32), state_ref[rows, states:].astype(F32)
        sre = sre + (hre * tre + him * tim)
        sim = sim + (him * tre - hre * tim)
        hre, him = (
            gs_ref[rows, :states] + lre * hre + lim * him,
            gs_ref[rows, states:] + lre * him - lim * hre,
        )
        sgam = sgam + (hre * src_ref[rows, :states] + him * src_ref[rows, states:])
        gdrive_ref[rows, :states] = (hre * gam).astype(BF16)
        gdrive_ref[rows, states:] = (him * gam).astype(BF16)
    h_ref[:, :states] = hre
    h_ref[:, states:] = him
    lam_ref[:, :states] = sre
    lam_ref[:, states : 2 * states] = sim
    lam_ref[:, 2 * states :] = sgam

    for r in range(0, rows_all, 16):
        norm_ref[r : r + 16, :] = (xhat_ref[r : r + 16, :] * gain_ref[...] + bias_ref[...]).astype(BF16)
    gin_ref[...] += tn(gdrive_ref[...], norm_ref[...])
    gn_ref[...] = nn(gdrive_ref[...], wt_ref[...])
    sum_gain = jnp.zeros((16, width), F32)
    sum_bias = jnp.zeros((16, width), F32)
    for r in range(0, rows_all, 16):
        rows = slice(r, r + 16)
        xhat = xhat_ref[rows, :]
        g = gn_ref[rows, :] + skip_ref[...] * glru_ref[rows, :]
        sum_gain = sum_gain + g * xhat
        sum_bias = sum_bias + g
        gh = g * gain_ref[...]
        first = jnp.mean(gh, -1, keepdims=True)
        second = jnp.mean(gh * xhat, -1, keepdims=True)
        dx_ref[rows, :] = rstd_ref[rows, 0:1] * (gh - first - xhat * second)
    vec_ref[0:1, :] += jnp.sum(sum_gain, 0, keepdims=True)
    vec_ref[1:2, :] += jnp.sum(sum_bias, 0, keepdims=True)
    gx_ref[...] = cot_ref[...] + jnp.swapaxes(dx_ref[...].reshape(per, CHUNKS, width), 0, 1)

    @pl.when(step == pl.num_programs(0) - 1)
    def _():
        total = jnp.sum(lam_ref[...], 0, keepdims=True)
        vec_ref[2:3, :] = total[:, :width]
        vec_ref[3:4, :] = jnp.concatenate([total[:, 2 * states :], jnp.zeros((1, states), F32)], 1)


def whole(shape):
    return pl.BlockSpec(shape, lambda i, idx: (0,) * len(shape))


def call(kernel, grid, in_specs, out_specs, out_shape, scratch, flops):
    return pl.pallas_call(
        kernel,
        grid_spec=pltpu.PrefetchScalarGridSpec(
            num_scalar_prefetch=1, grid=grid, in_specs=in_specs, out_specs=out_specs, scratch_shapes=scratch
        ),
        out_shape=out_shape,
        compiler_params=pltpu.CompilerParams(vmem_limit_bytes=VMEM_LIMIT),
        cost_estimate=pl.CostEstimate(flops=flops, bytes_accessed=16 * 1024 * 1024, transcendentals=0),
    )


def xor_pairs(n, s):
    return [(i, i ^ s) for i in range(n)]


def from_each(value, axis, n):
    return [value] + [lax.ppermute(value, axis, xor_pairs(n, s)) for s in range(1, n)]


def tree_sum(parts):
    parts = list(parts)
    while len(parts) > 1:
        parts = [parts[i] + parts[i + 1] for i in range(0, len(parts), 2)]
    return parts[0]


def high_low(v):
    high = lax.reduce_precision(v, 8, 7)
    low = lax.reduce_precision(v - high, 8, 7)
    return high, low


def on_device(
    block_input, ln_gain, ln_bias, nu_log, theta_log, gamma_log, in_weight, out_weight, skip, glu_weight, glu_bias,
    out_cotangent,
):
    mp = lax.axis_size("mp")
    dp = lax.axis_size("dp")
    me = lax.axis_index("mp")
    dpi = lax.axis_index("dp")
    core = dpi & 1
    idx = jnp.stack([me, core]).astype(jnp.int32)
    tokens, width = block_input.shape[1:]
    ns = nu_log.shape[0]
    states = ns * mp
    hid = glu_weight.shape[2]
    chunk = tokens // CHUNKS
    per = STEP_ROWS // CHUNKS
    steps = chunk // per
    x = block_input.reshape(CHUNKS, chunk, width)
    cot = out_cotangent.reshape(CHUNKS, chunk, width)
    gain, bias, skp = ln_gain[None], ln_bias[None], skip[None]

    def decay(nu, theta):
        radius = jnp.exp(-jnp.exp(nu))
        turn = jnp.exp(theta)
        return radius * jnp.cos(turn), radius * jnp.sin(turn)

    (lam_re, lam_im), decay_back = jax.vjp(decay, nu_log, theta_log)
    gamma = jnp.exp(gamma_log)

    here = (jnp.arange(mp) == me).astype(F32)[:, None]

    def placed(v):
        return (here * v[None]).reshape(-1)

    def thirds(v):
        high, rest = high_low(v)
        return [high, rest, lax.reduce_precision(v - high - rest, 8, 7)]

    lam_row = jnp.concatenate([placed(lam_re), placed(lam_im)])
    gam_row = jnp.concatenate([placed(gamma), placed(gamma)])
    bias_rows = [placed(glu_bias[p].astype(F32)) for p in range(2)]
    params = jnp.stack(thirds(lam_row) + thirds(gam_row) + bias_rows).astype(BF16)
    params = jnp.pad(params, ((0, PARAM_ROWS - params.shape[0]), (0, 0)))

    in_part = lax.dynamic_index_in_dim(in_weight, core, 1, keepdims=False).T
    out_part = lax.dynamic_index_in_dim(out_weight, core, 0, keepdims=False)
    glu_part = lax.dynamic_index_in_dim(glu_weight, core, 1, keepdims=False).T
    first_own = jnp.stack(from_each(jnp.concatenate([in_part, params]), "mp", mp))
    first_other = lax.ppermute(first_own, "dp", xor_pairs(dp, 1))
    second_own = jnp.stack(from_each(jnp.concatenate([out_part, glu_part]), "mp", mp))
    second_other = lax.ppermute(second_own, "dp", xor_pairs(dp, 1))

    chunked = pl.BlockSpec((CHUNKS, per, width), lambda i, idx: (0, i, 0))
    rowed = pl.BlockSpec((STEP_ROWS, width), lambda i, idx: (i, 0))
    narrow = pl.BlockSpec((STEP_ROWS, 128), lambda i, idx: (i, 0))
    vector = whole((1, width))
    big = jax.ShapeDtypeStruct((tokens, width), F32)
    big_low = jax.ShapeDtypeStruct((tokens, width), BF16)

    def shape(*dims):
        return jax.ShapeDtypeStruct(dims, F32)

    product = 2 * tokens * width * width
    npar = 8 + mp
    xhat, rstd, src, wt, par, ends, last = call(
        partial(forward_first, chunk, mp),
        (steps,),
        [chunked, vector, vector, whole(first_own.shape), whole(first_own.shape)],
        [rowed, narrow, rowed, whole((width, width)), whole((npar, width)), whole((CHUNKS, width)), whole((8, width))],
        [big, shape(tokens, 128), big, jax.ShapeDtypeStruct((width, width), BF16), shape(npar, width),
         shape(CHUNKS, width), shape(8, width)],
        [pltpu.VMEM((CHUNKS, width), F32), pltpu.VMEM((STEP_ROWS, width), BF16), pltpu.VMEM((STEP_ROWS, width), F32)],
        product,
    )(idx, x, gain, bias, first_own, first_other)

    lasts = from_each(last, "mp", mp)[1:]
    small = whole((8, width))
    y, state, glru, gs, gglu, gout, adj, first, vec_mid = call(
        partial(middle, mp),
        (steps,),
        [chunked, chunked, rowed, rowed, whole((npar, width)), whole((CHUNKS, width)), vector, vector, vector,
         whole(second_own.shape), whole(second_own.shape)] + [small] * (mp - 1),
        [chunked, rowed, rowed, rowed, whole((2 * width, width)), whole((width, width)), whole((CHUNKS, width)), small,
         small],
        [shape(CHUNKS, chunk, width), big_low, big, big, shape(2 * width, width), shape(width, width),
         shape(CHUNKS, width), shape(8, width), shape(8, width)],
        [
            pltpu.VMEM((3 * width, width), BF16),
            pltpu.VMEM((CHUNKS, width), F32),
            pltpu.VMEM((8, width), F32),
            pltpu.VMEM((STEP_ROWS, width), F32),
            pltpu.VMEM((STEP_ROWS, width), BF16),
            pltpu.VMEM((STEP_ROWS, width), F32),
            pltpu.VMEM((STEP_ROWS, 2 * width), F32),
            pltpu.VMEM((STEP_ROWS, 2 * width), BF16),
            pltpu.VMEM((STEP_ROWS, width), BF16),
            pltpu.VMEM((STEP_ROWS, width), F32),
        ],
        9 * product,
    )(idx, x, cot, xhat, src, par, ends, gain, bias, skp, second_own, second_other, *lasts)

    firsts = from_each(first, "mp", mp)[1:]

    def back(i, idx):
        return (steps - 1 - i, 0)

    rowed_back = pl.BlockSpec((STEP_ROWS, width), back)
    narrow_back = pl.BlockSpec((STEP_ROWS, 128), back)
    chunked_back = pl.BlockSpec((CHUNKS, per, width), lambda i, idx: (0, steps - 1 - i, 0))
    gx, gin, vec_last = call(
        partial(backward_last, mp),
        (steps,),
        [chunked_back, rowed_back, narrow_back, rowed_back, rowed_back, rowed_back, rowed_back, whole((npar, width)),
         whole((CHUNKS, width)), vector, vector, vector, whole((width, width))] + [small] * (mp - 1),
        [chunked_back, whole((width, width)), small],
        [shape(CHUNKS, chunk, width), shape(width, width), shape(8, width)],
        [
            pltpu.VMEM((CHUNKS, width), F32),
            pltpu.VMEM((STEP_ROWS, width), BF16),
            pltpu.VMEM((STEP_ROWS, width), BF16),
            pltpu.VMEM((STEP_ROWS, width), F32),
            pltpu.VMEM((STEP_ROWS, width), F32),
            pltpu.VMEM((CHUNKS, 3 * states), F32),
        ],
        2 * product,
    )(idx, cot, xhat, rstd, src, state, glru, gs, par, adj, gain, bias, skp, wt, *firsts)

    vec = jnp.concatenate([vec_mid[0:3], vec_last[0:4], jnp.zeros((1, width), F32)])
    grads = jnp.concatenate(
        [gin.reshape(2, mp, ns, width), gout.reshape(2, mp, ns, width), gglu.reshape(2, mp, hid, width)], 2
    )

    def exchange(send, vec, axis, perm):
        high, low = high_low(vec)
        buffer = jnp.concatenate([send.reshape(-1, width).astype(BF16), high.astype(BF16), low.astype(BF16)])
        got = lax.ppermute(buffer, axis, perm)
        n = got.shape[0] - 16
        return got[:n].astype(F32).reshape(send.shape), (
            got[n : n + 8].astype(F32) + got[n + 8 :].astype(F32)
        ), high + low

    bits = log2_of(dp)
    rows = grads
    for b in range(bits):
        bit = (dpi >> b) & 1
        if b > 0:
            half = rows.shape[1] // 2
            rows = rows.reshape(mp, 2, half, width).swapaxes(0, 1)
        keep = lax.dynamic_index_in_dim(rows, bit, 0, keepdims=False)
        send = lax.dynamic_index_in_dim(rows, 1 - bit, 0, keepdims=False)
        got, vec_got, vec_own = exchange(send, vec, "dp", xor_pairs(dp, 1 << b))
        rows, vec = keep + got, vec_own + vec_got
    pieces = [lax.dynamic_index_in_dim(rows, me, 0, keepdims=False)]
    vecs = []
    for s in range(1, mp):
        send = lax.dynamic_index_in_dim(rows, me ^ s, 0, keepdims=False)
        got, vec_got, vec_own = exchange(send, vec, "mp", xor_pairs(mp, s))
        pieces.append(got)
        vecs.append(vec_got)
    vec = tree_sum([vec_own] + vecs)
    piece = tree_sum(pieces).astype(BF16)
    for b in range(bits - 1, -1, -1):
        bit = (dpi >> b) & 1
        other = lax.ppermute(piece, "dp", xor_pairs(dp, 1 << b))
        piece = jnp.where(bit == 0, jnp.stack([piece, other]), jnp.stack([other, piece]))
        if b > 0:
            piece = piece.reshape(-1, width)
    total = piece.astype(F32)

    grad_in_weight = total[:, :ns].transpose(2, 0, 1)
    grad_out = total[:, ns : 2 * ns]
    grad_out_weight = jnp.stack([grad_out[0], -grad_out[1]])
    grad_glu_weight = total[:, 2 * ns :].transpose(2, 0, 1)
    grad_skip = vec[0]
    grad_glu_bias = lax.dynamic_slice_in_dim(vec[1:3], me * hid, hid, 1)
    grad_lam = lax.dynamic_slice_in_dim(vec[5].reshape(2, states), me * ns, ns, 1)
    grad_nu_log, grad_theta_log = decay_back((grad_lam[0], grad_lam[1]))
    grad_gamma_log = lax.dynamic_slice_in_dim(vec[6], me * ns, ns, 0)
    return (
        y.reshape(block_input.shape),
        gx.reshape(block_input.shape),
        vec[3],
        vec[4],
        grad_nu_log,
        grad_theta_log,
        grad_gamma_log,
        grad_in_weight,
        grad_out_weight,
        grad_skip,
        grad_glu_weight,
        grad_glu_bias,
    )


def solution(mesh):
    in_specs = (
        P("dp", "mp", None), P(), P(), P("mp"), P("mp"), P("mp"), P(None, None, "mp"), P(None, "mp", None), P(),
        P(None, None, "mp"), P(None, "mp"), P("dp", "mp", None),
    )
    out_specs = (
        P("dp", "mp", None), P("dp", "mp", None), P(), P(), P("mp"), P("mp"), P("mp"), P(None, None, "mp"),
        P(None, "mp", None), P(), P(None, None, "mp"), P(None, "mp"),
    )
    return jax.shard_map(on_device, mesh=mesh, in_specs=in_specs, out_specs=out_specs, check_vma=False)
```

```python
from functools import partial

import jax
import jax.numpy as jnp
from jax import lax
from jax.experimental import pallas as pl
from jax.experimental.pallas import tpu as pltpu
from jax.sharding import PartitionSpec as P

EPS = 1e-05
F32 = jnp.float32
BF16 = jnp.bfloat16
CHUNKS = 16
STEP_ROWS = 512
BLOCK = 256
PARAM_ROWS = 16
MIB = 1024 * 1024
INV_SQRT2 = 0.7071067811865476
INV_SQRT_2PI = 0.3989422804014327


def nt(a, b):
    return lax.dot_general(a, b, (((1,), (1,)), ((), ())), preferred_element_type=F32)


def nn(a, b):
    return lax.dot_general(a, b, (((1,), (0,)), ((), ())), preferred_element_type=F32)


def tn(a, b):
    return lax.dot_general(a, b, (((0,), (0,)), ((), ())), preferred_element_type=F32)


def cmul(ar, ai, br, bi):
    return ar * br - ai * bi, ar * bi + ai * br


def cpower(re, im, log2):
    for _ in range(log2):
        re, im = cmul(re, im, re, im)
    return re, im


def log2_of(n):
    return n.bit_length() - 1


def block_rows(step, block):
    return pl.ds(pl.multiple_of(step * STEP_ROWS + block * BLOCK, BLOCK), BLOCK)


def tile_rows(step, start):
    return pl.ds(pl.multiple_of(step * STEP_ROWS + start, 16), 16)


def alternate(first, second):
    i = j = 0
    while i < len(first) or j < len(second):
        if j >= len(second) or (i < len(first) and i * len(second) <= j * len(first)):
            first[i]()
            i += 1
        else:
            second[j]()
            j += 1


def run(pieces):
    for piece in pieces:
        piece()


def product_nt(out, left, right, size=256):
    def piece(n):
        out[:, n : n + size] = nt(left(), right[n : n + size, :])

    return [partial(piece, n) for n in range(0, right.shape[0], size)]


def product_nn(out, left, right, size=256):
    def piece(n):
        out[:, n : n + size] = nn(left(), right[:, n : n + size])

    return [partial(piece, n) for n in range(0, right.shape[1], size)]


def product_tn(total, left, right, size=256):
    def piece(n):
        total[n : n + size, :] += tn(left(slice(n, n + size)), right())

    return [partial(piece, n) for n in range(0, total.shape[0], size)]


def assemble(dst, own, other, first, rows, me, core, slots, negate_second):
    for slot in range(slots):
        for part in range(2):
            mine = own[me ^ slot, first : first + rows, :]
            theirs = other[me ^ slot, first : first + rows, :]
            value = jnp.where(core == part, mine, theirs)
            start = (part * slots + slot) * rows
            dst[start : start + rows, :] = -value if negate_second and part == 1 else value


def prepare(idx, x_ref, gain_ref, bias_ref, xhat_ref, norm_ref, rstd_ref):
    step = pl.program_id(0)
    width = x_ref.shape[2]
    per = x_ref.shape[1]
    gain, bias = gain_ref[...], bias_ref[...]
    for k in range(0, per, 8):
        rows = jnp.swapaxes(x_ref[:, k : k + 8, :], 0, 1).reshape(8 * CHUNKS, width)
        for r in range(0, 8 * CHUNKS, 16):
            place = tile_rows(step, k * CHUNKS + r)
            part = rows[r : r + 16]
            mean = jnp.mean(part, -1, keepdims=True)
            cen = part - mean
            var = jnp.mean(cen * cen, -1, keepdims=True)
            rstd = lax.rsqrt(var + EPS)
            xhat = cen * rstd
            xhat_ref[place, :] = xhat
            rstd_ref[place, :] = jnp.broadcast_to(rstd, (16, 128))
            norm_ref[place, :] = (xhat * gain + bias).astype(BF16)


def lower(idx, cot_ref, cotlow_ref):
    step = pl.program_id(0)
    width = cot_ref.shape[2]
    for k in range(0, cot_ref.shape[1], 8):
        rows = jnp.swapaxes(cot_ref[:, k : k + 8, :], 0, 1).reshape(8 * CHUNKS, width)
        place = pl.ds(pl.multiple_of(step * STEP_ROWS + k * CHUNKS, 128), 8 * CHUNKS)
        cotlow_ref[place, :] = rows.astype(BF16)


def first_scan(
    chunk, mp, idx, norm_ref, own_ref, other_ref,
    src_ref, wt_ref, par_ref, ends_ref, last_ref, h_ref, drive_a, drive_b,
):
    step = pl.program_id(0)
    width = norm_ref.shape[1]
    states = width // 2
    ns = states // mp

    @pl.when(step == 0)
    def _():
        me, core = idx[0], idx[1]
        assemble(wt_ref, own_ref, other_ref, 0, ns, me, core, mp, False)
        total = own_ref[0, ns : ns + PARAM_ROWS, :].astype(F32)
        for s in range(1, mp):
            total = total + own_ref[s, ns : ns + PARAM_ROWS, :].astype(F32)
        decay = total[0:1] + total[1:2] + total[2:3]
        gam = jnp.exp(total[3:4] + total[4:5] + total[5:6])
        radius = jnp.exp(-jnp.exp(decay[:, :states]))
        turn = jnp.exp(decay[:, states:])
        re, im = radius * jnp.cos(turn), radius * jnp.sin(turn)
        lre, lim = cpower(re, im, log2_of(chunk))
        tre, tim = cpower(lre, lim, log2_of(CHUNKS))
        par_ref[0:1, :] = jnp.concatenate([re, im], 1)
        par_ref[1:2, :] = gam
        par_ref[2:3, :] = jnp.concatenate([lre, lim], 1)
        par_ref[3:5, :] = total[6:8]
        par_ref[5:8, :] = jnp.zeros((3, width), F32)
        pre, pim = jnp.ones_like(tre), jnp.zeros_like(tim)
        for s in range(mp):
            par_ref[8 + s : 9 + s, :] = jnp.concatenate([pre, pim], 1)
            pre, pim = cmul(pre, pim, tre, tim)
        h_ref[...] = jnp.zeros_like(h_ref)

    gam = par_ref[1:2, :]
    lre, lim = par_ref[0:1, :states], par_ref[0:1, states:]
    h = [h_ref[:, :states], h_ref[:, states:]]

    def drive_pieces(b, drive):
        return product_nt(drive, lambda: norm_ref[block_rows(step, b), :], wt_ref)

    def scan_piece(b, drive, r):
        hre, him = h
        src = drive[r : r + CHUNKS, :] * gam
        src_ref[tile_rows(step, b * BLOCK + r), :] = src
        h[0] = src[:, :states] + lre * hre - lim * him
        h[1] = src[:, states:] + lre * him + lim * hre

    def scan_pieces(b, drive):
        return [partial(scan_piece, b, drive, r) for r in range(0, BLOCK, CHUNKS)]

    run(drive_pieces(0, drive_a))
    alternate(drive_pieces(1, drive_b), scan_pieces(0, drive_a))
    run(scan_pieces(1, drive_b))
    hre, him = h
    h_ref[:, :states] = hre
    h_ref[:, states:] = him

    @pl.when(step == pl.num_programs(0) - 1)
    def _():
        ends_ref[...] = h_ref[...]
        pre, pim = par_ref[2:3, :states], par_ref[2:3, states:]
        re, im = h_ref[0:1, :states], h_ref[0:1, states:]
        for c in range(1, CHUNKS):
            mre, mim = cmul(pre, pim, re, im)
            re, im = mre + h_ref[c : c + 1, :states], mim + h_ref[c : c + 1, states:]
        last_ref[...] = jnp.broadcast_to(jnp.concatenate([re, im], 1), last_ref.shape)


def gelu_parts(v):
    cdf = 0.5 * (1.0 + lax.erf(v * INV_SQRT2))
    pdf = jnp.exp(-0.5 * v * v) * INV_SQRT_2PI
    return v * cdf, cdf + v * pdf


def readout(mp, idx, xhat_ref, src_ref, par_ref, ends_ref, gain_ref, bias_ref, skip_ref, own_ref, other_ref, *rest):
    others = rest[: mp - 1]
    (state_ref, act_ref, slope_ref, wc_ref, h_ref, low_a, low_b, mix_a, mix_b) = rest[mp - 1 :]
    step = pl.program_id(0)
    width = xhat_ref.shape[1]
    states = width // 2
    me, core = idx[0], idx[1]

    @pl.when(step == 0)
    def _():
        assemble(wc_ref, own_ref, other_ref, 0, states // mp, me, core, mp, True)
        re = jnp.zeros((1, states), F32)
        im = jnp.zeros((1, states), F32)
        for s in range(1, mp):
            j = me ^ s
            power = jnp.maximum(me - 1 - j, 0)
            row = par_ref[pl.ds(8 + power, 1), :]
            sre, sim = cmul(row[:, :states], row[:, states:], others[s - 1][0:1, :states], others[s - 1][0:1, states:])
            keep = (j < me).astype(F32)
            re, im = re + keep * sre, im + keep * sim
        lre, lim = par_ref[2:3, :states], par_ref[2:3, states:]
        for c in range(CHUNKS):
            h_ref[c : c + 1, :states] = re
            h_ref[c : c + 1, states:] = im
            mre, mim = cmul(lre, lim, re, im)
            re, im = mre + ends_ref[c : c + 1, :states], mim + ends_ref[c : c + 1, states:]

    lre, lim = par_ref[0:1, :states], par_ref[0:1, states:]
    h = [h_ref[:, :states], h_ref[:, states:]]

    def scan_piece(b, low, r):
        hre, him = h
        rows = tile_rows(step, b * BLOCK + r)
        hre, him = (
            src_ref[rows, :states] + lre * hre - lim * him,
            src_ref[rows, states:] + lre * him + lim * hre,
        )
        low[r : r + CHUNKS, :states] = hre.astype(BF16)
        low[r : r + CHUNKS, states:] = him.astype(BF16)
        state_ref[rows, :] = low[r : r + CHUNKS, :]
        h[0], h[1] = hre, him

    def gelu_piece(b, mix, r):
        rows = tile_rows(step, b * BLOCK + r)
        for c in range(0, width, 128):
            cols = slice(c, c + 128)
            normed = xhat_ref[rows, cols] * gain_ref[:, cols] + bias_ref[:, cols]
            lru = mix[r : r + 16, cols] + skip_ref[:, cols] * normed
            act, slope = gelu_parts(lru)
            act_ref[rows, cols] = act.astype(BF16)
            slope_ref[rows, cols] = slope

    def scans(b, low):
        return [partial(scan_piece, b, low, r) for r in range(0, BLOCK, CHUNKS)]

    def mixes(low, mix):
        return product_nn(mix, lambda: low[...], wc_ref)

    def gelus(b, mix):
        return [partial(gelu_piece, b, mix, r) for r in range(0, BLOCK, 16)]

    run(scans(0, low_a))
    alternate(mixes(low_a, mix_a), scans(1, low_b))
    alternate(mixes(low_b, mix_b), gelus(0, mix_a))
    run(gelus(1, mix_b))
    h_ref[:, :states] = h[0]
    h_ref[:, states:] = h[1]


def add_branch(idx, x_ref, br_ref, y_ref):
    width = x_ref.shape[2]
    for k in range(0, x_ref.shape[1], 8):
        rows = br_ref[k * CHUNKS : (k + 8) * CHUNKS, :].astype(F32).reshape(8, CHUNKS, width)
        y_ref[:, k : k + 8, :] = x_ref[:, k : k + 8, :] + jnp.swapaxes(rows, 0, 1)


def gating(mp, idx, cotlow_ref, act_ref, par_ref, own_ref, other_ref,
           br_ref, gpre_ref, wg_ref, vec_ref, pre_a, pre_b):
    step = pl.program_id(0)
    width = act_ref.shape[1]
    core = idx[1]

    @pl.when(step == 0)
    def _():
        assemble(wg_ref, own_ref, other_ref, width // 2 // mp, width // mp, idx[0], core, mp, False)
        vec_ref[...] = jnp.zeros_like(vec_ref)

    def pre_pieces(block, pre):
        rows = pl.ds(pl.multiple_of(block * BLOCK, BLOCK), BLOCK)
        return product_nt(pre, lambda: act_ref[rows, :], wg_ref)

    @pl.when(step == 0)
    def _():
        run(pre_pieces(0, pre_a))

    sums = {}

    def gate_piece(b, pre, start, c):
        cols = slice(c, c + 128)
        gate_cols = slice(width + c, width + c + 128)
        for r in range(start, start + 64, 16):
            rows = tile_rows(step, b * BLOCK + r)
            value = pre[r : r + 16, cols] + par_ref[3:4, cols]
            gate = pre[r : r + 16, gate_cols] + par_ref[4:5, cols]
            sig = 0.5 * jnp.tanh(0.5 * gate) + 0.5
            branch = value * sig
            br_ref[b * BLOCK + r : b * BLOCK + r + 16, cols] = branch.astype(BF16)
            g = cotlow_ref[rows, cols].astype(F32)
            g_value = (g * sig).astype(BF16)
            g_gate = (g * branch * (1.0 - sig)).astype(BF16)
            gpre_ref[rows, cols] = g_value
            gpre_ref[rows, gate_cols] = g_gate
            for key, part in ((("value", c), g_value), (("gate", c), g_gate)):
                part = part.astype(F32)
                sums[key] = sums[key] + part if key in sums else part

    def gate_pieces(b, pre):
        return [
            partial(gate_piece, b, pre, start, c) for start in range(0, BLOCK, 64) for c in range(0, width, 128)
        ]

    after = jnp.minimum(2 * step + 2, act_ref.shape[0] // BLOCK - 1)
    alternate(pre_pieces(2 * step + 1, pre_b), gate_pieces(0, pre_a))
    alternate(pre_pieces(after, pre_a), gate_pieces(1, pre_b))
    for c in range(0, width, 128):
        vec_ref[1:2, c : c + 128] += jnp.sum(sums["value", c], 0, keepdims=True)
        vec_ref[2:3, c : c + 128] += jnp.sum(sums["gate", c], 0, keepdims=True)


def weight_products(idx, gpre_ref, act_ref, state_ref, gmix_ref, keep_ref, send_ref):
    core = idx[1]

    def product(left_ref, right_ref, first):
        columns = left_ref.shape[1]
        size = columns // 2
        for n in range(0, columns, 256):
            total = tn(left_ref[:, n : n + 256], right_ref[...])
            here = slice(first + n % size, first + n % size + 256)

            @pl.when(core == n // size)
            def _():
                keep_ref[here, :] = total

            @pl.when(core != n // size)
            def _():
                send_ref[here, :] = total.astype(BF16)

    product(gpre_ref, act_ref, 0)
    product(state_ref, gmix_ref, gpre_ref.shape[1] // 2)


def unmix(idx, gpre_ref, slope_ref, norm_ref, wg_ref, wc_ref, par_ref,
          gmix_ref, gs_ref, adj_ref, first_ref, vec_ref, p_ref, ga_a, ga_b, gmix_a, gmix_b, gs_a, gs_b):
    step = pl.program_id(0)
    width = norm_ref.shape[1]
    states = width // 2
    core = idx[1]

    @pl.when(step == 0)
    def _():
        p_ref[:, :states] = jnp.ones((8, states), F32)
        p_ref[:, states:] = jnp.zeros((8, states), F32)
        adj_ref[...] = jnp.zeros_like(adj_ref)
        vec_ref[...] = jnp.zeros_like(vec_ref)

    sums = {}

    def act_pieces(b, ga):
        return product_nn(ga, lambda: gpre_ref[block_rows(step, b), :], wg_ref)

    def lru_piece(b, ga, gmix, r):
        rows = tile_rows(step, b * BLOCK + r)
        for c in range(0, width, 128):
            cols = slice(c, c + 128)
            g_lru = ga[r : r + 16, cols] * slope_ref[rows, cols]
            low = g_lru.astype(BF16)
            gmix[r : r + 16, cols] = low
            gmix_ref[rows, cols] = low
            part = g_lru * norm_ref[rows, cols].astype(F32)
            sums[c] = sums[c] + part if c in sums else part

    def lru_pieces(b, ga, gmix):
        return [partial(lru_piece, b, ga, gmix, r) for r in range(0, BLOCK, 16)]

    def mix_pieces(b, gs, gmix):
        return product_nt(gs, lambda: gmix[...], wc_ref)

    lre, lim = par_ref[0:1, :states], par_ref[0:1, states:]
    power = [p_ref[:, :states], p_ref[:, states:]]
    are = [adj_ref[c : c + 8, :states] for c in range(0, CHUNKS, 8)]
    aim = [adj_ref[c : c + 8, states:] for c in range(0, CHUNKS, 8)]

    def end_piece(b, gs, r):
        pre, pim = power
        for n, c in enumerate(range(0, CHUNKS, 8)):
            gre, gim = gs[r + c : r + c + 8, :states], gs[r + c : r + c + 8, states:]
            mre, mim = cmul(pre, pim, gre, gim)
            are[n], aim[n] = are[n] + mre, aim[n] + mim
        gs_ref[tile_rows(step, b * BLOCK + r), :] = gs[r : r + CHUNKS, :]
        power[0], power[1] = pre * lre + pim * lim, pim * lre - pre * lim

    def end_pieces(b, gs):
        return [partial(end_piece, b, gs, r) for r in range(0, BLOCK, CHUNKS)]

    run(act_pieces(0, ga_a))
    alternate(act_pieces(1, ga_b), lru_pieces(0, ga_a, gmix_a))
    alternate(mix_pieces(0, gs_a, gmix_a), lru_pieces(1, ga_b, gmix_b))
    alternate(mix_pieces(1, gs_b, gmix_b), end_pieces(0, gs_a))
    run(end_pieces(1, gs_b))
    for c in range(0, width, 128):
        vec_ref[0:1, c : c + 128] += jnp.sum(sums[c], 0, keepdims=True)
    for n, c in enumerate(range(0, CHUNKS, 8)):
        adj_ref[c : c + 8, :states] = are[n]
        adj_ref[c : c + 8, states:] = aim[n]
    p_ref[:, :states] = power[0]
    p_ref[:, states:] = power[1]

    @pl.when(step == pl.num_programs(0) - 1)
    def _():
        lre, lim = par_ref[2:3, :states], -par_ref[2:3, states:]
        last = CHUNKS - 1
        re, im = adj_ref[last : last + 1, :states], adj_ref[last : last + 1, states:]
        for c in range(CHUNKS - 2, -1, -1):
            mre, mim = cmul(lre, lim, re, im)
            re, im = mre + adj_ref[c : c + 1, :states], mim + adj_ref[c : c + 1, states:]
        first_ref[...] = jnp.broadcast_to(jnp.concatenate([re, im], 1), first_ref.shape)


def adjoint_scan(mp, idx, keep_in, send_in, gs_ref, state_ref, src_ref, norm_ref, par_ref, adj_ref, *rest):
    others = rest[: mp - 1]
    (gdrive_ref, keep_ref, send_ref, vec_ref, acc_ref, h_ref, gdrive_a, gdrive_b) = rest[mp - 1 :]
    step = 0
    width = gs_ref.shape[1]
    states = width // 2
    me, core = idx[0], idx[1]

    re = jnp.zeros((1, states), F32)
    im = jnp.zeros((1, states), F32)
    for s in range(1, mp):
        j = me ^ s
        power = jnp.maximum(j - me - 1, 0)
        row = par_ref[pl.ds(8 + power, 1), :]
        sre, sim = cmul(row[:, :states], -row[:, states:], others[s - 1][0:1, :states], others[s - 1][0:1, states:])
        keep = (j > me).astype(F32)
        re, im = re + keep * sre, im + keep * sim
    lre, lim = par_ref[2:3, :states], -par_ref[2:3, states:]
    for c in range(CHUNKS - 1, -1, -1):
        h_ref[c : c + 1, :states] = re
        h_ref[c : c + 1, states:] = im
        mre, mim = cmul(lre, lim, re, im)
        re, im = mre + adj_ref[c : c + 1, :states], mim + adj_ref[c : c + 1, states:]
    acc_ref[...] = jnp.zeros_like(acc_ref)

    lre, lim = par_ref[0:1, :states], par_ref[0:1, states:]
    gam = par_ref[1:2, :states]
    h = [h_ref[:, :states], h_ref[:, states:]]
    sums = [jnp.zeros((CHUNKS, states), F32)] * 3

    def scan_piece(b, gdrive, r):
        hre, him = h
        rows = tile_rows(step, b * BLOCK + r)
        tre, tim = state_ref[rows, :states].astype(F32), state_ref[rows, states:].astype(F32)
        sums[0] = sums[0] + (hre * tre + him * tim)
        sums[1] = sums[1] + (him * tre - hre * tim)
        hre, him = (
            gs_ref[rows, :states] + lre * hre + lim * him,
            gs_ref[rows, states:] + lre * him - lim * hre,
        )
        sums[2] = sums[2] + (hre * src_ref[rows, :states] + him * src_ref[rows, states:])
        gdrive[r : r + CHUNKS, :states] = (hre * gam).astype(BF16)
        gdrive[r : r + CHUNKS, states:] = (him * gam).astype(BF16)
        gdrive_ref[rows, :] = gdrive[r : r + CHUNKS, :]
        h[0], h[1] = hre, him

    def scans(b, gdrive):
        return [partial(scan_piece, b, gdrive, r) for r in range(BLOCK - CHUNKS, -1, -CHUNKS)]

    def weight_pieces(b, gdrive):
        return product_tn(acc_ref, lambda cols: gdrive[:, cols], lambda: norm_ref[block_rows(step, b), :])

    last = gs_ref.shape[0] // BLOCK - 1
    buffers = (gdrive_a, gdrive_b)
    run(scans(last, buffers[last % 2]))
    for b in range(last - 1, -1, -1):
        alternate(weight_pieces(b + 1, buffers[(b + 1) % 2]), scans(b, buffers[b % 2]))
    run(weight_pieces(0, buffers[0]))
    first = keep_ref.shape[0] - states
    keep_ref[first:, :] = acc_ref[pl.ds(core * states, states), :]
    send_ref[first:, :] = acc_ref[pl.ds((1 - core) * states, states), :].astype(BF16)
    sre, sim, sgam = [jnp.sum(v, 0, keepdims=True) for v in sums]
    vec_ref[0:1, :] = jnp.concatenate([sre, sim], 1)
    vec_ref[1:2, :] = jnp.concatenate([sgam, jnp.zeros((1, states), F32)], 1)
    vec_ref[2:8, :] = jnp.zeros((6, width), F32)


def norm_back(idx, cot_ref, gdrive_ref, wt_ref, gmix_ref, xhat_ref, rstd_ref, gain_ref, skip_ref,
              gx_ref, vec_ref, gn_a, gn_b, dx_ref):
    step = pl.program_id(0)
    width = cot_ref.shape[2]
    per = STEP_ROWS // CHUNKS

    @pl.when(step == 0)
    def _():
        vec_ref[...] = jnp.zeros_like(vec_ref)

    def normed_pieces(block, gn):
        rows = pl.ds(pl.multiple_of(block * BLOCK, BLOCK), BLOCK)
        return product_nn(gn, lambda: gdrive_ref[rows, :], wt_ref)

    @pl.when(step == 0)
    def _():
        run(normed_pieces(0, gn_a))

    sums = [jnp.zeros((16, width), F32), jnp.zeros((16, width), F32)]

    def norm_piece(b, gn, r):
        rows = tile_rows(step, b * BLOCK + r)
        xhat = xhat_ref[rows, :]
        g = gn[r : r + 16, :] + skip_ref[...] * gmix_ref[rows, :].astype(F32)
        sums[0] = sums[0] + g * xhat
        sums[1] = sums[1] + g
        gh = g * gain_ref[...]
        first = jnp.mean(gh, -1, keepdims=True)
        second = jnp.mean(gh * xhat, -1, keepdims=True)
        rstd = jnp.concatenate([rstd_ref[rows, :]] * (width // 128), 1)
        dx_ref[b * BLOCK + r : b * BLOCK + r + 16, :] = rstd * (gh - first - xhat * second)

    def norm_pieces(b, gn):
        return [partial(norm_piece, b, gn, r) for r in range(0, BLOCK, 16)]

    def output_piece(k):
        rows = dx_ref[k * CHUNKS : (k + 8) * CHUNKS, :].reshape(8, CHUNKS, width)
        place = pl.ds(pl.multiple_of(step * per + k, 8), 8)
        gx_ref[:, k : k + 8, :] = cot_ref[:, place, :] + jnp.swapaxes(rows, 0, 1)

    after = jnp.minimum(2 * step + 2, gdrive_ref.shape[0] // BLOCK - 1)
    outputs = [partial(output_piece, k) for k in range(0, per, 8)]
    alternate(normed_pieces(2 * step + 1, gn_b), norm_pieces(0, gn_a))
    alternate(normed_pieces(after, gn_a), outputs[: len(outputs) // 2] + norm_pieces(1, gn_b) + outputs[len(outputs) // 2 :])
    vec_ref[0:1, :] += jnp.sum(sums[0], 0, keepdims=True)
    vec_ref[1:2, :] += jnp.sum(sums[1], 0, keepdims=True)


def pack_rows(idx, *refs):
    *parts, out = refs
    for i, part in enumerate(parts):
        out[i] = part[...]


def split_pieces(slots, count, hid, ns, idx, keep_ref, got_ref, skip_ref, glu_ref, norm_ref, lam_ref,
                 own_ref, vec_ref, *sends):
    place = idx[2]
    height = (hid + 2 * ns) // count
    for slot in range(slots):
        parts = ((slot * hid, hid, 0), (slots * hid + slot * ns, ns, hid), (slots * (hid + ns) + slot * ns, ns, hid + ns))
        for s in range(count):
            for first, size, low in parts:
                rows = size // count
                start = pl.multiple_of(first + (place ^ s) * rows, rows)
                piece = keep_ref[pl.ds(start, rows), :] + got_ref[pl.ds(start, rows), :].astype(F32)
                begin = slot * height + low // count
                if s == 0:
                    own_ref[begin : begin + rows, :] = piece
                else:
                    sends[s - 1][begin : begin + rows, :] = piece.astype(BF16)
    rows = [skip_ref[0:1, :], glu_ref[1:3, :], norm_ref[0:2, :], lam_ref[0:2, :], jnp.zeros((1, skip_ref.shape[1]), F32)]
    vec = jnp.concatenate(rows, 0)
    high = vec.astype(BF16)
    low = (vec - high.astype(F32)).astype(BF16)
    vec_ref[...] = high.astype(F32) + low.astype(F32)
    for send in sends:
        send[slots * height :, :] = jnp.concatenate([high.astype(F32), low.astype(F32)], 0).astype(BF16)


def call(kernel, steps, ins, outs, scratch, mib, flops, moved, in_place=None):
    def in_hbm(array, block):
        return array if block is None or array.size < 65536 else pltpu.with_memory_space_constraint(array, pltpu.HBM)

    def spec(block):
        return pl.BlockSpec(memory_space=pltpu.VMEM) if block is None else block

    return pl.pallas_call(
        kernel,
        grid_spec=pltpu.PrefetchScalarGridSpec(
            num_scalar_prefetch=1,
            grid=(steps,),
            in_specs=[spec(block) for _, block in ins[1:]],
            out_specs=[spec(block) for _, _, block in outs],
            scratch_shapes=[pltpu.VMEM(*s) for s in scratch],
        ),
        out_shape=[jax.ShapeDtypeStruct(s, t) if block is None else pltpu.HBM(s, t) for s, t, block in outs],
        input_output_aliases=in_place or {},
        compiler_params=pltpu.CompilerParams(vmem_limit_bytes=mib * MIB),
        cost_estimate=pl.CostEstimate(flops=flops, bytes_accessed=moved * MIB, transcendentals=0),
    )(*[in_hbm(a, block) for a, block in ins])


def xor_pairs(n, s):
    return [(i, i ^ s) for i in range(n)]


def from_each(value, axis, n):
    return [value] + [lax.ppermute(value, axis, xor_pairs(n, s)) for s in range(1, n)]


def tree_sum(parts):
    parts = list(parts)
    while len(parts) > 1:
        parts = [parts[i] + parts[i + 1] for i in range(0, len(parts), 2)]
    return parts[0]


def high_low(v):
    high = lax.reduce_precision(v, 8, 7)
    return high, lax.reduce_precision(v - high, 8, 7)


def scatter_sum(rows, position, count, permute, vec=None):
    width = rows.shape[-1]
    own = lax.dynamic_index_in_dim(rows, position, 0, keepdims=False)
    tail = []
    if vec is not None:
        high, low = high_low(vec)
        tail = [high.astype(BF16), low.astype(BF16)]
        vec = high + low
    got, vecs = [own], [vec]
    for s in range(1, count):
        send = lax.dynamic_index_in_dim(rows, position ^ s, 0, keepdims=False).astype(BF16)
        buffer = permute(jnp.concatenate([send.reshape(-1, width)] + tail) if tail else send, s)
        if tail:
            n = buffer.shape[0] - 2 * vec.shape[0]
            vecs.append(buffer[n : n + vec.shape[0]].astype(F32) + buffer[n + vec.shape[0] :].astype(F32))
            buffer = buffer[:n].reshape(own.shape)
        got.append(buffer.astype(F32))
    return tree_sum(got), (None if vec is None else tree_sum(vecs))


def flip(stack, position):
    n = stack.shape[0]
    for b in range(log2_of(n)):
        pairs = stack.reshape((n >> (b + 1), 2, 1 << b) + stack.shape[1:])
        pairs = jnp.where((position >> b) & 1 == 1, pairs[:, ::-1], pairs)
        stack = pairs.reshape(stack.shape)
    return stack


def on_device(
    block_input, ln_gain, ln_bias, nu_log, theta_log, gamma_log, in_weight, out_weight, skip, glu_weight, glu_bias,
    out_cotangent,
):
    mp = lax.axis_size("mp")
    dp = lax.axis_size("dp")
    plane = dp // 2
    me = lax.axis_index("mp")
    dpi = lax.axis_index("dp")
    core = dpi & 1
    place = dpi >> 1
    idx = jnp.stack([me, core, place]).astype(jnp.int32)
    tokens, width = block_input.shape[1:]
    ns = nu_log.shape[0]
    states = ns * mp
    hid = glu_weight.shape[2]
    chunk = tokens // CHUNKS
    per = STEP_ROWS // CHUNKS
    steps = tokens // STEP_ROWS
    x = block_input.reshape(CHUNKS, chunk, width)
    cot = out_cotangent.reshape(CHUNKS, chunk, width)
    gain, bias, skp = ln_gain[None], ln_bias[None], skip[None]

    def over_core(v):
        return lax.ppermute(v, "dp", xor_pairs(dp, 1))

    def over_plane(v, s):
        return lax.ppermute(v, "dp", xor_pairs(dp, 2 * s))

    def over_mp(v, s):
        return lax.ppermute(v, "mp", xor_pairs(mp, s))

    here = (jnp.arange(mp) == me).astype(F32)[:, None]

    def placed(v):
        return (here * v[None]).reshape(-1)

    def thirds(v):
        high, rest = high_low(v)
        return [high, rest, lax.reduce_precision(v - high - rest, 8, 7)]

    decay_row = jnp.concatenate([placed(nu_log), placed(theta_log)])
    gam_row = jnp.concatenate([placed(gamma_log), placed(gamma_log)])
    bias_rows = [placed(glu_bias[p].astype(F32)) for p in range(2)]
    params = jnp.stack(thirds(decay_row) + thirds(gam_row) + bias_rows).astype(BF16)
    params = jnp.pad(params, ((0, PARAM_ROWS - params.shape[0]), (0, 0)))

    def gathered(value, name):
        with jax.named_scope(name):
            return [value] + [over_mp(value, s) for s in range(1, mp)]

    def packed(parts, *earlier):
        value = parts[0]
        parts = lax.optimization_barrier(tuple(parts) + earlier)[: len(parts)]
        shape = (mp,) + value.shape
        return call(pack_rows, 1, [(idx, None)] + [(p, None) for p in parts], [(shape, value.dtype, None)], [], 1, 0, 0)[0]

    def tied(value, *earlier):
        return lax.optimization_barrier((value,) + earlier)[0]

    in_part = lax.dynamic_index_in_dim(in_weight, core, 1, keepdims=False).T
    out_part = lax.dynamic_index_in_dim(out_weight, core, 0, keepdims=False)
    glu_part = lax.dynamic_index_in_dim(glu_weight, core, 1, keepdims=False).T
    in_send = jnp.concatenate([in_part, params])
    both_part = jnp.concatenate([out_part, glu_part])
    x = tied(x, in_send, both_part)
    in_own = gathered(in_send, "gather_in")

    chunked = pl.BlockSpec((CHUNKS, per, width), lambda i, idx: (0, i, 0))
    vector = pl.BlockSpec((1, width), lambda i, idx: (0, 0))
    rowed = pl.BlockSpec((STEP_ROWS, width), lambda i, idx: (i, 0))
    big = (tokens, width)
    npar = 8 + mp
    product = 2 * tokens * width * width
    small = ((8, width), F32, None)

    def scratch(*kinds):
        return [((rows, cols), kind) for rows, cols, kind in kinds]

    xhat, norm, rstd = call(
        prepare, steps,
        [(idx, None), (x, chunked), (gain, vector), (bias, vector)],
        [(big, F32, None), (big, BF16, None), ((tokens, 128), F32, None)],
        [], 6, product, 12,
    )
    in_own = packed(in_own, norm)
    in_other = over_core(in_own)
    both_own = gathered(tied(both_part, in_own), "gather_out_glu")
    (cotlow,) = call(lower, steps, [(idx, None), (tied(cot, in_own), chunked)], [(big, BF16, None)], [], 5, 0, 8)
    norm = tied(norm, cotlow)
    src, wt, par, ends, last = call(
        partial(first_scan, chunk, mp), steps,
        [(idx, None), (norm, None), (in_own, None), (in_other, None)],
        [(big, F32, None), ((width, width), BF16, None), ((npar, width), F32, None), ((CHUNKS, width), F32, None), small],
        scratch((CHUNKS, width, F32), (BLOCK, width, F32), (BLOCK, width, F32)), 5, product, 8,
    )
    with jax.named_scope("carry"):
        lasts = [over_mp(last, s) for s in range(1, mp)]
    both_own = packed(both_own, *lasts)
    both_other = over_core(both_own)
    state, act, slope, wc = call(
        partial(readout, mp), steps,
        [(idx, None), (xhat, None), (src, None), (par, None), (ends, None), (gain, vector), (bias, vector), (skp, vector),
         (both_own, None), (both_other, None)] + [(v, None) for v in lasts],
        [(big, BF16, None), (big, BF16, None), (big, F32, None), ((width, width), BF16, None)],
        scratch((CHUNKS, width, F32), (BLOCK, width, BF16), (BLOCK, width, BF16), (BLOCK, width, F32), (BLOCK, width, F32)), 8, product, 8,
    )
    branch, gpre, wg, vec_glu = call(
        partial(gating, mp), steps,
        [(idx, None), (cotlow, None), (act, None), (par, None), (both_own, None), (both_other, None)],
        [(big, BF16, rowed), ((tokens, 2 * width), BF16, None), ((2 * width, width), BF16, None), small],
        scratch((BLOCK, 2 * width, F32), (BLOCK, 2 * width, F32)),
        10, 2 * product, 8,
    )
    gmix, gs, adj, first, vec_skip = call(
        unmix, steps,
        [(idx, None), (gpre, None), (slope, None), (norm, None), (wg, None), (wc, None), (par, None)],
        [(big, BF16, None), (big, F32, None), ((CHUNKS, width), F32, None), small, small],
        scratch((8, width, F32), (BLOCK, width, F32), (BLOCK, width, F32), (BLOCK, width, BF16),
                (BLOCK, width, BF16), (BLOCK, width, F32), (BLOCK, width, F32)),
        10, 4 * product, 8,
    )
    with jax.named_scope("carry_back"):
        firsts = [over_mp(first, s) for s in range(1, mp)]
    early_rows = mp * (hid + ns)
    half_rows = early_rows + states
    sums = [((half_rows, width), F32, None), ((half_rows, width), BF16, None)]
    keep, send = call(
        weight_products, 1,
        [(idx, None), (tied(gpre, first), None), (act, None), (state, None), (gmix, None)],
        sums, [], 12, 0, 0,
    )
    firsts[0] = tied(firsts[0], send)
    gdrive, keep, send, vec_lam = call(
        partial(adjoint_scan, mp), 1,
        [(idx, None), (keep, None), (send, None), (gs, None), (state, None), (src, None), (norm, None), (par, None),
         (adj, None)] + [(v, None) for v in firsts],
        [(big, BF16, None)] + sums + [small],
        scratch((width, width, F32), (CHUNKS, width, F32), (BLOCK, width, BF16),
                (BLOCK, width, BF16)), 8, product, 8, {1: 1, 2: 2},
    )
    with jax.named_scope("sum_core"):
        got = over_core(send)
    gx, vec_norm = call(
        norm_back, steps,
        [(idx, None), (cot, None), (gdrive, None), (wt, None), (gmix, None), (xhat, None), (rstd, None),
         (gain, vector), (skp, vector)],
        [((CHUNKS, chunk, width), F32, chunked), small],
        scratch((BLOCK, width, F32), (BLOCK, width, F32), (STEP_ROWS, width, F32)), 8, product, 8,
    )
    (y,) = call(add_branch, steps, [(idx, None), (x, chunked), (tied(branch, vec_norm), rowed)],
                [((CHUNKS, chunk, width), F32, chunked)], [], 10, 0, 0)
    keep, nu_log, theta_log, me, core, place = lax.optimization_barrier(
        (keep, nu_log, theta_log, me, core, place, vec_norm)
    )[:6]
    height = mp * (hid + 2 * ns) // plane
    if ns // plane % 16 == 0 and hid // plane % 16 == 0:
        own_piece, vec, *sends = call(
            partial(split_pieces, mp, plane, hid, ns), 1,
            [(idx, None), (keep, None), (got, None), (vec_skip, None), (vec_glu, None), (vec_norm, None), (vec_lam, None)],
            [((height, width), F32, None), small] + [((height + 16, width), BF16, None)] * (plane - 1), [], 4, 0, 0,
        )
    else:
        vec = jnp.concatenate([vec_skip[0:1], vec_glu[1:3], vec_norm[0:2], vec_lam[0:2], jnp.zeros((1, width), F32)])
        vec_high, vec_low = high_low(vec)
        vec, vec_rows = vec_high + vec_low, jnp.concatenate([vec_high, vec_low]).astype(BF16)
        both = keep + got.astype(F32)
        both = [both[: mp * hid], both[mp * hid : early_rows], both[early_rows:]]
        both = jnp.concatenate([v.reshape(mp, plane, -1, width) for v in both], 2).swapaxes(0, 1)
        sends = [lax.dynamic_index_in_dim(both, place ^ s, 0, keepdims=False) for s in range(plane)]
        sends = [v.reshape(-1, width) for v in sends]
        own_piece, sends = sends[0], [jnp.concatenate([v.astype(BF16), vec_rows]) for v in sends[1:]]
    with jax.named_scope("sum_plane"):
        pieces = [over_plane(v, s + 1) for s, v in enumerate(sends)]
    pieces[0] = tied(pieces[0], y)
    vec = tree_sum(
        [vec] + [p[height : height + 8].astype(F32) + p[height + 8 :].astype(F32) for p in pieces]
    )
    rows = tree_sum([own_piece] + [p[:height].astype(F32) for p in pieces]).reshape(mp, -1, width)
    with jax.named_scope("sum_mp"):
        piece, vec = scatter_sum(rows, me, mp, over_mp, vec)
    high, low = high_low(vec)
    with jax.named_scope("spread_plane"):
        piece = piece.astype(BF16)
        stack = jnp.stack([piece] + [over_plane(piece, s) for s in range(1, plane)])
    n = plane * piece.shape[0]
    got = over_core(jnp.concatenate([stack.reshape(n, width), high.astype(BF16), low.astype(BF16)]))
    vec = high + low + (got[n : n + 8].astype(F32) + got[n + 8 :].astype(F32))
    total = jnp.stack([flip(stack, place), flip(got[:n].reshape(stack.shape), place)])
    total = flip(total, core).astype(F32)
    nh, nr = hid // plane, ns // plane

    def part(start, size):
        return total[:, :, start : start + size].reshape(2, -1, width)

    grad_glu_weight = part(0, nh).transpose(2, 0, 1)
    grad_out = part(nh, nr)
    grad_out_weight = jnp.stack([grad_out[0], -grad_out[1]])
    grad_in_weight = part(nh + nr, nr).transpose(2, 0, 1)

    def decay(nu, theta):
        radius = jnp.exp(-jnp.exp(nu))
        turn = jnp.exp(theta)
        return radius * jnp.cos(turn), radius * jnp.sin(turn)

    _, decay_back = jax.vjp(decay, nu_log, theta_log)
    grad_glu_bias = lax.dynamic_slice_in_dim(vec[1:3], me * hid, hid, 1)
    grad_lam = lax.dynamic_slice_in_dim(vec[5].reshape(2, states), me * ns, ns, 1)
    grad_nu_log, grad_theta_log = decay_back((grad_lam[0], grad_lam[1]))
    grad_gamma_log = lax.dynamic_slice_in_dim(vec[6], me * ns, ns, 0)
    return (
        y.reshape(block_input.shape),
        gx.reshape(block_input.shape),
        vec[3],
        vec[4],
        grad_nu_log,
        grad_theta_log,
        grad_gamma_log,
        grad_in_weight,
        grad_out_weight,
        vec[0],
        grad_glu_weight,
        grad_glu_bias,
    )


def solution(mesh):
    in_specs = (
        P("dp", "mp", None), P(), P(), P("mp"), P("mp"), P("mp"), P(None, None, "mp"), P(None, "mp", None), P(),
        P(None, None, "mp"), P(None, "mp"), P("dp", "mp", None),
    )
    out_specs = (
        P("dp", "mp", None), P("dp", "mp", None), P(), P(), P("mp"), P("mp"), P("mp"), P(None, None, "mp"),
        P(None, "mp", None), P(), P(None, None, "mp"), P(None, "mp"),
    )
    return jax.shard_map(on_device, mesh=mesh, in_specs=in_specs, out_specs=out_specs, check_vma=False)
```

```python
from functools import partial

import jax
import jax.numpy as jnp
from jax import lax
from jax.experimental import pallas as pl
from jax.experimental.pallas import tpu as pltpu
from jax.sharding import PartitionSpec as P

EPS = 1e-05
F32 = jnp.float32
BF16 = jnp.bfloat16
CHUNKS = 16
STEP_ROWS = 512
BLOCK = 256
PARAM_ROWS = 16
MIB = 1024 * 1024
INV_SQRT2 = 0.7071067811865476
INV_SQRT_2PI = 0.3989422804014327


def nt(a, b):
    return lax.dot_general(a, b, (((1,), (1,)), ((), ())), preferred_element_type=F32)


def nn(a, b):
    return lax.dot_general(a, b, (((1,), (0,)), ((), ())), preferred_element_type=F32)


def tn(a, b):
    return lax.dot_general(a, b, (((0,), (0,)), ((), ())), preferred_element_type=F32)


def cmul(ar, ai, br, bi):
    return ar * br - ai * bi, ar * bi + ai * br


def cpower(re, im, log2):
    for _ in range(log2):
        re, im = cmul(re, im, re, im)
    return re, im


def log2_of(n):
    return n.bit_length() - 1


def block_rows(step, block):
    if isinstance(step, int):
        return slice(block * BLOCK, (block + 1) * BLOCK)
    return pl.ds(pl.multiple_of(step * STEP_ROWS + block * BLOCK, BLOCK), BLOCK)


def tile_rows(step, start):
    if isinstance(step, int):
        return slice(step * STEP_ROWS + start, step * STEP_ROWS + start + 16)
    return pl.ds(pl.multiple_of(step * STEP_ROWS + start, 16), 16)


def alternate(first, second):
    i = j = 0
    while i < len(first) or j < len(second):
        if j >= len(second) or (i < len(first) and i * len(second) <= j * len(first)):
            first[i]()
            i += 1
        else:
            second[j]()
            j += 1


def run(pieces):
    for piece in pieces:
        piece()


def product_nt(out, left, right, size=256):
    def piece(n):
        out[:, n : n + size] = nt(left(), right[n : n + size, :])

    return [partial(piece, n) for n in range(0, right.shape[0], size)]


def product_nn(out, left, right, size=256):
    def piece(n):
        out[:, n : n + size] = nn(left(), right[:, n : n + size])

    return [partial(piece, n) for n in range(0, right.shape[1], size)]


def product_tn(total, left, right, size=256):
    def piece(n):
        total[n : n + size, :] += tn(left(slice(n, n + size)), right())

    return [partial(piece, n) for n in range(0, total.shape[0], size)]


def assemble(dst, own, other, first, rows, me, core, slots, negate_second):
    for slot in range(slots):
        for part in range(2):
            mine = own[me ^ slot, first : first + rows, :]
            theirs = other[me ^ slot, first : first + rows, :]
            value = jnp.where(core == part, mine, theirs)
            start = (part * slots + slot) * rows
            dst[start : start + rows, :] = -value if negate_second and part == 1 else value


def prepare(idx, x_ref, gain_ref, bias_ref, xhat_ref, norm_ref, rstd_ref):
    step = pl.program_id(0)
    width = x_ref.shape[2]
    per = x_ref.shape[1]
    gain, bias = gain_ref[...], bias_ref[...]
    for k in range(0, per, 8):
        rows = jnp.swapaxes(x_ref[:, k : k + 8, :], 0, 1).reshape(8 * CHUNKS, width)
        for r in range(0, 8 * CHUNKS, 16):
            place = tile_rows(step, k * CHUNKS + r)
            part = rows[r : r + 16]
            mean = jnp.mean(part, -1, keepdims=True)
            cen = part - mean
            var = jnp.mean(cen * cen, -1, keepdims=True)
            rstd = lax.rsqrt(var + EPS)
            xhat = cen * rstd
            xhat_ref[place, :] = xhat
            rstd_ref[place, :] = jnp.broadcast_to(rstd, (16, 128))
            norm_ref[place, :] = (xhat * gain + bias).astype(BF16)


def lower(idx, cot_ref, cotlow_ref):
    step = pl.program_id(0)
    width = cot_ref.shape[2]
    for k in range(0, cot_ref.shape[1], 8):
        rows = jnp.swapaxes(cot_ref[:, k : k + 8, :], 0, 1).reshape(8 * CHUNKS, width)
        place = pl.ds(pl.multiple_of(step * STEP_ROWS + k * CHUNKS, 128), 8 * CHUNKS)
        cotlow_ref[place, :] = rows.astype(BF16)


def first_scan(
    chunk, mp, idx, norm_ref, own_ref, other_ref,
    src_ref, wt_ref, par_ref, ends_ref, last_ref, h_ref, drive_a, drive_b,
):
    step = 0
    width = norm_ref.shape[1]
    states = width // 2
    ns = states // mp

    me, core = idx[0], idx[1]
    assemble(wt_ref, own_ref, other_ref, 0, ns, me, core, mp, False)
    total = own_ref[0, ns : ns + PARAM_ROWS, :].astype(F32)
    for s in range(1, mp):
        total = total + own_ref[s, ns : ns + PARAM_ROWS, :].astype(F32)
    decay = total[0:1] + total[2:3] + total[4:5]
    gamma = jnp.exp(total[1:2] + total[3:4] + total[5:6])
    radius = jnp.exp(-jnp.exp(decay[:, :states]))
    turn = jnp.exp(decay[:, states:])
    re, im = radius * jnp.cos(turn), radius * jnp.sin(turn)
    lre, lim = cpower(re, im, log2_of(chunk))
    tre, tim = cpower(lre, lim, log2_of(CHUNKS))
    par_ref[0:1, :] = jnp.concatenate([re, im], 1)
    par_ref[1:2, :] = gamma
    par_ref[2:3, :] = jnp.concatenate([lre, lim], 1)
    par_ref[3:5, :] = total[6:8]
    par_ref[5:8, :] = jnp.zeros((3, width), F32)
    pre, pim = jnp.ones_like(tre), jnp.zeros_like(tim)
    for s in range(mp):
        par_ref[8 + s : 9 + s, :] = jnp.concatenate([pre, pim], 1)
        pre, pim = cmul(pre, pim, tre, tim)

    gam = par_ref[1:2, :]
    lre, lim = par_ref[0:1, :states], par_ref[0:1, states:]
    h = [jnp.zeros((CHUNKS, states), F32)] * 2

    def drive_pieces(b, drive):
        return product_nt(drive, lambda: norm_ref[block_rows(step, b), :], wt_ref)

    def scan_piece(b, drive, r):
        hre, him = h
        src = drive[r : r + CHUNKS, :] * gam
        src_ref[tile_rows(step, b * BLOCK + r), :] = src
        h[0] = src[:, :states] + lre * hre - lim * him
        h[1] = src[:, states:] + lre * him + lim * hre

    def scan_pieces(b, drive):
        return [partial(scan_piece, b, drive, r) for r in range(0, BLOCK, CHUNKS)]

    blocks = norm_ref.shape[0] // BLOCK
    drives = (drive_a, drive_b)
    run(drive_pieces(0, drive_a))
    for b in range(blocks):
        more = drive_pieces(b + 1, drives[(b + 1) % 2]) if b + 1 < blocks else []
        alternate(more, scan_pieces(b, drives[b % 2]))
    h_ref[:, :states], h_ref[:, states:] = h
    ends_ref[...] = h_ref[...]
    pre, pim = par_ref[2:3, :states], par_ref[2:3, states:]
    re, im = h_ref[0:1, :states], h_ref[0:1, states:]
    for c in range(1, CHUNKS):
        mre, mim = cmul(pre, pim, re, im)
        re, im = mre + h_ref[c : c + 1, :states], mim + h_ref[c : c + 1, states:]
    last_ref[...] = jnp.broadcast_to(jnp.concatenate([re, im], 1), last_ref.shape)


def gelu_parts(v):
    cdf = 0.5 * (1.0 + lax.erf(v * INV_SQRT2))
    pdf = jnp.exp(-0.5 * v * v) * INV_SQRT_2PI
    return v * cdf, cdf + v * pdf


def readout(mp, idx, xhat_ref, src_ref, par_ref, ends_ref, gain_ref, bias_ref, skip_ref, own_ref, other_ref, *rest):
    others = rest[: mp - 1]
    (state_ref, act_ref, slope_ref, wc_ref, h_ref, low_a, low_b, mix_a, mix_b) = rest[mp - 1 :]
    step = 0
    width = xhat_ref.shape[1]
    states = width // 2
    me, core = idx[0], idx[1]

    assemble(wc_ref, own_ref, other_ref, 0, states // mp, me, core, mp, True)
    re = jnp.zeros((1, states), F32)
    im = jnp.zeros((1, states), F32)
    for s in range(1, mp):
        j = me ^ s
        power = jnp.maximum(me - 1 - j, 0)
        row = par_ref[pl.ds(8 + power, 1), :]
        sre, sim = cmul(row[:, :states], row[:, states:], others[s - 1][0:1, :states], others[s - 1][0:1, states:])
        keep = (j < me).astype(F32)
        re, im = re + keep * sre, im + keep * sim
    lre, lim = par_ref[2:3, :states], par_ref[2:3, states:]
    for c in range(CHUNKS):
        h_ref[c : c + 1, :states] = re
        h_ref[c : c + 1, states:] = im
        mre, mim = cmul(lre, lim, re, im)
        re, im = mre + ends_ref[c : c + 1, :states], mim + ends_ref[c : c + 1, states:]

    lre, lim = par_ref[0:1, :states], par_ref[0:1, states:]
    h = [h_ref[:, :states], h_ref[:, states:]]

    def scan_piece(b, low, r):
        hre, him = h
        rows = tile_rows(step, b * BLOCK + r)
        hre, him = (
            src_ref[rows, :states] + lre * hre - lim * him,
            src_ref[rows, states:] + lre * him + lim * hre,
        )
        low[r : r + CHUNKS, :states] = hre.astype(BF16)
        low[r : r + CHUNKS, states:] = him.astype(BF16)
        state_ref[rows, :] = low[r : r + CHUNKS, :]
        h[0], h[1] = hre, him

    def gelu_piece(b, mix, r):
        rows = tile_rows(step, b * BLOCK + r)
        for c in range(0, width, 128):
            cols = slice(c, c + 128)
            normed = xhat_ref[rows, cols] * gain_ref[:, cols] + bias_ref[:, cols]
            lru = mix[r : r + 16, cols] + skip_ref[:, cols] * normed
            act, slope = gelu_parts(lru)
            act_ref[rows, cols] = act.astype(BF16)
            slope_ref[rows, cols] = slope

    def scans(b, low):
        return [partial(scan_piece, b, low, r) for r in range(0, BLOCK, CHUNKS)]

    def mixes(low, mix):
        return product_nn(mix, lambda: low[...], wc_ref)

    def gelus(b, mix):
        return [partial(gelu_piece, b, mix, r) for r in range(0, BLOCK, 16)]

    blocks = src_ref.shape[0] // BLOCK
    lows, mix_refs = (low_a, low_b), (mix_a, mix_b)
    run(scans(0, low_a))
    for b in range(blocks):
        other = scans(b + 1, lows[(b + 1) % 2]) if b + 1 < blocks else []
        other = (gelus(b - 1, mix_refs[(b - 1) % 2]) if b else []) + other
        alternate(mixes(lows[b % 2], mix_refs[b % 2]), other)
    run(gelus(blocks - 1, mix_refs[(blocks - 1) % 2]))


def add_branch(idx, x_ref, br_ref, y_ref):
    width = x_ref.shape[2]
    for k in range(0, x_ref.shape[1], 8):
        rows = br_ref[k * CHUNKS : (k + 8) * CHUNKS, :].astype(F32).reshape(8, CHUNKS, width)
        y_ref[:, k : k + 8, :] = x_ref[:, k : k + 8, :] + jnp.swapaxes(rows, 0, 1)


def gating(mp, idx, cotlow_ref, act_ref, par_ref, own_ref, other_ref,
           br_ref, gpre_ref, wg_ref, vec_ref, pre_a, pre_b):
    width = act_ref.shape[1]
    core = idx[1]
    assemble(wg_ref, own_ref, other_ref, width // 2 // mp, width // mp, idx[0], core, mp, False)
    vec_ref[...] = jnp.zeros_like(vec_ref)
    blocks = act_ref.shape[0] // BLOCK
    buffers = (pre_a, pre_b)

    def pre_pieces(b):
        return product_nt(buffers[b % 2], lambda: act_ref[b * BLOCK : (b + 1) * BLOCK, :], wg_ref) if b < blocks else []

    sums = {}

    def gate_piece(b, start, c):
        pre = buffers[b % 2]
        cols = slice(c, c + 128)
        gate_cols = slice(width + c, width + c + 128)
        for r in range(start, start + 64, 16):
            rows = slice(b * BLOCK + r, b * BLOCK + r + 16)
            value = pre[r : r + 16, cols] + par_ref[3:4, cols]
            gate = pre[r : r + 16, gate_cols] + par_ref[4:5, cols]
            sig = 0.5 * jnp.tanh(0.5 * gate) + 0.5
            branch = value * sig
            br_ref[rows, cols] = branch.astype(BF16)
            g = cotlow_ref[rows, cols].astype(F32)
            g_value = g * sig
            g_gate = g * branch * (1.0 - sig)
            gpre_ref[rows, cols] = g_value.astype(BF16)
            gpre_ref[rows, gate_cols] = g_gate.astype(BF16)
            for key, part in ((("value", c), g_value), (("gate", c), g_gate)):
                sums[key] = sums[key] + part if key in sums else part

    def gate_pieces(b):
        return [partial(gate_piece, b, start, c) for start in range(0, BLOCK, 64) for c in range(0, width, 128)]

    run(pre_pieces(0))
    for b in range(blocks):
        alternate(pre_pieces(b + 1), gate_pieces(b))
        for c in range(0, width, 128):
            vec_ref[1:2, c : c + 128] += jnp.sum(sums.pop(("value", c)), 0, keepdims=True)
            vec_ref[2:3, c : c + 128] += jnp.sum(sums.pop(("gate", c)), 0, keepdims=True)


def weight_products(idx, gpre_ref, act_ref, state_ref, gmix_ref, keep_ref, send_ref):
    core = idx[1]

    def product(left_ref, right_ref, first):
        columns = left_ref.shape[1]
        size = columns // 2
        for n in range(0, columns, 256):
            total = tn(left_ref[:, n : n + 256], right_ref[...])
            here = slice(first + n % size, first + n % size + 256)

            @pl.when(core == n // size)
            def _():
                keep_ref[here, :] = total

            @pl.when(core != n // size)
            def _():
                send_ref[here, :] = total.astype(BF16)

    product(gpre_ref, act_ref, 0)
    product(state_ref, gmix_ref, gpre_ref.shape[1] // 2)


def unmix(idx, gpre_ref, slope_ref, norm_ref, wg_ref, wc_ref, par_ref,
          gmix_ref, gs_ref, adj_ref, first_ref, vec_ref, ga_a, ga_b, gmix_a, gmix_b, gs_a, gs_b):
    step = 0
    width = norm_ref.shape[1]
    states = width // 2
    core = idx[1]

    vec_ref[...] = jnp.zeros_like(vec_ref)
    sums = {}

    def act_pieces(b, ga):
        return product_nn(ga, lambda: gpre_ref[block_rows(step, b), :], wg_ref)

    def lru_piece(b, ga, gmix, r):
        rows = tile_rows(step, b * BLOCK + r)
        for c in range(0, width, 128):
            cols = slice(c, c + 128)
            g_lru = ga[r : r + 16, cols] * slope_ref[rows, cols]
            low = g_lru.astype(BF16)
            gmix[r : r + 16, cols] = low
            gmix_ref[rows, cols] = low
            part = g_lru * norm_ref[rows, cols].astype(F32)
            sums[c] = sums[c] + part if c in sums else part

    def lru_pieces(b, ga, gmix):
        return [partial(lru_piece, b, ga, gmix, r) for r in range(0, BLOCK, 16)]

    def mix_pieces(b, gs, gmix):
        return product_nt(gs, lambda: gmix[...], wc_ref)

    lre, lim = par_ref[0:1, :states], par_ref[0:1, states:]
    power = [jnp.ones((8, states), F32), jnp.zeros((8, states), F32)]
    are = [jnp.zeros((8, states), F32) for _ in range(0, CHUNKS, 8)]
    aim = [jnp.zeros((8, states), F32) for _ in range(0, CHUNKS, 8)]

    def end_piece(b, gs, r):
        pre, pim = power
        for n, c in enumerate(range(0, CHUNKS, 8)):
            gre, gim = gs[r + c : r + c + 8, :states], gs[r + c : r + c + 8, states:]
            mre, mim = cmul(pre, pim, gre, gim)
            are[n], aim[n] = are[n] + mre, aim[n] + mim
        gs_ref[tile_rows(step, b * BLOCK + r), :] = gs[r : r + CHUNKS, :]
        power[0], power[1] = pre * lre + pim * lim, pim * lre - pre * lim

    def end_pieces(b, gs):
        return [partial(end_piece, b, gs, r) for r in range(0, BLOCK, CHUNKS)]

    blocks = gpre_ref.shape[0] // BLOCK
    gas, gmixes, gss = (ga_a, ga_b), (gmix_a, gmix_b), (gs_a, gs_b)
    run(act_pieces(0, ga_a))
    for b in range(blocks + 2):
        products = act_pieces(b + 1, gas[(b + 1) % 2]) if b + 1 < blocks else []
        products += mix_pieces(b - 1, gss[(b - 1) % 2], gmixes[(b - 1) % 2]) if 0 <= b - 1 < blocks else []
        other = lru_pieces(b, gas[b % 2], gmixes[b % 2]) if b < blocks else []
        other += end_pieces(b - 2, gss[b % 2]) if b >= 2 else []
        alternate(products, other)
    for c in range(0, width, 128):
        vec_ref[0:1, c : c + 128] += jnp.sum(sums[c], 0, keepdims=True)
    for n, c in enumerate(range(0, CHUNKS, 8)):
        adj_ref[c : c + 8, :states] = are[n]
        adj_ref[c : c + 8, states:] = aim[n]
    lre, lim = par_ref[2:3, :states], -par_ref[2:3, states:]
    last = CHUNKS - 1
    re, im = adj_ref[last : last + 1, :states], adj_ref[last : last + 1, states:]
    for c in range(CHUNKS - 2, -1, -1):
        mre, mim = cmul(lre, lim, re, im)
        re, im = mre + adj_ref[c : c + 1, :states], mim + adj_ref[c : c + 1, states:]
    first_ref[...] = jnp.broadcast_to(jnp.concatenate([re, im], 1), first_ref.shape)


def adjoint_scan(mp, idx, keep_in, send_in, gs_ref, state_ref, src_ref, norm_ref, par_ref, adj_ref, *rest):
    others = rest[: mp - 1]
    (gdrive_ref, keep_ref, send_ref, vec_ref, acc_ref, h_ref, gdrive_a, gdrive_b) = rest[mp - 1 :]
    step = 0
    width = gs_ref.shape[1]
    states = width // 2
    me, core = idx[0], idx[1]

    re = jnp.zeros((1, states), F32)
    im = jnp.zeros((1, states), F32)
    for s in range(1, mp):
        j = me ^ s
        power = jnp.maximum(j - me - 1, 0)
        row = par_ref[pl.ds(8 + power, 1), :]
        sre, sim = cmul(row[:, :states], -row[:, states:], others[s - 1][0:1, :states], others[s - 1][0:1, states:])
        keep = (j > me).astype(F32)
        re, im = re + keep * sre, im + keep * sim
    lre, lim = par_ref[2:3, :states], -par_ref[2:3, states:]
    for c in range(CHUNKS - 1, -1, -1):
        h_ref[c : c + 1, :states] = re
        h_ref[c : c + 1, states:] = im
        mre, mim = cmul(lre, lim, re, im)
        re, im = mre + adj_ref[c : c + 1, :states], mim + adj_ref[c : c + 1, states:]
    acc_ref[...] = jnp.zeros_like(acc_ref)

    lre, lim = par_ref[0:1, :states], par_ref[0:1, states:]
    gam = par_ref[1:2, :states]
    h = [h_ref[:, :states], h_ref[:, states:]]
    sums = [jnp.zeros((CHUNKS, states), F32)] * 3

    def scan_piece(b, gdrive, r):
        hre, him = h
        rows = tile_rows(step, b * BLOCK + r)
        tre, tim = state_ref[rows, :states].astype(F32), state_ref[rows, states:].astype(F32)
        sums[0] = sums[0] + (hre * tre + him * tim)
        sums[1] = sums[1] + (him * tre - hre * tim)
        hre, him = (
            gs_ref[rows, :states] + lre * hre + lim * him,
            gs_ref[rows, states:] + lre * him - lim * hre,
        )
        sums[2] = sums[2] + (hre * src_ref[rows, :states] + him * src_ref[rows, states:])
        gdrive[r : r + CHUNKS, :states] = (hre * gam).astype(BF16)
        gdrive[r : r + CHUNKS, states:] = (him * gam).astype(BF16)
        gdrive_ref[rows, :] = gdrive[r : r + CHUNKS, :]
        h[0], h[1] = hre, him

    def scans(b, gdrive):
        return [partial(scan_piece, b, gdrive, r) for r in range(BLOCK - CHUNKS, -1, -CHUNKS)]

    def weight_pieces(b, gdrive):
        return product_tn(acc_ref, lambda cols: gdrive[:, cols], lambda: norm_ref[block_rows(step, b), :])

    last = gs_ref.shape[0] // BLOCK - 1
    buffers = (gdrive_a, gdrive_b)
    run(scans(last, buffers[last % 2]))
    for b in range(last - 1, -1, -1):
        alternate(weight_pieces(b + 1, buffers[(b + 1) % 2]), scans(b, buffers[b % 2]))
    run(weight_pieces(0, buffers[0]))
    first = keep_ref.shape[0] - states
    keep_ref[first:, :] = acc_ref[pl.ds(core * states, states), :]
    send_ref[first:, :] = acc_ref[pl.ds((1 - core) * states, states), :].astype(BF16)
    sre, sim, sgam = [jnp.sum(v, 0, keepdims=True) for v in sums]
    vec_ref[0:1, :] = jnp.concatenate([sre, sim], 1)
    vec_ref[1:2, :] = jnp.concatenate([sgam, jnp.zeros((1, states), F32)], 1)
    vec_ref[2:8, :] = jnp.zeros((6, width), F32)


def norm_back(idx, cot_ref, gdrive_ref, wt_ref, gmix_ref, xhat_ref, rstd_ref, gain_ref, skip_ref,
              gx_ref, vec_ref, gn_a, gn_b, dx_ref):
    step = pl.program_id(0)
    width = cot_ref.shape[2]
    per = STEP_ROWS // CHUNKS

    @pl.when(step == 0)
    def _():
        vec_ref[...] = jnp.zeros_like(vec_ref)

    def normed_pieces(block, gn):
        rows = pl.ds(pl.multiple_of(block * BLOCK, BLOCK), BLOCK)
        return product_nn(gn, lambda: gdrive_ref[rows, :], wt_ref)

    @pl.when(step == 0)
    def _():
        run(normed_pieces(0, gn_a))

    sums = [jnp.zeros((16, width), F32), jnp.zeros((16, width), F32)]

    def norm_piece(b, gn, r):
        rows = tile_rows(step, b * BLOCK + r)
        xhat = xhat_ref[rows, :]
        g = gn[r : r + 16, :] + skip_ref[...] * gmix_ref[rows, :].astype(F32)
        sums[0] = sums[0] + g * xhat
        sums[1] = sums[1] + g
        gh = g * gain_ref[...]
        first = jnp.mean(gh, -1, keepdims=True)
        second = jnp.mean(gh * xhat, -1, keepdims=True)
        rstd = jnp.concatenate([rstd_ref[rows, :]] * (width // 128), 1)
        dx_ref[b * BLOCK + r : b * BLOCK + r + 16, :] = rstd * (gh - first - xhat * second)

    def norm_pieces(b, gn):
        return [partial(norm_piece, b, gn, r) for r in range(0, BLOCK, 16)]

    def output_piece(k):
        rows = dx_ref[k * CHUNKS : (k + 8) * CHUNKS, :].reshape(8, CHUNKS, width)
        place = pl.ds(pl.multiple_of(step * per + k, 8), 8)
        gx_ref[:, k : k + 8, :] = cot_ref[:, place, :] + jnp.swapaxes(rows, 0, 1)

    after = jnp.minimum(2 * step + 2, gdrive_ref.shape[0] // BLOCK - 1)
    outputs = [partial(output_piece, k) for k in range(0, per, 8)]
    alternate(normed_pieces(2 * step + 1, gn_b), norm_pieces(0, gn_a))
    alternate(normed_pieces(after, gn_a), outputs[: len(outputs) // 2] + norm_pieces(1, gn_b) + outputs[len(outputs) // 2 :])
    vec_ref[0:1, :] += jnp.sum(sums[0], 0, keepdims=True)
    vec_ref[1:2, :] += jnp.sum(sums[1], 0, keepdims=True)


def pack_rows(idx, *refs):
    *parts, out = refs
    for i, part in enumerate(parts):
        out[i] = part[...]


def split_pieces(slots, count, hid, ns, idx, keep_ref, got_ref, skip_ref, glu_ref, norm_ref, lam_ref,
                 own_ref, vec_ref, vec_send_ref, *sends):
    place = idx[2]
    height = (hid + 2 * ns) // count
    for slot in range(slots):
        parts = ((slot * hid, hid, 0), (slots * hid + slot * ns, ns, hid), (slots * (hid + ns) + slot * ns, ns, hid + ns))
        for s in range(count):
            for first, size, low in parts:
                rows = size // count
                start = pl.multiple_of(first + (place ^ s) * rows, rows)
                piece = keep_ref[pl.ds(start, rows), :] + got_ref[pl.ds(start, rows), :].astype(F32)
                begin = slot * height + low // count
                if s == 0:
                    own_ref[begin : begin + rows, :] = piece
                else:
                    sends[s - 1][begin : begin + rows, :] = piece.astype(BF16)
    rows = [skip_ref[0:1, :], glu_ref[1:3, :], norm_ref[0:2, :], lam_ref[0:2, :], jnp.zeros((1, skip_ref.shape[1]), F32)]
    vec = jnp.concatenate(rows, 0)
    high = vec.astype(BF16)
    low = (vec - high.astype(F32)).astype(BF16)
    vec_ref[...] = high.astype(F32) + low.astype(F32)
    vec_send_ref[...] = jnp.concatenate([high.astype(F32), low.astype(F32)], 0).astype(BF16)


def call(kernel, steps, ins, outs, scratch, mib, flops, moved, in_place=None, first=False):
    def in_hbm(array, block):
        return array if block is None or (array.size < 65536 and not first) else pltpu.with_memory_space_constraint(array, pltpu.HBM)

    def spec(block):
        return pl.BlockSpec(memory_space=pltpu.VMEM) if block is None else block

    return pl.pallas_call(
        kernel,
        grid_spec=pltpu.PrefetchScalarGridSpec(
            num_scalar_prefetch=1,
            grid=(steps,),
            in_specs=[spec(block) for _, block in ins[1:]],
            out_specs=[spec(block) for _, _, block in outs],
            scratch_shapes=[pltpu.VMEM(*s) for s in scratch],
        ),
        out_shape=[jax.ShapeDtypeStruct(s, t) if block is None else pltpu.HBM(s, t) for s, t, block in outs],
        input_output_aliases=in_place or {},
        compiler_params=pltpu.CompilerParams(vmem_limit_bytes=mib * MIB),
        cost_estimate=pl.CostEstimate(flops=flops, bytes_accessed=moved * MIB, transcendentals=0),
    )(*[in_hbm(a, block) for a, block in ins])


def xor_pairs(n, s):
    return [(i, i ^ s) for i in range(n)]


def from_each(value, axis, n):
    return [value] + [lax.ppermute(value, axis, xor_pairs(n, s)) for s in range(1, n)]


def tree_sum(parts):
    parts = list(parts)
    while len(parts) > 1:
        parts = [parts[i] + parts[i + 1] for i in range(0, len(parts), 2)]
    return parts[0]


def high_low(v):
    high = lax.reduce_precision(v, 8, 7)
    return high, lax.reduce_precision(v - high, 8, 7)


def vector_rows(v):
    high, low = high_low(v)
    return high + low, jnp.concatenate([high, low]).astype(BF16)


def vector_sum(rows):
    n = rows.shape[0] // 2
    return rows[:n].astype(F32) + rows[n:].astype(F32)


def flip(stack, position):
    n = stack.shape[0]
    for b in range(log2_of(n)):
        pairs = stack.reshape((n >> (b + 1), 2, 1 << b) + stack.shape[1:])
        pairs = jnp.where((position >> b) & 1 == 1, pairs[:, ::-1], pairs)
        stack = pairs.reshape(stack.shape)
    return stack


def on_device(
    block_input, ln_gain, ln_bias, nu_log, theta_log, gamma_log, in_weight, out_weight, skip, glu_weight, glu_bias,
    out_cotangent,
):
    mp = lax.axis_size("mp")
    dp = lax.axis_size("dp")
    plane = dp // 2
    me = lax.axis_index("mp")
    dpi = lax.axis_index("dp")
    core = dpi & 1
    place = dpi >> 1
    idx = jnp.stack([me, core, place]).astype(jnp.int32)
    tokens, width = block_input.shape[1:]
    ns = nu_log.shape[0]
    states = ns * mp
    hid = glu_weight.shape[2]
    chunk = tokens // CHUNKS
    per = STEP_ROWS // CHUNKS
    steps = tokens // STEP_ROWS
    x = block_input.reshape(CHUNKS, chunk, width)
    cot = out_cotangent.reshape(CHUNKS, chunk, width)
    gain, bias, skp = ln_gain[None], ln_bias[None], skip[None]

    def over_core(v):
        return lax.ppermute(v, "dp", xor_pairs(dp, 1))

    def over_plane(v, s):
        return lax.ppermute(v, "dp", xor_pairs(dp, 2 * s))

    def over_mp(v, s):
        return lax.ppermute(v, "mp", xor_pairs(mp, s))

    here = (jnp.arange(mp) == me).astype(F32)[:, None]

    def placed(v):
        return (here * v[None]).reshape(-1)

    def thirds(v):
        high, rest = high_low(v)
        return [high, rest, lax.reduce_precision(v - high - rest, 8, 7)]

    first_rows = [placed(nu_log), placed(gamma_log)], [placed(theta_log), placed(gamma_log)]
    first_rows = jnp.concatenate([jnp.stack(v) for v in first_rows], 1)
    bias_rows = jnp.stack([placed(glu_bias[p].astype(F32)) for p in range(2)])
    first_rows, bias_rows = lax.optimization_barrier((first_rows, bias_rows))
    params = jnp.concatenate(thirds(first_rows) + [bias_rows]).astype(BF16)
    params = jnp.pad(params, ((0, PARAM_ROWS - params.shape[0]), (0, 0)))

    def gathered(value, name):
        with jax.named_scope(name):
            return [value] + [over_mp(value, s) for s in range(1, mp)]

    def packed(parts, *earlier):
        value = parts[0]
        parts = lax.optimization_barrier(tuple(parts) + earlier)[: len(parts)]
        shape = (mp,) + value.shape
        return call(pack_rows, 1, [(idx, None)] + [(p, None) for p in parts], [(shape, value.dtype, None)], [], 1, 0, 0)[0]

    def tied(value, *earlier):
        return lax.optimization_barrier((value,) + earlier)[0]

    in_part = lax.dynamic_index_in_dim(in_weight, core, 1, keepdims=False).T
    out_part = lax.dynamic_index_in_dim(out_weight, core, 0, keepdims=False)
    glu_part = lax.dynamic_index_in_dim(glu_weight, core, 1, keepdims=False).T
    in_send = jnp.concatenate([in_part, params])
    both_part = jnp.concatenate([out_part, glu_part])
    x = tied(x, in_send, both_part)
    in_parts = gathered(in_send, "gather_in")

    chunked = pl.BlockSpec((CHUNKS, per, width), lambda i, idx: (0, i, 0))
    vector = pl.BlockSpec((1, width), lambda i, idx: (0, 0))
    rowed = pl.BlockSpec((STEP_ROWS, width), lambda i, idx: (i, 0))
    big = (tokens, width)
    npar = 8 + mp
    product = 2 * tokens * width * width
    small = ((8, width), F32, None)

    def scratch(*kinds):
        return [((rows, cols), kind) for rows, cols, kind in kinds]

    xhat, norm, rstd = call(
        prepare, steps,
        [(idx, None), (x, chunked), (gain, vector), (bias, vector)],
        [(big, F32, None), (big, BF16, None), ((tokens, 128), F32, None)],
        [], 6, product, 12, None, True,
    )
    in_parts = list(lax.optimization_barrier(tuple(in_parts) + (norm,))[:-1])
    both_own = gathered(tied(both_part, *in_parts[1:]), "gather_out_glu")
    in_own = packed(in_parts, norm)
    in_other = over_core(in_own)
    (cotlow,) = call(lower, steps, [(idx, None), (tied(cot, in_own), chunked)], [(big, BF16, None)], [], 5, 0, 8)
    norm = tied(norm, cotlow)
    src, wt, par, ends, last = call(
        partial(first_scan, chunk, mp), 1,
        [(idx, None), (norm, None), (in_own, None), (in_other, None)],
        [(big, F32, None), ((width, width), BF16, None), ((npar, width), F32, None), ((CHUNKS, width), F32, None), small],
        scratch((CHUNKS, width, F32), (BLOCK, width, F32), (BLOCK, width, F32)), 5, product, 8,
    )
    with jax.named_scope("carry"):
        lasts = [over_mp(last, s) for s in range(1, mp)]
    both_own = packed(both_own, *lasts)
    both_other = over_core(both_own)
    state, act, slope, wc = call(
        partial(readout, mp), 1,
        [(idx, None), (xhat, None), (src, None), (par, None), (ends, None), (gain, vector), (bias, vector), (skp, vector),
         (both_own, None), (both_other, None)] + [(v, None) for v in lasts],
        [(big, BF16, None), (big, BF16, None), (big, F32, None), ((width, width), BF16, None)],
        scratch((CHUNKS, width, F32), (BLOCK, width, BF16), (BLOCK, width, BF16), (BLOCK, width, F32), (BLOCK, width, F32)), 8, product, 8,
    )
    branch, gpre, wg, vec_glu = call(
        partial(gating, mp), 1,
        [(idx, None), (cotlow, None), (act, None), (par, None), (both_own, None), (both_other, None)],
        [(big, BF16, None), ((tokens, 2 * width), BF16, None), ((2 * width, width), BF16, None), small],
        scratch((BLOCK, 2 * width, F32), (BLOCK, 2 * width, F32)),
        10, 2 * product, 8,
    )
    gmix, gs, adj, first, vec_skip = call(
        unmix, 1,
        [(idx, None), (gpre, None), (slope, None), (norm, None), (wg, None), (wc, None), (par, None)],
        [(big, BF16, None), (big, F32, None), ((CHUNKS, width), F32, None), small, small],
        scratch((BLOCK, width, F32), (BLOCK, width, F32), (BLOCK, width, BF16),
                (BLOCK, width, BF16), (BLOCK, width, F32), (BLOCK, width, F32)),
        10, 4 * product, 8,
    )
    with jax.named_scope("carry_back"):
        firsts = [over_mp(first, s) for s in range(1, mp)]
    early_rows = mp * (hid + ns)
    half_rows = early_rows + states
    sums = [((half_rows, width), F32, None), ((half_rows, width), BF16, None)]
    keep, send = call(
        weight_products, 1,
        [(idx, None), (tied(gpre, first), None), (act, None), (state, None), (gmix, None)],
        sums, [], 12, 0, 0,
    )
    firsts[0] = tied(firsts[0], send)
    gdrive, keep, send, vec_lam = call(
        partial(adjoint_scan, mp), 1,
        [(idx, None), (keep, None), (send, None), (gs, None), (state, None), (src, None), (norm, None), (par, None),
         (adj, None)] + [(v, None) for v in firsts],
        [(big, BF16, None)] + sums + [small],
        scratch((width, width, F32), (CHUNKS, width, F32), (BLOCK, width, BF16),
                (BLOCK, width, BF16)), 8, product, 8, {1: 1, 2: 2},
    )
    with jax.named_scope("sum_core"):
        got = over_core(send)
    gx, vec_norm = call(
        norm_back, steps,
        [(idx, None), (cot, None), (gdrive, None), (wt, None), (gmix, None), (xhat, None), (rstd, None),
         (gain, vector), (skp, vector)],
        [((CHUNKS, chunk, width), F32, chunked), small],
        scratch((BLOCK, width, F32), (BLOCK, width, F32), (STEP_ROWS, width, F32)), 8, product, 8,
    )
    (y,) = call(add_branch, steps, [(idx, None), (x, chunked), (tied(branch, vec_norm), rowed)],
                [((CHUNKS, chunk, width), F32, chunked)], [], 10, 0, 0)
    keep, nu_log, theta_log, me, core, place = lax.optimization_barrier(
        (keep, nu_log, theta_log, me, core, place, vec_norm)
    )[:6]
    height = mp * (hid + 2 * ns) // plane
    if ns // plane % 16 == 0 and hid // plane % 16 == 0:
        own_piece, vec, vec_rows, *sends = call(
            partial(split_pieces, mp, plane, hid, ns), 1,
            [(idx, None), (keep, None), (got, None), (vec_skip, None), (vec_glu, None), (vec_norm, None), (vec_lam, None)],
            [((height, width), F32, None), small, ((16, width), BF16, None)] + [((height, width), BF16, None)] * (plane - 1),
            [], 4, 0, 0,
        )
    else:
        vec = jnp.concatenate([vec_skip[0:1], vec_glu[1:3], vec_norm[0:2], vec_lam[0:2], jnp.zeros((1, width), F32)])
        vec, vec_rows = vector_rows(vec)
        both = keep + got.astype(F32)
        both = [both[: mp * hid], both[mp * hid : early_rows], both[early_rows:]]
        both = jnp.concatenate([v.reshape(mp, plane, -1, width) for v in both], 2).swapaxes(0, 1)
        sends = [lax.dynamic_index_in_dim(both, place ^ s, 0, keepdims=False) for s in range(plane)]
        sends = [v.reshape(-1, width) for v in sends]
        own_piece, sends = sends[0], [v.astype(BF16) for v in sends[1:]]
    with jax.named_scope("sum_vectors_core"):
        vec = vec + vector_sum(over_core(vec_rows))
    with jax.named_scope("sum_plane"):
        pieces = [over_plane(v, s + 1) for s, v in enumerate(sends)]
    pieces[0] = tied(pieces[0], y)
    rows = tree_sum([own_piece] + [p.astype(F32) for p in pieces]).reshape(mp, -1, width)
    with jax.named_scope("sum_mp"):
        vec, vec_rows = vector_rows(vec)
        got, vecs = [lax.dynamic_index_in_dim(rows, me, 0, keepdims=False)], [vec]
        n = got[0].shape[0]
        for s in range(1, mp):
            send = lax.dynamic_index_in_dim(rows, me ^ s, 0, keepdims=False).astype(BF16)
            buffer = over_mp(jnp.concatenate([send, vec_rows]), s)
            got.append(buffer[:n].astype(F32))
            vecs.append(vector_sum(buffer[n:]))
    piece, vec = tree_sum(got).astype(BF16), tree_sum(vecs)
    with jax.named_scope("spread_plane"):
        vec, vec_rows = vector_rows(vec)
        piece = jnp.concatenate([piece, vec_rows])
        stack = [piece] + [over_plane(piece, s) for s in range(1, plane)]
    vec = tree_sum([vec] + [vector_sum(v[n:]) for v in stack[1:]])
    stack = jnp.stack([v[:n] for v in stack])
    with jax.named_scope("spread_core"):
        got = over_core(stack)
    total = jnp.stack([flip(stack, place), flip(got, place)])
    total = flip(total, core).astype(F32)
    nh, nr = hid // plane, ns // plane

    def part(start, size):
        return total[:, :, start : start + size].reshape(2, -1, width)

    grad_glu_weight = part(0, nh).transpose(2, 0, 1)
    grad_out = part(nh, nr)
    grad_out_weight = jnp.stack([grad_out[0], -grad_out[1]])
    grad_in_weight = part(nh + nr, nr).transpose(2, 0, 1)

    def decay(nu, theta):
        radius = jnp.exp(-jnp.exp(nu))
        turn = jnp.exp(theta)
        return radius * jnp.cos(turn), radius * jnp.sin(turn)

    _, decay_back = jax.vjp(decay, nu_log, theta_log)
    grad_glu_bias = lax.dynamic_slice_in_dim(vec[1:3], me * hid, hid, 1)
    grad_lam = lax.dynamic_slice_in_dim(vec[5].reshape(2, states), me * ns, ns, 1)
    grad_nu_log, grad_theta_log = decay_back((grad_lam[0], grad_lam[1]))
    grad_gamma_log = lax.dynamic_slice_in_dim(vec[6], me * ns, ns, 0)
    return (
        y.reshape(block_input.shape),
        gx.reshape(block_input.shape),
        vec[3],
        vec[4],
        grad_nu_log,
        grad_theta_log,
        grad_gamma_log,
        grad_in_weight,
        grad_out_weight,
        vec[0],
        grad_glu_weight,
        grad_glu_bias,
    )


def solution(mesh):
    in_specs = (
        P("dp", "mp", None), P(), P(), P("mp"), P("mp"), P("mp"), P(None, None, "mp"), P(None, "mp", None), P(),
        P(None, None, "mp"), P(None, "mp"), P("dp", "mp", None),
    )
    out_specs = (
        P("dp", "mp", None), P("dp", "mp", None), P(), P(), P("mp"), P("mp"), P("mp"), P(None, None, "mp"),
        P(None, "mp", None), P(), P(None, None, "mp"), P(None, "mp"),
    )
    return jax.shard_map(on_device, mesh=mesh, in_specs=in_specs, out_specs=out_specs, check_vma=False)
```

```python
from functools import partial

import jax
import jax.numpy as jnp
from jax import lax
from jax.experimental import pallas as pl
from jax.experimental.pallas import tpu as pltpu
from jax.sharding import PartitionSpec as P

EPS = 1e-05
F32 = jnp.float32
BF16 = jnp.bfloat16
CHUNKS = 16
STEP_ROWS = 512
BLOCK = 256
PARAM_ROWS = 16
MIB = 1024 * 1024
INV_SQRT2 = 0.7071067811865476
INV_SQRT_2PI = 0.3989422804014327


def nt(a, b):
    return lax.dot_general(a, b, (((1,), (1,)), ((), ())), preferred_element_type=F32)


def nn(a, b):
    return lax.dot_general(a, b, (((1,), (0,)), ((), ())), preferred_element_type=F32)


def tn(a, b):
    return lax.dot_general(a, b, (((0,), (0,)), ((), ())), preferred_element_type=F32)


def cmul(ar, ai, br, bi):
    return ar * br - ai * bi, ar * bi + ai * br


def cpower(re, im, log2):
    for _ in range(log2):
        re, im = cmul(re, im, re, im)
    return re, im


def log2_of(n):
    return n.bit_length() - 1


def block_rows(step, block):
    if isinstance(step, int):
        return slice(block * BLOCK, (block + 1) * BLOCK)
    return pl.ds(pl.multiple_of(step * STEP_ROWS + block * BLOCK, BLOCK), BLOCK)


def tile_rows(step, start):
    if isinstance(step, int):
        return slice(step * STEP_ROWS + start, step * STEP_ROWS + start + 16)
    return pl.ds(pl.multiple_of(step * STEP_ROWS + start, 16), 16)


def alternate(first, second):
    i = j = 0
    while i < len(first) or j < len(second):
        if j >= len(second) or (i < len(first) and i * len(second) <= j * len(first)):
            first[i]()
            i += 1
        else:
            second[j]()
            j += 1


def run(pieces):
    for piece in pieces:
        piece()


def product_nt(out, left, right, size=256):
    def piece(n):
        out[:, n : n + size] = nt(left(), right[n : n + size, :])

    return [partial(piece, n) for n in range(0, right.shape[0], size)]


def product_nn(out, left, right, size=256):
    def piece(n):
        out[:, n : n + size] = nn(left(), right[:, n : n + size])

    return [partial(piece, n) for n in range(0, right.shape[1], size)]


def product_tn(total, left, right, size=256):
    def piece(n):
        total[n : n + size, :] += tn(left(slice(n, n + size)), right())

    return [partial(piece, n) for n in range(0, total.shape[0], size)]


def assemble(dst, own, other, first, rows, me, core, slots, negate_second):
    for slot in range(slots):
        for part in range(2):
            mine = own[me ^ slot, first : first + rows, :]
            theirs = other[me ^ slot, first : first + rows, :]
            value = jnp.where(core == part, mine, theirs)
            start = (part * slots + slot) * rows
            dst[start : start + rows, :] = -value if negate_second and part == 1 else value


def prepare(idx, x_ref, gain_ref, bias_ref, xhat_ref, norm_ref, rstd_ref):
    step = pl.program_id(0)
    width = x_ref.shape[2]
    per = x_ref.shape[1]
    gain, bias = gain_ref[...], bias_ref[...]
    for k in range(0, per, 8):
        rows = jnp.swapaxes(x_ref[:, k : k + 8, :], 0, 1).reshape(8 * CHUNKS, width)
        for r in range(0, 8 * CHUNKS, 16):
            place = tile_rows(step, k * CHUNKS + r)
            part = rows[r : r + 16]
            mean = jnp.mean(part, -1, keepdims=True)
            cen = part - mean
            var = jnp.mean(cen * cen, -1, keepdims=True)
            rstd = lax.rsqrt(var + EPS)
            xhat = cen * rstd
            xhat_ref[place, :] = xhat
            rstd_ref[place, :] = jnp.broadcast_to(rstd, (16, 128))
            norm_ref[place, :] = (xhat * gain + bias).astype(BF16)


def lower(idx, cot_ref, cotlow_ref):
    step = pl.program_id(0)
    width = cot_ref.shape[2]
    for k in range(0, cot_ref.shape[1], 8):
        rows = jnp.swapaxes(cot_ref[:, k : k + 8, :], 0, 1).reshape(8 * CHUNKS, width)
        place = pl.ds(pl.multiple_of(step * STEP_ROWS + k * CHUNKS, 128), 8 * CHUNKS)
        cotlow_ref[place, :] = rows.astype(BF16)


def first_scan(
    chunk, mp, idx, norm_ref, own_ref, other_ref,
    src_ref, wt_ref, par_ref, ends_ref, last_ref, h_ref, drive_a, drive_b,
):
    step = 0
    width = norm_ref.shape[1]
    states = width // 2
    ns = states // mp

    me, core = idx[0], idx[1]
    assemble(wt_ref, own_ref, other_ref, 0, ns, me, core, mp, False)
    total = own_ref[0, ns : ns + PARAM_ROWS, :].astype(F32)
    for s in range(1, mp):
        total = total + own_ref[s, ns : ns + PARAM_ROWS, :].astype(F32)
    decay = total[0:1] + total[2:3] + total[4:5]
    gamma = jnp.exp(total[1:2] + total[3:4] + total[5:6])
    radius = jnp.exp(-jnp.exp(decay[:, :states]))
    turn = jnp.exp(decay[:, states:])
    re, im = radius * jnp.cos(turn), radius * jnp.sin(turn)
    lre, lim = cpower(re, im, log2_of(chunk))
    tre, tim = cpower(lre, lim, log2_of(CHUNKS))
    par_ref[0:1, :] = jnp.concatenate([re, im], 1)
    par_ref[1:2, :] = gamma
    par_ref[2:3, :] = jnp.concatenate([lre, lim], 1)
    par_ref[3:5, :] = total[6:8]
    par_ref[5:8, :] = jnp.zeros((3, width), F32)
    pre, pim = jnp.ones_like(tre), jnp.zeros_like(tim)
    for s in range(mp):
        par_ref[8 + s : 9 + s, :] = jnp.concatenate([pre, pim], 1)
        pre, pim = cmul(pre, pim, tre, tim)

    gam = par_ref[1:2, :]
    lre, lim = par_ref[0:1, :states], par_ref[0:1, states:]
    h = [jnp.zeros((CHUNKS, states), F32)] * 2

    def drive_pieces(b, drive):
        return product_nt(drive, lambda: norm_ref[block_rows(step, b), :], wt_ref)

    def scan_piece(b, drive, r):
        hre, him = h
        src = drive[r : r + CHUNKS, :] * gam
        src_ref[tile_rows(step, b * BLOCK + r), :] = src
        h[0] = src[:, :states] + lre * hre - lim * him
        h[1] = src[:, states:] + lre * him + lim * hre

    def scan_pieces(b, drive):
        return [partial(scan_piece, b, drive, r) for r in range(0, BLOCK, CHUNKS)]

    blocks = norm_ref.shape[0] // BLOCK
    drives = (drive_a, drive_b)
    run(drive_pieces(0, drive_a))
    for b in range(blocks):
        more = drive_pieces(b + 1, drives[(b + 1) % 2]) if b + 1 < blocks else []
        alternate(more, scan_pieces(b, drives[b % 2]))
    h_ref[:, :states], h_ref[:, states:] = h
    ends_ref[...] = h_ref[...]
    pre, pim = par_ref[2:3, :states], par_ref[2:3, states:]
    re, im = h_ref[0:1, :states], h_ref[0:1, states:]
    for c in range(1, CHUNKS):
        mre, mim = cmul(pre, pim, re, im)
        re, im = mre + h_ref[c : c + 1, :states], mim + h_ref[c : c + 1, states:]
    last_ref[...] = jnp.broadcast_to(jnp.concatenate([re, im], 1), last_ref.shape)


def gelu_parts(v):
    cdf = 0.5 * (1.0 + lax.erf(v * INV_SQRT2))
    pdf = jnp.exp(-0.5 * v * v) * INV_SQRT_2PI
    return v * cdf, cdf + v * pdf


def readout(mp, idx, xhat_ref, src_ref, par_ref, ends_ref, gain_ref, bias_ref, skip_ref, own_ref, other_ref, *rest):
    others = rest[: mp - 1]
    (state_ref, act_ref, slope_ref, wc_ref, h_ref, low_a, low_b, mix_a, mix_b) = rest[mp - 1 :]
    step = 0
    width = xhat_ref.shape[1]
    states = width // 2
    me, core = idx[0], idx[1]

    assemble(wc_ref, own_ref, other_ref, 0, states // mp, me, core, mp, True)
    re = jnp.zeros((1, states), F32)
    im = jnp.zeros((1, states), F32)
    for s in range(1, mp):
        j = me ^ s
        power = jnp.maximum(me - 1 - j, 0)
        row = par_ref[pl.ds(8 + power, 1), :]
        sre, sim = cmul(row[:, :states], row[:, states:], others[s - 1][0:1, :states], others[s - 1][0:1, states:])
        keep = (j < me).astype(F32)
        re, im = re + keep * sre, im + keep * sim
    lre, lim = par_ref[2:3, :states], par_ref[2:3, states:]
    for c in range(CHUNKS):
        h_ref[c : c + 1, :states] = re
        h_ref[c : c + 1, states:] = im
        mre, mim = cmul(lre, lim, re, im)
        re, im = mre + ends_ref[c : c + 1, :states], mim + ends_ref[c : c + 1, states:]

    lre, lim = par_ref[0:1, :states], par_ref[0:1, states:]
    h = [h_ref[:, :states], h_ref[:, states:]]

    def scan_piece(b, low, r):
        hre, him = h
        rows = tile_rows(step, b * BLOCK + r)
        hre, him = (
            src_ref[rows, :states] + lre * hre - lim * him,
            src_ref[rows, states:] + lre * him + lim * hre,
        )
        low[r : r + CHUNKS, :states] = hre.astype(BF16)
        low[r : r + CHUNKS, states:] = him.astype(BF16)
        state_ref[rows, :] = low[r : r + CHUNKS, :]
        h[0], h[1] = hre, him

    def gelu_piece(b, mix, r):
        rows = tile_rows(step, b * BLOCK + r)
        for c in range(0, width, 128):
            cols = slice(c, c + 128)
            normed = xhat_ref[rows, cols] * gain_ref[:, cols] + bias_ref[:, cols]
            lru = mix[r : r + 16, cols] + skip_ref[:, cols] * normed
            act, slope = gelu_parts(lru)
            act_ref[rows, cols] = act.astype(BF16)
            slope_ref[rows, cols] = slope

    def scans(b, low):
        return [partial(scan_piece, b, low, r) for r in range(0, BLOCK, CHUNKS)]

    def mixes(low, mix):
        return product_nn(mix, lambda: low[...], wc_ref)

    def gelus(b, mix):
        return [partial(gelu_piece, b, mix, r) for r in range(0, BLOCK, 16)]

    blocks = src_ref.shape[0] // BLOCK
    lows, mix_refs = (low_a, low_b), (mix_a, mix_b)
    run(scans(0, low_a))
    for b in range(blocks):
        other = scans(b + 1, lows[(b + 1) % 2]) if b + 1 < blocks else []
        other = (gelus(b - 1, mix_refs[(b - 1) % 2]) if b else []) + other
        alternate(mixes(lows[b % 2], mix_refs[b % 2]), other)
    run(gelus(blocks - 1, mix_refs[(blocks - 1) % 2]))


def add_branch(idx, x_ref, br_ref, y_ref):
    width = x_ref.shape[2]
    for k in range(0, x_ref.shape[1], 8):
        rows = br_ref[k * CHUNKS : (k + 8) * CHUNKS, :].astype(F32).reshape(8, CHUNKS, width)
        y_ref[:, k : k + 8, :] = x_ref[:, k : k + 8, :] + jnp.swapaxes(rows, 0, 1)


def gating(mp, idx, cotlow_ref, act_ref, par_ref, own_ref, other_ref,
           br_ref, gpre_ref, wg_ref, vec_ref, pre_a, pre_b):
    width = act_ref.shape[1]
    core = idx[1]
    assemble(wg_ref, own_ref, other_ref, width // 2 // mp, width // mp, idx[0], core, mp, False)
    vec_ref[...] = jnp.zeros_like(vec_ref)
    blocks = act_ref.shape[0] // BLOCK
    buffers = (pre_a, pre_b)

    def pre_pieces(b):
        return product_nt(buffers[b % 2], lambda: act_ref[b * BLOCK : (b + 1) * BLOCK, :], wg_ref) if b < blocks else []

    sums = {}

    def gate_piece(b, start, c):
        pre = buffers[b % 2]
        cols = slice(c, c + 128)
        gate_cols = slice(width + c, width + c + 128)
        for r in range(start, start + 64, 16):
            rows = slice(b * BLOCK + r, b * BLOCK + r + 16)
            value = pre[r : r + 16, cols] + par_ref[3:4, cols]
            gate = pre[r : r + 16, gate_cols] + par_ref[4:5, cols]
            sig = 0.5 * jnp.tanh(0.5 * gate) + 0.5
            branch = value * sig
            br_ref[rows, cols] = branch.astype(BF16)
            g = cotlow_ref[rows, cols].astype(F32)
            g_value = g * sig
            g_gate = g * branch * (1.0 - sig)
            gpre_ref[rows, cols] = g_value.astype(BF16)
            gpre_ref[rows, gate_cols] = g_gate.astype(BF16)
            for key, part in ((("value", c), g_value), (("gate", c), g_gate)):
                sums[key] = sums[key] + part if key in sums else part

    def gate_pieces(b):
        return [partial(gate_piece, b, start, c) for start in range(0, BLOCK, 64) for c in range(0, width, 128)]

    run(pre_pieces(0))
    for b in range(blocks):
        alternate(pre_pieces(b + 1), gate_pieces(b))
        for c in range(0, width, 128):
            vec_ref[1:2, c : c + 128] += jnp.sum(sums.pop(("value", c)), 0, keepdims=True)
            vec_ref[2:3, c : c + 128] += jnp.sum(sums.pop(("gate", c)), 0, keepdims=True)


def weight_products(idx, gpre_ref, act_ref, state_ref, gmix_ref, keep_ref, send_ref):
    core = idx[1]

    def product(left_ref, right_ref, first):
        columns = left_ref.shape[1]
        size = columns // 2
        for n in range(0, columns, 256):
            total = tn(left_ref[:, n : n + 256], right_ref[...])
            here = slice(first + n % size, first + n % size + 256)

            @pl.when(core == n // size)
            def _():
                keep_ref[here, :] = total

            @pl.when(core != n // size)
            def _():
                send_ref[here, :] = total.astype(BF16)

    product(gpre_ref, act_ref, 0)
    product(state_ref, gmix_ref, gpre_ref.shape[1] // 2)


def unmix(idx, gpre_ref, slope_ref, norm_ref, wg_ref, wc_ref, par_ref,
          gmix_ref, gs_ref, adj_ref, first_ref, vec_ref, ga_a, ga_b, gmix_a, gmix_b, gs_a, gs_b):
    step = 0
    width = norm_ref.shape[1]
    states = width // 2
    core = idx[1]

    vec_ref[...] = jnp.zeros_like(vec_ref)
    sums = {}

    def act_pieces(b, ga):
        return product_nn(ga, lambda: gpre_ref[block_rows(step, b), :], wg_ref)

    def lru_piece(b, ga, gmix, r):
        rows = tile_rows(step, b * BLOCK + r)
        for c in range(0, width, 128):
            cols = slice(c, c + 128)
            g_lru = ga[r : r + 16, cols] * slope_ref[rows, cols]
            low = g_lru.astype(BF16)
            gmix[r : r + 16, cols] = low
            gmix_ref[rows, cols] = low
            part = g_lru * norm_ref[rows, cols].astype(F32)
            sums[c] = sums[c] + part if c in sums else part

    def lru_pieces(b, ga, gmix):
        return [partial(lru_piece, b, ga, gmix, r) for r in range(0, BLOCK, 16)]

    def mix_pieces(b, gs, gmix):
        return product_nt(gs, lambda: gmix[...], wc_ref)

    lre, lim = par_ref[0:1, :states], par_ref[0:1, states:]
    power = [jnp.ones((8, states), F32), jnp.zeros((8, states), F32)]
    are = [jnp.zeros((8, states), F32) for _ in range(0, CHUNKS, 8)]
    aim = [jnp.zeros((8, states), F32) for _ in range(0, CHUNKS, 8)]

    def end_piece(b, gs, r):
        pre, pim = power
        for n, c in enumerate(range(0, CHUNKS, 8)):
            gre, gim = gs[r + c : r + c + 8, :states], gs[r + c : r + c + 8, states:]
            mre, mim = cmul(pre, pim, gre, gim)
            are[n], aim[n] = are[n] + mre, aim[n] + mim
        gs_ref[tile_rows(step, b * BLOCK + r), :] = gs[r : r + CHUNKS, :]
        power[0], power[1] = pre * lre + pim * lim, pim * lre - pre * lim

    def end_pieces(b, gs):
        return [partial(end_piece, b, gs, r) for r in range(0, BLOCK, CHUNKS)]

    blocks = gpre_ref.shape[0] // BLOCK
    gas, gmixes, gss = (ga_a, ga_b), (gmix_a, gmix_b), (gs_a, gs_b)
    run(act_pieces(0, ga_a))
    for b in range(blocks + 2):
        products = act_pieces(b + 1, gas[(b + 1) % 2]) if b + 1 < blocks else []
        products += mix_pieces(b - 1, gss[(b - 1) % 2], gmixes[(b - 1) % 2]) if 0 <= b - 1 < blocks else []
        other = lru_pieces(b, gas[b % 2], gmixes[b % 2]) if b < blocks else []
        other += end_pieces(b - 2, gss[b % 2]) if b >= 2 else []
        alternate(products, other)
    for c in range(0, width, 128):
        vec_ref[0:1, c : c + 128] += jnp.sum(sums[c], 0, keepdims=True)
    for n, c in enumerate(range(0, CHUNKS, 8)):
        adj_ref[c : c + 8, :states] = are[n]
        adj_ref[c : c + 8, states:] = aim[n]
    lre, lim = par_ref[2:3, :states], -par_ref[2:3, states:]
    last = CHUNKS - 1
    re, im = adj_ref[last : last + 1, :states], adj_ref[last : last + 1, states:]
    for c in range(CHUNKS - 2, -1, -1):
        mre, mim = cmul(lre, lim, re, im)
        re, im = mre + adj_ref[c : c + 1, :states], mim + adj_ref[c : c + 1, states:]
    first_ref[...] = jnp.broadcast_to(jnp.concatenate([re, im], 1), first_ref.shape)


def adjoint_scan(mp, idx, keep_in, send_in, gs_ref, state_ref, src_ref, norm_ref, par_ref, adj_ref, *rest):
    others = rest[: mp - 1]
    (gdrive_ref, keep_ref, send_ref, vec_ref, acc_ref, h_ref, gdrive_a, gdrive_b) = rest[mp - 1 :]
    step = 0
    width = gs_ref.shape[1]
    states = width // 2
    me, core = idx[0], idx[1]

    re = jnp.zeros((1, states), F32)
    im = jnp.zeros((1, states), F32)
    for s in range(1, mp):
        j = me ^ s
        power = jnp.maximum(j - me - 1, 0)
        row = par_ref[pl.ds(8 + power, 1), :]
        sre, sim = cmul(row[:, :states], -row[:, states:], others[s - 1][0:1, :states], others[s - 1][0:1, states:])
        keep = (j > me).astype(F32)
        re, im = re + keep * sre, im + keep * sim
    lre, lim = par_ref[2:3, :states], -par_ref[2:3, states:]
    for c in range(CHUNKS - 1, -1, -1):
        h_ref[c : c + 1, :states] = re
        h_ref[c : c + 1, states:] = im
        mre, mim = cmul(lre, lim, re, im)
        re, im = mre + adj_ref[c : c + 1, :states], mim + adj_ref[c : c + 1, states:]
    acc_ref[...] = jnp.zeros_like(acc_ref)

    lre, lim = par_ref[0:1, :states], par_ref[0:1, states:]
    gam = par_ref[1:2, :states]
    h = [h_ref[:, :states], h_ref[:, states:]]
    sums = [jnp.zeros((CHUNKS, states), F32)] * 3

    def scan_piece(b, gdrive, r):
        hre, him = h
        rows = tile_rows(step, b * BLOCK + r)
        tre, tim = state_ref[rows, :states].astype(F32), state_ref[rows, states:].astype(F32)
        sums[0] = sums[0] + (hre * tre + him * tim)
        sums[1] = sums[1] + (him * tre - hre * tim)
        hre, him = (
            gs_ref[rows, :states] + lre * hre + lim * him,
            gs_ref[rows, states:] + lre * him - lim * hre,
        )
        sums[2] = sums[2] + (hre * src_ref[rows, :states] + him * src_ref[rows, states:])
        gdrive[r : r + CHUNKS, :states] = (hre * gam).astype(BF16)
        gdrive[r : r + CHUNKS, states:] = (him * gam).astype(BF16)
        gdrive_ref[rows, :] = gdrive[r : r + CHUNKS, :]
        h[0], h[1] = hre, him

    def scans(b, gdrive):
        return [partial(scan_piece, b, gdrive, r) for r in range(BLOCK - CHUNKS, -1, -CHUNKS)]

    def weight_pieces(b, gdrive):
        return product_tn(acc_ref, lambda cols: gdrive[:, cols], lambda: norm_ref[block_rows(step, b), :])

    last = gs_ref.shape[0] // BLOCK - 1
    buffers = (gdrive_a, gdrive_b)
    run(scans(last, buffers[last % 2]))
    for b in range(last - 1, -1, -1):
        alternate(weight_pieces(b + 1, buffers[(b + 1) % 2]), scans(b, buffers[b % 2]))
    run(weight_pieces(0, buffers[0]))
    first = keep_ref.shape[0] - states
    keep_ref[first:, :] = acc_ref[pl.ds(core * states, states), :]
    send_ref[first:, :] = acc_ref[pl.ds((1 - core) * states, states), :].astype(BF16)
    sre, sim, sgam = [jnp.sum(v, 0, keepdims=True) for v in sums]
    vec_ref[0:1, :] = jnp.concatenate([sre, sim], 1)
    vec_ref[1:2, :] = jnp.concatenate([sgam, jnp.zeros((1, states), F32)], 1)
    vec_ref[2:8, :] = jnp.zeros((6, width), F32)


def norm_back(idx, cot_ref, gdrive_ref, wt_ref, gmix_ref, xhat_ref, rstd_ref, gain_ref, skip_ref,
              gx_ref, vec_ref, gn_a, gn_b, dx_ref):
    step = pl.program_id(0)
    width = cot_ref.shape[2]
    per = STEP_ROWS // CHUNKS

    @pl.when(step == 0)
    def _():
        vec_ref[...] = jnp.zeros_like(vec_ref)

    def normed_pieces(block, gn):
        rows = pl.ds(pl.multiple_of(block * BLOCK, BLOCK), BLOCK)
        return product_nn(gn, lambda: gdrive_ref[rows, :], wt_ref)

    @pl.when(step == 0)
    def _():
        run(normed_pieces(0, gn_a))

    sums = [jnp.zeros((16, width), F32), jnp.zeros((16, width), F32)]

    def norm_piece(b, gn, r):
        rows = tile_rows(step, b * BLOCK + r)
        xhat = xhat_ref[rows, :]
        g = gn[r : r + 16, :] + skip_ref[...] * gmix_ref[rows, :].astype(F32)
        sums[0] = sums[0] + g * xhat
        sums[1] = sums[1] + g
        gh = g * gain_ref[...]
        first = jnp.mean(gh, -1, keepdims=True)
        second = jnp.mean(gh * xhat, -1, keepdims=True)
        rstd = jnp.concatenate([rstd_ref[rows, :]] * (width // 128), 1)
        dx_ref[b * BLOCK + r : b * BLOCK + r + 16, :] = rstd * (gh - first - xhat * second)

    def norm_pieces(b, gn):
        return [partial(norm_piece, b, gn, r) for r in range(0, BLOCK, 16)]

    def output_piece(k):
        rows = dx_ref[k * CHUNKS : (k + 8) * CHUNKS, :].reshape(8, CHUNKS, width)
        place = pl.ds(pl.multiple_of(step * per + k, 8), 8)
        gx_ref[:, k : k + 8, :] = cot_ref[:, place, :] + jnp.swapaxes(rows, 0, 1)

    after = jnp.minimum(2 * step + 2, gdrive_ref.shape[0] // BLOCK - 1)
    outputs = [partial(output_piece, k) for k in range(0, per, 8)]
    alternate(normed_pieces(2 * step + 1, gn_b), norm_pieces(0, gn_a))
    alternate(normed_pieces(after, gn_a), outputs[: len(outputs) // 2] + norm_pieces(1, gn_b) + outputs[len(outputs) // 2 :])
    vec_ref[0:1, :] += jnp.sum(sums[0], 0, keepdims=True)
    vec_ref[1:2, :] += jnp.sum(sums[1], 0, keepdims=True)


def pack_rows(idx, *refs):
    *parts, out = refs
    for i, part in enumerate(parts):
        out[i] = part[...]


def split_pieces(slots, count, hid, ns, idx, keep_ref, got_ref, skip_ref, glu_ref, norm_ref, lam_ref,
                 own_ref, vec_ref, vec_send_ref, *sends):
    place = idx[2]
    height = (hid + 2 * ns) // count
    for slot in range(slots):
        parts = ((slot * hid, hid, 0), (slots * hid + slot * ns, ns, hid), (slots * (hid + ns) + slot * ns, ns, hid + ns))
        for s in range(count):
            for first, size, low in parts:
                rows = size // count
                start = pl.multiple_of(first + (place ^ s) * rows, rows)
                piece = keep_ref[pl.ds(start, rows), :] + got_ref[pl.ds(start, rows), :].astype(F32)
                begin = slot * height + low // count
                if s == 0:
                    own_ref[begin : begin + rows, :] = piece
                else:
                    sends[s - 1][begin : begin + rows, :] = piece.astype(BF16)
    rows = [skip_ref[0:1, :], glu_ref[1:3, :], norm_ref[0:2, :], lam_ref[0:2, :], jnp.zeros((1, skip_ref.shape[1]), F32)]
    vec = jnp.concatenate(rows, 0)
    high = vec.astype(BF16)
    low = (vec - high.astype(F32)).astype(BF16)
    vec_ref[...] = high.astype(F32) + low.astype(F32)
    vec_send_ref[...] = jnp.concatenate([high.astype(F32), low.astype(F32)], 0).astype(BF16)


def finish(width, idx, own_ref, got_ref, in_ref, out_ref, glu_ref):
    core, place = idx[1], idx[2]
    count, height = own_ref.shape[0], own_ref.shape[1]
    ns, hid = in_ref.shape[1], glu_ref.shape[1]
    for part in range(2):
        for i in range(count):
            mine, theirs = own_ref[i ^ place], got_ref[i ^ place]
            rows = jnp.where(core == part, mine, theirs).astype(F32)
            low = 0
            for ref, size in ((glu_ref, hid // count), (out_ref, ns // count), (in_ref, ns // count)):
                value = rows[low : low + size]
                ref[part, i * size : (i + 1) * size, :] = -value if ref is out_ref and part == 1 else value
                low += size


def small_outputs(hid, ns, idx, vec_ref, nu_ref, theta_ref, gain_ref, bias_ref, skip_ref, nu_out, theta_out, gamma_out, glu_ref):
    me = idx[0]
    width = vec_ref.shape[1]
    states = width // 2
    skip_ref[...] = vec_ref[0:1, :]
    gain_ref[...] = vec_ref[3:4, :]
    bias_ref[...] = vec_ref[4:5, :]

    def share(rows, start, size, count):
        total = jnp.zeros((rows.shape[0], size), F32)
        for j in range(count):
            total = total + jnp.where(me == j, rows[:, start + j * size : start + (j + 1) * size], 0.0)
        return total

    glu_ref[...] = share(vec_ref[1:3, :], 0, hid, width // hid)
    re = share(vec_ref[5:6, :], 0, ns, states // ns)
    im = share(vec_ref[5:6, :], states, ns, states // ns)
    gamma_out[...] = share(vec_ref[6:7, :], 0, ns, states // ns)
    speed, turn = jnp.exp(nu_ref[...]), jnp.exp(theta_ref[...])
    radius = jnp.exp(-speed)
    cos, sin = radius * jnp.cos(turn), radius * jnp.sin(turn)
    nu_out[...] = -speed * (cos * re + sin * im)
    theta_out[...] = turn * (cos * im - sin * re)


def call(kernel, steps, ins, outs, scratch, mib, flops, moved, in_place=None, first=False):
    def in_hbm(array, block):
        return array if block is None or (array.size < 65536 and not first) else pltpu.with_memory_space_constraint(array, pltpu.HBM)

    def spec(block):
        return pl.BlockSpec(memory_space=pltpu.VMEM) if block is None else block

    return pl.pallas_call(
        kernel,
        grid_spec=pltpu.PrefetchScalarGridSpec(
            num_scalar_prefetch=1,
            grid=(steps,),
            in_specs=[spec(block) for _, block in ins[1:]],
            out_specs=[spec(block) for _, _, block in outs],
            scratch_shapes=[pltpu.VMEM(*s) for s in scratch],
        ),
        out_shape=[jax.ShapeDtypeStruct(s, t) if block is None else pltpu.HBM(s, t) for s, t, block in outs],
        input_output_aliases=in_place or {},
        compiler_params=pltpu.CompilerParams(vmem_limit_bytes=mib * MIB),
        cost_estimate=pl.CostEstimate(flops=flops, bytes_accessed=moved * MIB, transcendentals=0),
    )(*[in_hbm(a, block) for a, block in ins])


def xor_pairs(n, s):
    return [(i, i ^ s) for i in range(n)]


def from_each(value, axis, n):
    return [value] + [lax.ppermute(value, axis, xor_pairs(n, s)) for s in range(1, n)]


def tree_sum(parts):
    parts = list(parts)
    while len(parts) > 1:
        parts = [parts[i] + parts[i + 1] for i in range(0, len(parts), 2)]
    return parts[0]


def high_low(v):
    high = lax.reduce_precision(v, 8, 7)
    return high, lax.reduce_precision(v - high, 8, 7)


def vector_rows(v):
    high, low = high_low(v)
    return high + low, jnp.concatenate([high, low]).astype(BF16)


def vector_sum(rows):
    n = rows.shape[0] // 2
    return rows[:n].astype(F32) + rows[n:].astype(F32)


def flip(stack, position):
    n = stack.shape[0]
    for b in range(log2_of(n)):
        pairs = stack.reshape((n >> (b + 1), 2, 1 << b) + stack.shape[1:])
        pairs = jnp.where((position >> b) & 1 == 1, pairs[:, ::-1], pairs)
        stack = pairs.reshape(stack.shape)
    return stack


def on_device(
    block_input, ln_gain, ln_bias, nu_log, theta_log, gamma_log, in_weight, out_weight, skip, glu_weight, glu_bias,
    out_cotangent,
):
    mp = lax.axis_size("mp")
    dp = lax.axis_size("dp")
    plane = dp // 2
    me = lax.axis_index("mp")
    dpi = lax.axis_index("dp")
    core = dpi & 1
    place = dpi >> 1
    idx = jnp.stack([me, core, place]).astype(jnp.int32)
    tokens, width = block_input.shape[1:]
    ns = nu_log.shape[0]
    states = ns * mp
    hid = glu_weight.shape[2]
    chunk = tokens // CHUNKS
    per = STEP_ROWS // CHUNKS
    steps = tokens // STEP_ROWS
    x = block_input.reshape(CHUNKS, chunk, width)
    cot = out_cotangent.reshape(CHUNKS, chunk, width)
    gain, bias, skp = ln_gain[None], ln_bias[None], skip[None]

    def over_core(v):
        return lax.ppermute(v, "dp", xor_pairs(dp, 1))

    def over_plane(v, s):
        return lax.ppermute(v, "dp", xor_pairs(dp, 2 * s))

    def over_mp(v, s):
        return lax.ppermute(v, "mp", xor_pairs(mp, s))

    here = (jnp.arange(mp) == me).astype(F32)[:, None]

    def placed(v):
        return (here * v[None]).reshape(-1)

    def thirds(v):
        high, rest = high_low(v)
        return [high, rest, lax.reduce_precision(v - high - rest, 8, 7)]

    first_rows = [placed(nu_log), placed(gamma_log)], [placed(theta_log), placed(gamma_log)]
    first_rows = jnp.concatenate([jnp.stack(v) for v in first_rows], 1)
    bias_rows = jnp.stack([placed(glu_bias[p].astype(F32)) for p in range(2)])
    first_rows, bias_rows = lax.optimization_barrier((first_rows, bias_rows))
    params = jnp.concatenate(thirds(first_rows) + [bias_rows]).astype(BF16)
    params = jnp.pad(params, ((0, PARAM_ROWS - params.shape[0]), (0, 0)))

    def gathered(value, name):
        with jax.named_scope(name):
            return [value] + [over_mp(value, s) for s in range(1, mp)]

    def packed(parts, *earlier):
        value = parts[0]
        parts = lax.optimization_barrier(tuple(parts) + earlier)[: len(parts)]
        shape = (mp,) + value.shape
        return call(pack_rows, 1, [(idx, None)] + [(p, None) for p in parts], [(shape, value.dtype, None)], [], 1, 0, 0)[0]

    def tied(value, *earlier):
        return lax.optimization_barrier((value,) + earlier)[0]

    in_part = lax.dynamic_index_in_dim(in_weight, core, 1, keepdims=False).T
    out_part = lax.dynamic_index_in_dim(out_weight, core, 0, keepdims=False)
    glu_part = lax.dynamic_index_in_dim(glu_weight, core, 1, keepdims=False).T
    in_send = jnp.concatenate([in_part, params])
    both_part = jnp.concatenate([out_part, glu_part])
    x = tied(x, in_send, both_part)
    in_parts = gathered(in_send, "gather_in")

    chunked = pl.BlockSpec((CHUNKS, per, width), lambda i, idx: (0, i, 0))
    vector = pl.BlockSpec((1, width), lambda i, idx: (0, 0))
    rowed = pl.BlockSpec((STEP_ROWS, width), lambda i, idx: (i, 0))
    big = (tokens, width)
    npar = 8 + mp
    product = 2 * tokens * width * width
    small = ((8, width), F32, None)

    def scratch(*kinds):
        return [((rows, cols), kind) for rows, cols, kind in kinds]

    xhat, norm, rstd = call(
        prepare, steps,
        [(idx, None), (x, chunked), (gain, vector), (bias, vector)],
        [(big, F32, None), (big, BF16, None), ((tokens, 128), F32, None)],
        [], 6, product, 12, None, True,
    )
    in_parts = list(lax.optimization_barrier(tuple(in_parts) + (norm,))[:-1])
    both_own = gathered(tied(both_part, *in_parts[1:]), "gather_out_glu")
    in_own = packed(in_parts, norm)
    in_other = over_core(in_own)
    (cotlow,) = call(lower, steps, [(idx, None), (tied(cot, in_own), chunked)], [(big, BF16, None)], [], 5, 0, 8)
    norm = tied(norm, cotlow)
    src, wt, par, ends, last = call(
        partial(first_scan, chunk, mp), 1,
        [(idx, None), (norm, None), (in_own, None), (in_other, None)],
        [(big, F32, None), ((width, width), BF16, None), ((npar, width), F32, None), ((CHUNKS, width), F32, None), small],
        scratch((CHUNKS, width, F32), (BLOCK, width, F32), (BLOCK, width, F32)), 5, product, 8,
    )
    with jax.named_scope("carry"):
        lasts = [over_mp(last, s) for s in range(1, mp)]
    both_own = packed(both_own, *lasts)
    both_other = over_core(both_own)
    state, act, slope, wc = call(
        partial(readout, mp), 1,
        [(idx, None), (xhat, None), (src, None), (par, None), (ends, None), (gain, vector), (bias, vector), (skp, vector),
         (both_own, None), (both_other, None)] + [(v, None) for v in lasts],
        [(big, BF16, None), (big, BF16, None), (big, F32, None), ((width, width), BF16, None)],
        scratch((CHUNKS, width, F32), (BLOCK, width, BF16), (BLOCK, width, BF16), (BLOCK, width, F32), (BLOCK, width, F32)), 8, product, 8,
    )
    branch, gpre, wg, vec_glu = call(
        partial(gating, mp), 1,
        [(idx, None), (cotlow, None), (act, None), (par, None), (both_own, None), (both_other, None)],
        [(big, BF16, None), ((tokens, 2 * width), BF16, None), ((2 * width, width), BF16, None), small],
        scratch((BLOCK, 2 * width, F32), (BLOCK, 2 * width, F32)),
        10, 2 * product, 8,
    )
    gmix, gs, adj, first, vec_skip = call(
        unmix, 1,
        [(idx, None), (gpre, None), (slope, None), (norm, None), (wg, None), (wc, None), (par, None)],
        [(big, BF16, None), (big, F32, None), ((CHUNKS, width), F32, None), small, small],
        scratch((BLOCK, width, F32), (BLOCK, width, F32), (BLOCK, width, BF16),
                (BLOCK, width, BF16), (BLOCK, width, F32), (BLOCK, width, F32)),
        10, 4 * product, 8,
    )
    with jax.named_scope("carry_back"):
        firsts = [over_mp(first, s) for s in range(1, mp)]
    early_rows = mp * (hid + ns)
    half_rows = early_rows + states
    sums = [((half_rows, width), F32, None), ((half_rows, width), BF16, None)]
    keep, send = call(
        weight_products, 1,
        [(idx, None), (tied(gpre, first), None), (act, None), (state, None), (gmix, None)],
        sums, [], 12, 0, 0,
    )
    firsts[0] = tied(firsts[0], send)
    gdrive, keep, send, vec_lam = call(
        partial(adjoint_scan, mp), 1,
        [(idx, None), (keep, None), (send, None), (gs, None), (state, None), (src, None), (norm, None), (par, None),
         (adj, None)] + [(v, None) for v in firsts],
        [(big, BF16, None)] + sums + [small],
        scratch((width, width, F32), (CHUNKS, width, F32), (BLOCK, width, BF16),
                (BLOCK, width, BF16)), 8, product, 8, {1: 1, 2: 2},
    )
    with jax.named_scope("sum_core"):
        got = over_core(send)
    gx, vec_norm = call(
        norm_back, steps,
        [(idx, None), (cot, None), (gdrive, None), (wt, None), (gmix, None), (xhat, None), (rstd, None),
         (gain, vector), (skp, vector)],
        [((CHUNKS, chunk, width), F32, chunked), small],
        scratch((BLOCK, width, F32), (BLOCK, width, F32), (STEP_ROWS, width, F32)), 8, product, 8,
    )
    (y,) = call(add_branch, steps, [(idx, None), (x, chunked), (tied(branch, vec_norm), rowed)],
                [((CHUNKS, chunk, width), F32, chunked)], [], 10, 0, 0)
    keep, nu_log, theta_log, me, core, place = lax.optimization_barrier(
        (keep, nu_log, theta_log, me, core, place, vec_norm)
    )[:6]
    height = mp * (hid + 2 * ns) // plane
    if ns // plane % 16 == 0 and hid // plane % 16 == 0:
        own_piece, vec, vec_rows, *sends = call(
            partial(split_pieces, mp, plane, hid, ns), 1,
            [(idx, None), (keep, None), (got, None), (vec_skip, None), (vec_glu, None), (vec_norm, None), (vec_lam, None)],
            [((height, width), F32, None), small, ((16, width), BF16, None)] + [((height, width), BF16, None)] * (plane - 1),
            [], 4, 0, 0,
        )
    else:
        vec = jnp.concatenate([vec_skip[0:1], vec_glu[1:3], vec_norm[0:2], vec_lam[0:2], jnp.zeros((1, width), F32)])
        vec, vec_rows = vector_rows(vec)
        both = keep + got.astype(F32)
        both = [both[: mp * hid], both[mp * hid : early_rows], both[early_rows:]]
        both = jnp.concatenate([v.reshape(mp, plane, -1, width) for v in both], 2).swapaxes(0, 1)
        sends = [lax.dynamic_index_in_dim(both, place ^ s, 0, keepdims=False) for s in range(plane)]
        sends = [v.reshape(-1, width) for v in sends]
        own_piece, sends = sends[0], [v.astype(BF16) for v in sends[1:]]
    with jax.named_scope("sum_vectors_core"):
        vec = vec + vector_sum(over_core(vec_rows))
    with jax.named_scope("sum_plane"):
        pieces = [over_plane(v, s + 1) for s, v in enumerate(sends)]
    pieces[0] = tied(pieces[0], y)
    rows = tree_sum([own_piece] + [p.astype(F32) for p in pieces]).reshape(mp, -1, width)
    with jax.named_scope("sum_mp"):
        vec, vec_rows = vector_rows(vec)
        got, vecs = [lax.dynamic_index_in_dim(rows, me, 0, keepdims=False)], [vec]
        n = got[0].shape[0]
        for s in range(1, mp):
            send = lax.dynamic_index_in_dim(rows, me ^ s, 0, keepdims=False).astype(BF16)
            buffer = over_mp(jnp.concatenate([send, vec_rows]), s)
            got.append(buffer[:n].astype(F32))
            vecs.append(vector_sum(buffer[n:]))
    piece, vec = tree_sum(got).astype(BF16), tree_sum(vecs)
    with jax.named_scope("spread_plane"):
        vec, vec_rows = vector_rows(vec)
        piece = jnp.concatenate([piece, vec_rows])
        stack = [piece] + [over_plane(piece, s) for s in range(1, plane)]
    vec = tree_sum([vec] + [vector_sum(v[n:]) for v in stack[1:]])
    stack = jnp.stack([v[:n] for v in stack])
    with jax.named_scope("spread_core"):
        got = over_core(stack)
    line = pl.BlockSpec((1, width), lambda i, idx: (0, 0))
    share = pl.BlockSpec((1, ns), lambda i, idx: (0, 0))
    grad_ln_gain, grad_ln_bias, grad_skip, grad_nu, grad_theta, grad_gamma, grad_glu_bias = call(
        partial(small_outputs, hid, ns), 1,
        [(idx, None), (vec, None), (nu_log[None], None), (theta_log[None], None)],
        [((1, width), F32, line)] * 3 + [((1, ns), F32, share)] * 3
        + [((2, hid), F32, pl.BlockSpec((2, hid), lambda i, idx: (0, 0)))], [], 2, 0, 0,
    )
    if ns // plane % 16 == 0 and hid // plane % 16 == 0:
        grad_in, grad_out_weight, grad_glu = call(
            partial(finish, width), 1,
            [(idx, None), (stack, None), (got, None)],
            [((2, ns, width), F32, pl.BlockSpec((2, ns, width), lambda i, idx: (0, 0, 0))),
             ((2, ns, width), F32, pl.BlockSpec((2, ns, width), lambda i, idx: (0, 0, 0))),
             ((2, hid, width), F32, None)], [], 6, 0, 0,
        )
    else:
        total = jnp.stack([flip(stack, place), flip(got, place)])
        total = flip(total, core).astype(F32)
        nh, nr = hid // plane, ns // plane

        def part(start, size):
            return total[:, :, start : start + size].reshape(2, -1, width)

        grad_glu, grad_out, grad_in = part(0, nh), part(nh, nr), part(nh + nr, nr)
        grad_out_weight = jnp.stack([grad_out[0], -grad_out[1]])
    return (
        y.reshape(block_input.shape),
        gx.reshape(block_input.shape),
        grad_ln_gain[0],
        grad_ln_bias[0],
        grad_nu[0],
        grad_theta[0],
        grad_gamma[0],
        grad_in.transpose(2, 0, 1),
        grad_out_weight,
        grad_skip[0],
        grad_glu.transpose(2, 0, 1),
        grad_glu_bias,
    )


def solution(mesh):
    in_specs = (
        P("dp", "mp", None), P(), P(), P("mp"), P("mp"), P("mp"), P(None, None, "mp"), P(None, "mp", None), P(),
        P(None, None, "mp"), P(None, "mp"), P("dp", "mp", None),
    )
    out_specs = (
        P("dp", "mp", None), P("dp", "mp", None), P(), P(), P("mp"), P("mp"), P("mp"), P(None, None, "mp"),
        P(None, "mp", None), P(), P(None, None, "mp"), P(None, "mp"),
    )
    return jax.shard_map(on_device, mesh=mesh, in_specs=in_specs, out_specs=out_specs, check_vma=False)
```

```python
from functools import partial

import jax
import jax.numpy as jnp
from jax import lax
from jax.experimental import pallas as pl
from jax.experimental.pallas import tpu as pltpu
from jax.sharding import PartitionSpec as P

EPS = 1e-05
F32 = jnp.float32
BF16 = jnp.bfloat16
CHUNKS = 16
STEP_ROWS = 512
BLOCK = 256
PARAM_ROWS = 16
MIB = 1024 * 1024
INV_SQRT2 = 0.7071067811865476
INV_SQRT_2PI = 0.3989422804014327


def nt(a, b):
    return lax.dot_general(a, b, (((1,), (1,)), ((), ())), preferred_element_type=F32)


def nn(a, b):
    return lax.dot_general(a, b, (((1,), (0,)), ((), ())), preferred_element_type=F32)


def tn(a, b):
    return lax.dot_general(a, b, (((0,), (0,)), ((), ())), preferred_element_type=F32)


def cmul(ar, ai, br, bi):
    return ar * br - ai * bi, ar * bi + ai * br


def cpower(re, im, log2):
    for _ in range(log2):
        re, im = cmul(re, im, re, im)
    return re, im


def log2_of(n):
    return n.bit_length() - 1


def block_rows(step, block):
    if isinstance(step, int):
        return slice(block * BLOCK, (block + 1) * BLOCK)
    return pl.ds(pl.multiple_of(step * STEP_ROWS + block * BLOCK, BLOCK), BLOCK)


def tile_rows(step, start):
    if isinstance(step, int):
        return slice(step * STEP_ROWS + start, step * STEP_ROWS + start + 16)
    return pl.ds(pl.multiple_of(step * STEP_ROWS + start, 16), 16)


def alternate(first, second):
    i = j = 0
    while i < len(first) or j < len(second):
        if j >= len(second) or (i < len(first) and i * len(second) <= j * len(first)):
            first[i]()
            i += 1
        else:
            second[j]()
            j += 1


def run(pieces):
    for piece in pieces:
        piece()


def product_nt(out, left, right, size=256):
    def piece(n):
        out[:, n : n + size] = nt(left(), right[n : n + size, :])

    return [partial(piece, n) for n in range(0, right.shape[0], size)]


def product_nn(out, left, right, size=256):
    def piece(n):
        out[:, n : n + size] = nn(left(), right[:, n : n + size])

    return [partial(piece, n) for n in range(0, right.shape[1], size)]


def product_tn(total, left, right, size=256):
    def piece(n):
        total[n : n + size, :] += tn(left(slice(n, n + size)), right())

    return [partial(piece, n) for n in range(0, total.shape[0], size)]


def assemble(dst, own, other, first, rows, me, core, slots, negate_second):
    for slot in range(slots):
        for part in range(2):
            mine = own[me ^ slot, first : first + rows, :]
            theirs = other[me ^ slot, first : first + rows, :]
            value = jnp.where(core == part, mine, theirs)
            start = (part * slots + slot) * rows
            dst[start : start + rows, :] = -value if negate_second and part == 1 else value


def prepare(idx, x_ref, gain_ref, bias_ref, xhat_ref, norm_ref, rstd_ref):
    step = pl.program_id(0)
    width = x_ref.shape[2]
    per = x_ref.shape[1]
    gain, bias = gain_ref[...], bias_ref[...]
    for k in range(0, per, 8):
        rows = jnp.swapaxes(x_ref[:, k : k + 8, :], 0, 1).reshape(8 * CHUNKS, width)
        for r in range(0, 8 * CHUNKS, 16):
            place = tile_rows(step, k * CHUNKS + r)
            part = rows[r : r + 16]
            mean = jnp.mean(part, -1, keepdims=True)
            cen = part - mean
            var = jnp.mean(cen * cen, -1, keepdims=True)
            rstd = lax.rsqrt(var + EPS)
            xhat = cen * rstd
            xhat_ref[place, :] = xhat
            rstd_ref[place, :] = jnp.broadcast_to(rstd, (16, 128))
            norm_ref[place, :] = (xhat * gain + bias).astype(BF16)


def lower(idx, cot_ref, cotlow_ref):
    step = pl.program_id(0)
    width = cot_ref.shape[2]
    for k in range(0, cot_ref.shape[1], 8):
        rows = jnp.swapaxes(cot_ref[:, k : k + 8, :], 0, 1).reshape(8 * CHUNKS, width)
        place = pl.ds(pl.multiple_of(step * STEP_ROWS + k * CHUNKS, 128), 8 * CHUNKS)
        cotlow_ref[place, :] = rows.astype(BF16)


def first_scan(
    chunk, mp, idx, norm_ref, own_ref, other_ref,
    src_ref, wt_ref, par_ref, ends_ref, last_ref, h_ref, drive_a, drive_b,
):
    step = 0
    width = norm_ref.shape[1]
    states = width // 2
    ns = states // mp

    me, core = idx[0], idx[1]
    assemble(wt_ref, own_ref, other_ref, 0, ns, me, core, mp, False)
    total = own_ref[0, ns : ns + PARAM_ROWS, :].astype(F32)
    for s in range(1, mp):
        total = total + own_ref[s, ns : ns + PARAM_ROWS, :].astype(F32)
    decay = total[0:1] + total[2:3] + total[4:5]
    gamma = jnp.exp(total[1:2] + total[3:4] + total[5:6])
    radius = jnp.exp(-jnp.exp(decay[:, :states]))
    turn = jnp.exp(decay[:, states:])
    re, im = radius * jnp.cos(turn), radius * jnp.sin(turn)
    lre, lim = cpower(re, im, log2_of(chunk))
    tre, tim = cpower(lre, lim, log2_of(CHUNKS))
    par_ref[0:1, :] = jnp.concatenate([re, im], 1)
    par_ref[1:2, :] = gamma
    par_ref[2:3, :] = jnp.concatenate([lre, lim], 1)
    par_ref[3:5, :] = total[6:8]
    par_ref[5:8, :] = jnp.zeros((3, width), F32)
    pre, pim = jnp.ones_like(tre), jnp.zeros_like(tim)
    for s in range(mp):
        par_ref[8 + s : 9 + s, :] = jnp.concatenate([pre, pim], 1)
        pre, pim = cmul(pre, pim, tre, tim)

    gam = par_ref[1:2, :]
    lre, lim = par_ref[0:1, :states], par_ref[0:1, states:]
    h = [jnp.zeros((CHUNKS, states), F32)] * 2

    def drive_pieces(b, drive):
        return product_nt(drive, lambda: norm_ref[block_rows(step, b), :], wt_ref)

    def scan_piece(b, drive, r):
        hre, him = h
        src = drive[r : r + CHUNKS, :] * gam
        src_ref[tile_rows(step, b * BLOCK + r), :] = src
        h[0] = src[:, :states] + lre * hre - lim * him
        h[1] = src[:, states:] + lre * him + lim * hre

    def scan_pieces(b, drive):
        return [partial(scan_piece, b, drive, r) for r in range(0, BLOCK, CHUNKS)]

    blocks = norm_ref.shape[0] // BLOCK
    drives = (drive_a, drive_b)
    run(drive_pieces(0, drive_a))
    for b in range(blocks):
        more = drive_pieces(b + 1, drives[(b + 1) % 2]) if b + 1 < blocks else []
        alternate(more, scan_pieces(b, drives[b % 2]))
    h_ref[:, :states], h_ref[:, states:] = h
    ends_ref[...] = h_ref[...]
    pre, pim = par_ref[2:3, :states], par_ref[2:3, states:]
    re, im = h_ref[0:1, :states], h_ref[0:1, states:]
    for c in range(1, CHUNKS):
        mre, mim = cmul(pre, pim, re, im)
        re, im = mre + h_ref[c : c + 1, :states], mim + h_ref[c : c + 1, states:]
    last_ref[...] = jnp.broadcast_to(jnp.concatenate([re, im], 1), last_ref.shape)


def gelu_parts(v):
    cdf = 0.5 * (1.0 + lax.erf(v * INV_SQRT2))
    pdf = jnp.exp(-0.5 * v * v) * INV_SQRT_2PI
    return v * cdf, cdf + v * pdf


def readout(mp, idx, xhat_ref, src_ref, par_ref, ends_ref, gain_ref, bias_ref, skip_ref, own_ref, other_ref, *rest):
    others = rest[: mp - 1]
    (state_ref, act_ref, slope_ref, wc_ref, h_ref, low_a, low_b, mix_a, mix_b) = rest[mp - 1 :]
    step = 0
    width = xhat_ref.shape[1]
    states = width // 2
    me, core = idx[0], idx[1]

    assemble(wc_ref, own_ref, other_ref, 0, states // mp, me, core, mp, True)
    re = jnp.zeros((1, states), F32)
    im = jnp.zeros((1, states), F32)
    for s in range(1, mp):
        j = me ^ s
        power = jnp.maximum(me - 1 - j, 0)
        row = par_ref[pl.ds(8 + power, 1), :]
        sre, sim = cmul(row[:, :states], row[:, states:], others[s - 1][0:1, :states], others[s - 1][0:1, states:])
        keep = (j < me).astype(F32)
        re, im = re + keep * sre, im + keep * sim
    lre, lim = par_ref[2:3, :states], par_ref[2:3, states:]
    for c in range(CHUNKS):
        h_ref[c : c + 1, :states] = re
        h_ref[c : c + 1, states:] = im
        mre, mim = cmul(lre, lim, re, im)
        re, im = mre + ends_ref[c : c + 1, :states], mim + ends_ref[c : c + 1, states:]

    lre, lim = par_ref[0:1, :states], par_ref[0:1, states:]
    h = [h_ref[:, :states], h_ref[:, states:]]

    def scan_piece(b, low, r):
        hre, him = h
        rows = tile_rows(step, b * BLOCK + r)
        hre, him = (
            src_ref[rows, :states] + lre * hre - lim * him,
            src_ref[rows, states:] + lre * him + lim * hre,
        )
        low[r : r + CHUNKS, :states] = hre.astype(BF16)
        low[r : r + CHUNKS, states:] = him.astype(BF16)
        state_ref[rows, :] = low[r : r + CHUNKS, :]
        h[0], h[1] = hre, him

    def gelu_piece(b, mix, r):
        rows = tile_rows(step, b * BLOCK + r)
        for c in range(0, width, 128):
            cols = slice(c, c + 128)
            normed = xhat_ref[rows, cols] * gain_ref[:, cols] + bias_ref[:, cols]
            lru = mix[r : r + 16, cols] + skip_ref[:, cols] * normed
            act, slope = gelu_parts(lru)
            act_ref[rows, cols] = act.astype(BF16)
            slope_ref[rows, cols] = slope

    def scans(b, low):
        return [partial(scan_piece, b, low, r) for r in range(0, BLOCK, CHUNKS)]

    def mixes(low, mix):
        return product_nn(mix, lambda: low[...], wc_ref)

    def gelus(b, mix):
        return [partial(gelu_piece, b, mix, r) for r in range(0, BLOCK, 16)]

    blocks = src_ref.shape[0] // BLOCK
    lows, mix_refs = (low_a, low_b), (mix_a, mix_b)
    run(scans(0, low_a))
    for b in range(blocks):
        other = scans(b + 1, lows[(b + 1) % 2]) if b + 1 < blocks else []
        other = (gelus(b - 1, mix_refs[(b - 1) % 2]) if b else []) + other
        alternate(mixes(lows[b % 2], mix_refs[b % 2]), other)
    run(gelus(blocks - 1, mix_refs[(blocks - 1) % 2]))


def gating(mp, idx, cotlow_ref, act_ref, par_ref, own_ref, other_ref,
           br_ref, gpre_ref, wg_ref, vec_ref, pre_a, pre_b):
    width = act_ref.shape[1]
    core = idx[1]
    assemble(wg_ref, own_ref, other_ref, width // 2 // mp, width // mp, idx[0], core, mp, False)
    vec_ref[...] = jnp.zeros_like(vec_ref)
    blocks = act_ref.shape[0] // BLOCK
    buffers = (pre_a, pre_b)

    def pre_pieces(b):
        return product_nt(buffers[b % 2], lambda: act_ref[b * BLOCK : (b + 1) * BLOCK, :], wg_ref) if b < blocks else []

    sums = {}

    def gate_piece(b, start, c):
        pre = buffers[b % 2]
        cols = slice(c, c + 128)
        gate_cols = slice(width + c, width + c + 128)
        for r in range(start, start + 64, 16):
            rows = slice(b * BLOCK + r, b * BLOCK + r + 16)
            value = pre[r : r + 16, cols] + par_ref[3:4, cols]
            gate = pre[r : r + 16, gate_cols] + par_ref[4:5, cols]
            sig = 0.5 * jnp.tanh(0.5 * gate) + 0.5
            branch = value * sig
            br_ref[rows, cols] = branch.astype(BF16)
            g = cotlow_ref[rows, cols].astype(F32)
            g_value = g * sig
            g_gate = g * branch * (1.0 - sig)
            gpre_ref[rows, cols] = g_value.astype(BF16)
            gpre_ref[rows, gate_cols] = g_gate.astype(BF16)
            for key, part in ((("value", c), g_value), (("gate", c), g_gate)):
                sums[key] = sums[key] + part if key in sums else part

    def gate_pieces(b):
        return [partial(gate_piece, b, start, c) for start in range(0, BLOCK, 64) for c in range(0, width, 128)]

    run(pre_pieces(0))
    for b in range(blocks):
        alternate(pre_pieces(b + 1), gate_pieces(b))
        for c in range(0, width, 128):
            vec_ref[1:2, c : c + 128] += jnp.sum(sums.pop(("value", c)), 0, keepdims=True)
            vec_ref[2:3, c : c + 128] += jnp.sum(sums.pop(("gate", c)), 0, keepdims=True)


def weight_products(idx, gpre_ref, act_ref, state_ref, gmix_ref, keep_ref, send_ref):
    core = idx[1]

    def product(left_ref, right_ref, first):
        columns = left_ref.shape[1]
        size = columns // 2
        for n in range(0, columns, 256):
            total = tn(left_ref[:, n : n + 256], right_ref[...])
            here = slice(first + n % size, first + n % size + 256)

            @pl.when(core == n // size)
            def _():
                keep_ref[here, :] = total

            @pl.when(core != n // size)
            def _():
                send_ref[here, :] = total.astype(BF16)

    product(gpre_ref, act_ref, 0)
    product(state_ref, gmix_ref, gpre_ref.shape[1] // 2)


def unmix(idx, gpre_ref, slope_ref, norm_ref, wg_ref, wc_ref, par_ref,
          gmix_ref, gs_ref, adj_ref, first_ref, vec_ref, ga_a, ga_b, gmix_a, gmix_b, gs_a, gs_b):
    step = 0
    width = norm_ref.shape[1]
    states = width // 2
    core = idx[1]

    vec_ref[...] = jnp.zeros_like(vec_ref)
    sums = {}

    def act_pieces(b, ga):
        return product_nn(ga, lambda: gpre_ref[block_rows(step, b), :], wg_ref)

    def lru_piece(b, ga, gmix, r):
        rows = tile_rows(step, b * BLOCK + r)
        for c in range(0, width, 128):
            cols = slice(c, c + 128)
            g_lru = ga[r : r + 16, cols] * slope_ref[rows, cols]
            low = g_lru.astype(BF16)
            gmix[r : r + 16, cols] = low
            gmix_ref[rows, cols] = low
            part = g_lru * norm_ref[rows, cols].astype(F32)
            sums[c] = sums[c] + part if c in sums else part

    def lru_pieces(b, ga, gmix):
        return [partial(lru_piece, b, ga, gmix, r) for r in range(0, BLOCK, 16)]

    def mix_pieces(b, gs, gmix):
        return product_nt(gs, lambda: gmix[...], wc_ref)

    lre, lim = par_ref[0:1, :states], par_ref[0:1, states:]
    power = [jnp.ones((8, states), F32), jnp.zeros((8, states), F32)]
    are = [jnp.zeros((8, states), F32) for _ in range(0, CHUNKS, 8)]
    aim = [jnp.zeros((8, states), F32) for _ in range(0, CHUNKS, 8)]

    def end_piece(b, gs, r):
        pre, pim = power
        for n, c in enumerate(range(0, CHUNKS, 8)):
            gre, gim = gs[r + c : r + c + 8, :states], gs[r + c : r + c + 8, states:]
            mre, mim = cmul(pre, pim, gre, gim)
            are[n], aim[n] = are[n] + mre, aim[n] + mim
        gs_ref[tile_rows(step, b * BLOCK + r), :] = gs[r : r + CHUNKS, :]
        power[0], power[1] = pre * lre + pim * lim, pim * lre - pre * lim

    def end_pieces(b, gs):
        return [partial(end_piece, b, gs, r) for r in range(0, BLOCK, CHUNKS)]

    blocks = gpre_ref.shape[0] // BLOCK
    gas, gmixes, gss = (ga_a, ga_b), (gmix_a, gmix_b), (gs_a, gs_b)
    run(act_pieces(0, ga_a))
    for b in range(blocks + 2):
        products = act_pieces(b + 1, gas[(b + 1) % 2]) if b + 1 < blocks else []
        products += mix_pieces(b - 1, gss[(b - 1) % 2], gmixes[(b - 1) % 2]) if 0 <= b - 1 < blocks else []
        other = lru_pieces(b, gas[b % 2], gmixes[b % 2]) if b < blocks else []
        other += end_pieces(b - 2, gss[b % 2]) if b >= 2 else []
        alternate(products, other)
    for c in range(0, width, 128):
        vec_ref[0:1, c : c + 128] += jnp.sum(sums[c], 0, keepdims=True)
    for n, c in enumerate(range(0, CHUNKS, 8)):
        adj_ref[c : c + 8, :states] = are[n]
        adj_ref[c : c + 8, states:] = aim[n]
    lre, lim = par_ref[2:3, :states], -par_ref[2:3, states:]
    last = CHUNKS - 1
    re, im = adj_ref[last : last + 1, :states], adj_ref[last : last + 1, states:]
    for c in range(CHUNKS - 2, -1, -1):
        mre, mim = cmul(lre, lim, re, im)
        re, im = mre + adj_ref[c : c + 1, :states], mim + adj_ref[c : c + 1, states:]
    first_ref[...] = jnp.broadcast_to(jnp.concatenate([re, im], 1), first_ref.shape)


def adjoint_scan(mp, idx, keep_in, send_in, gs_ref, state_ref, src_ref, norm_ref, par_ref, adj_ref, *rest):
    others = rest[: mp - 1]
    (gdrive_ref, keep_ref, send_ref, vec_ref, acc_ref, h_ref, gdrive_a, gdrive_b) = rest[mp - 1 :]
    step = 0
    width = gs_ref.shape[1]
    states = width // 2
    me, core = idx[0], idx[1]

    re = jnp.zeros((1, states), F32)
    im = jnp.zeros((1, states), F32)
    for s in range(1, mp):
        j = me ^ s
        power = jnp.maximum(j - me - 1, 0)
        row = par_ref[pl.ds(8 + power, 1), :]
        sre, sim = cmul(row[:, :states], -row[:, states:], others[s - 1][0:1, :states], others[s - 1][0:1, states:])
        keep = (j > me).astype(F32)
        re, im = re + keep * sre, im + keep * sim
    lre, lim = par_ref[2:3, :states], -par_ref[2:3, states:]
    for c in range(CHUNKS - 1, -1, -1):
        h_ref[c : c + 1, :states] = re
        h_ref[c : c + 1, states:] = im
        mre, mim = cmul(lre, lim, re, im)
        re, im = mre + adj_ref[c : c + 1, :states], mim + adj_ref[c : c + 1, states:]
    acc_ref[...] = jnp.zeros_like(acc_ref)

    lre, lim = par_ref[0:1, :states], par_ref[0:1, states:]
    gam = par_ref[1:2, :states]
    h = [h_ref[:, :states], h_ref[:, states:]]
    sums = [jnp.zeros((CHUNKS, states), F32)] * 3

    def scan_piece(b, gdrive, r):
        hre, him = h
        rows = tile_rows(step, b * BLOCK + r)
        tre, tim = state_ref[rows, :states].astype(F32), state_ref[rows, states:].astype(F32)
        sums[0] = sums[0] + (hre * tre + him * tim)
        sums[1] = sums[1] + (him * tre - hre * tim)
        hre, him = (
            gs_ref[rows, :states] + lre * hre + lim * him,
            gs_ref[rows, states:] + lre * him - lim * hre,
        )
        sums[2] = sums[2] + (hre * src_ref[rows, :states] + him * src_ref[rows, states:])
        gdrive[r : r + CHUNKS, :states] = (hre * gam).astype(BF16)
        gdrive[r : r + CHUNKS, states:] = (him * gam).astype(BF16)
        gdrive_ref[rows, :] = gdrive[r : r + CHUNKS, :]
        h[0], h[1] = hre, him

    def scans(b, gdrive):
        return [partial(scan_piece, b, gdrive, r) for r in range(BLOCK - CHUNKS, -1, -CHUNKS)]

    def weight_pieces(b, gdrive):
        return product_tn(acc_ref, lambda cols: gdrive[:, cols], lambda: norm_ref[block_rows(step, b), :])

    last = gs_ref.shape[0] // BLOCK - 1
    buffers = (gdrive_a, gdrive_b)
    run(scans(last, buffers[last % 2]))
    for b in range(last - 1, -1, -1):
        alternate(weight_pieces(b + 1, buffers[(b + 1) % 2]), scans(b, buffers[b % 2]))
    run(weight_pieces(0, buffers[0]))
    first = keep_ref.shape[0] - states
    keep_ref[first:, :] = acc_ref[pl.ds(core * states, states), :]
    send_ref[first:, :] = acc_ref[pl.ds((1 - core) * states, states), :].astype(BF16)
    sre, sim, sgam = [jnp.sum(v, 0, keepdims=True) for v in sums]
    vec_ref[0:1, :] = jnp.concatenate([sre, sim], 1)
    vec_ref[1:2, :] = jnp.concatenate([sgam, jnp.zeros((1, states), F32)], 1)
    vec_ref[2:8, :] = jnp.zeros((6, width), F32)


def norm_back(idx, cot_ref, gdrive_ref, wt_ref, gmix_ref, xhat_ref, rstd_ref, gain_ref, skip_ref, x_ref, br_ref,
              vec_skip_ref, vec_glu_ref, vec_lam_ref, gx_ref, y_ref, parts_ref, send_ref, gn_a, gn_b, dx_ref, vec_ref):
    step = pl.program_id(0)
    width = cot_ref.shape[2]
    per = STEP_ROWS // CHUNKS

    @pl.when(step == 0)
    def _():
        vec_ref[...] = jnp.zeros_like(vec_ref)

    def normed_pieces(block, gn):
        rows = pl.ds(pl.multiple_of(block * BLOCK, BLOCK), BLOCK)
        return product_nn(gn, lambda: gdrive_ref[rows, :], wt_ref)

    @pl.when(step == 0)
    def _():
        run(normed_pieces(0, gn_a))

    sums = [jnp.zeros((16, width), F32), jnp.zeros((16, width), F32)]

    def norm_piece(b, gn, r):
        rows = tile_rows(step, b * BLOCK + r)
        xhat = xhat_ref[rows, :]
        g = gn[r : r + 16, :] + skip_ref[...] * gmix_ref[rows, :].astype(F32)
        sums[0] = sums[0] + g * xhat
        sums[1] = sums[1] + g
        gh = g * gain_ref[...]
        first = jnp.mean(gh, -1, keepdims=True)
        second = jnp.mean(gh * xhat, -1, keepdims=True)
        rstd = jnp.concatenate([rstd_ref[rows, :]] * (width // 128), 1)
        dx_ref[b * BLOCK + r : b * BLOCK + r + 16, :] = rstd * (gh - first - xhat * second)

    def norm_pieces(b, gn):
        return [partial(norm_piece, b, gn, r) for r in range(0, BLOCK, 16)]

    def output_piece(k):
        rows = dx_ref[k * CHUNKS : (k + 8) * CHUNKS, :].reshape(8, CHUNKS, width)
        place = pl.ds(pl.multiple_of(step * per + k, 8), 8)
        gx_ref[:, k : k + 8, :] = cot_ref[:, place, :] + jnp.swapaxes(rows, 0, 1)

    def branch_piece(k):
        here = pl.ds(pl.multiple_of(step * STEP_ROWS + k * CHUNKS, 128), 8 * CHUNKS)
        rows = br_ref[here, :].astype(F32).reshape(8, CHUNKS, width)
        y_ref[:, k : k + 8, :] = x_ref[:, k : k + 8, :] + jnp.swapaxes(rows, 0, 1)

    after = jnp.minimum(2 * step + 2, gdrive_ref.shape[0] // BLOCK - 1)
    outputs = [partial(output_piece, k) for k in range(0, per, 8)]
    run([partial(branch_piece, k) for k in range(0, per, 8)])
    alternate(normed_pieces(2 * step + 1, gn_b), norm_pieces(0, gn_a))
    alternate(normed_pieces(after, gn_a), outputs[: len(outputs) // 2] + norm_pieces(1, gn_b) + outputs[len(outputs) // 2 :])
    vec_ref[0:1, :] += jnp.sum(sums[0], 0, keepdims=True)
    vec_ref[1:2, :] += jnp.sum(sums[1], 0, keepdims=True)

    @pl.when(step == pl.num_programs(0) - 1)
    def _():
        rows = [vec_skip_ref[0:1, :], vec_glu_ref[1:3, :], vec_ref[0:2, :], vec_lam_ref[0:2, :], jnp.zeros((1, width), F32)]
        vec = jnp.concatenate(rows, 0)
        high = vec.astype(BF16)
        low = (vec - high.astype(F32)).astype(BF16)
        parts_ref[...] = high.astype(F32) + low.astype(F32)
        send_ref[...] = jnp.concatenate([high.astype(F32), low.astype(F32)], 0).astype(BF16)


def pack_rows(idx, *refs):
    *parts, out = refs
    for i, part in enumerate(parts):
        out[i] = part[...]


def split_pieces(slots, count, sizes, idx, keep_ref, got_ref, own_ref, *sends):
    place = idx[2]
    height = sum(sizes) // count
    for slot in range(slots):
        for s in range(count):
            base, low = 0, slot * height
            for size in sizes:
                rows = size // count
                start = pl.multiple_of(base + slot * size + (place ^ s) * rows, rows)
                piece = keep_ref[pl.ds(start, rows), :] + got_ref[pl.ds(start, rows), :].astype(F32)
                if s == 0:
                    own_ref[low : low + rows, :] = piece
                else:
                    sends[s - 1][low : low + rows, :] = piece.astype(BF16)
                base, low = base + slots * size, low + rows


def finish(hid, ns, count, idx, own_ref, got_ref, nu_ref, theta_ref, in_ref, out_ref, glu_ref, *rest):
    core, place = idx[1], idx[2]
    height = (hid + 2 * ns) // count
    for part in range(2):
        for i in range(count):
            here = pl.ds(pl.multiple_of((i ^ place) * height, 16), height)
            rows = jnp.where(core == part, own_ref[here, :], got_ref[here, :]).astype(F32)
            low = 0
            for ref, size in ((glu_ref, hid // count), (out_ref, ns // count), (in_ref, ns // count)):
                value = rows[low : low + size]
                ref[part, i * size : (i + 1) * size, :] = -value if ref is out_ref and part == 1 else value
                low += size
    first = count * height
    both = [ref[first : first + 16, :].astype(F32) for ref in (own_ref, got_ref)]
    vec = (both[0][:8] + both[0][8:]) + (both[1][:8] + both[1][8:])
    vector_outputs(hid, ns, idx, vec, nu_ref, theta_ref, *rest)


def vector_outputs(hid, ns, idx, vec, nu_ref, theta_ref, gain_ref, bias_ref, skip_ref, nu_out, theta_out, gamma_out, glu_ref):
    me = idx[0]
    width = vec.shape[1]
    states = width // 2
    skip_ref[...] = vec[0:1, :]
    gain_ref[...] = vec[3:4, :]
    bias_ref[...] = vec[4:5, :]

    def share(rows, start, size, count):
        total = jnp.zeros((rows.shape[0], size), F32)
        for j in range(count):
            total = total + jnp.where(me == j, rows[:, start + j * size : start + (j + 1) * size], 0.0)
        return total

    glu_ref[...] = share(vec[1:3, :], 0, hid, width // hid)
    re = share(vec[5:6, :], 0, ns, states // ns)
    im = share(vec[5:6, :], states, ns, states // ns)
    gamma_out[...] = share(vec[6:7, :], 0, ns, states // ns)
    speed, turn = jnp.exp(nu_ref[...]), jnp.exp(theta_ref[...])
    radius = jnp.exp(-speed)
    cos, sin = radius * jnp.cos(turn), radius * jnp.sin(turn)
    nu_out[...] = -speed * (cos * re + sin * im)
    theta_out[...] = turn * (cos * im - sin * re)


def small_outputs(hid, ns, idx, vec_ref, *rest):
    vector_outputs(hid, ns, idx, vec_ref[...], *rest)


def call(kernel, steps, ins, outs, scratch, mib, flops, moved, in_place=None, first=False):
    def in_hbm(array, block):
        return array if block is None or (array.size < 65536 and not first) else pltpu.with_memory_space_constraint(array, pltpu.HBM)

    def spec(block):
        return pl.BlockSpec(memory_space=pltpu.VMEM) if block is None else block

    return pl.pallas_call(
        kernel,
        grid_spec=pltpu.PrefetchScalarGridSpec(
            num_scalar_prefetch=1,
            grid=(steps,),
            in_specs=[spec(block) for _, block in ins[1:]],
            out_specs=[spec(block) for _, _, block in outs],
            scratch_shapes=[pltpu.VMEM(*s) for s in scratch],
        ),
        out_shape=[jax.ShapeDtypeStruct(s, t) if block is None else pltpu.HBM(s, t) for s, t, block in outs],
        input_output_aliases=in_place or {},
        compiler_params=pltpu.CompilerParams(vmem_limit_bytes=mib * MIB),
        cost_estimate=pl.CostEstimate(flops=flops, bytes_accessed=moved * MIB, transcendentals=0),
    )(*[in_hbm(a, block) for a, block in ins])


def xor_pairs(n, s):
    return [(i, i ^ s) for i in range(n)]


def from_each(value, axis, n):
    return [value] + [lax.ppermute(value, axis, xor_pairs(n, s)) for s in range(1, n)]


def tree_sum(parts):
    parts = list(parts)
    while len(parts) > 1:
        parts = [parts[i] + parts[i + 1] for i in range(0, len(parts), 2)]
    return parts[0]


def high_low(v):
    high = lax.reduce_precision(v, 8, 7)
    return high, lax.reduce_precision(v - high, 8, 7)


def vector_rows(v):
    high, low = high_low(v)
    return high + low, jnp.concatenate([high, low]).astype(BF16)


def vector_sum(rows):
    n = rows.shape[0] // 2
    return rows[:n].astype(F32) + rows[n:].astype(F32)


def flip(stack, position):
    n = stack.shape[0]
    for b in range(log2_of(n)):
        pairs = stack.reshape((n >> (b + 1), 2, 1 << b) + stack.shape[1:])
        pairs = jnp.where((position >> b) & 1 == 1, pairs[:, ::-1], pairs)
        stack = pairs.reshape(stack.shape)
    return stack


def on_device(
    block_input, ln_gain, ln_bias, nu_log, theta_log, gamma_log, in_weight, out_weight, skip, glu_weight, glu_bias,
    out_cotangent,
):
    mp = lax.axis_size("mp")
    dp = lax.axis_size("dp")
    plane = dp // 2
    me = lax.axis_index("mp")
    dpi = lax.axis_index("dp")
    core = dpi & 1
    place = dpi >> 1
    idx = jnp.stack([me, core, place]).astype(jnp.int32)
    tokens, width = block_input.shape[1:]
    ns = nu_log.shape[0]
    states = ns * mp
    hid = glu_weight.shape[2]
    chunk = tokens // CHUNKS
    per = STEP_ROWS // CHUNKS
    steps = tokens // STEP_ROWS
    x = block_input.reshape(CHUNKS, chunk, width)
    cot = out_cotangent.reshape(CHUNKS, chunk, width)
    gain, bias, skp = ln_gain[None], ln_bias[None], skip[None]

    def over_core(v):
        return lax.ppermute(v, "dp", xor_pairs(dp, 1))

    def over_plane(v, s):
        return lax.ppermute(v, "dp", xor_pairs(dp, 2 * s))

    def over_mp(v, s):
        return lax.ppermute(v, "mp", xor_pairs(mp, s))

    here = (jnp.arange(mp) == me).astype(F32)[:, None]

    def placed(v):
        return (here * v[None]).reshape(-1)

    def thirds(v):
        high, rest = high_low(v)
        return [high, rest, lax.reduce_precision(v - high - rest, 8, 7)]

    first_rows = [placed(nu_log), placed(gamma_log)], [placed(theta_log), placed(gamma_log)]
    first_rows = jnp.concatenate([jnp.stack(v) for v in first_rows], 1)
    bias_rows = jnp.stack([placed(glu_bias[p].astype(F32)) for p in range(2)])
    first_rows, bias_rows = lax.optimization_barrier((first_rows, bias_rows))
    params = jnp.concatenate(thirds(first_rows) + [bias_rows]).astype(BF16)
    params = jnp.pad(params, ((0, PARAM_ROWS - params.shape[0]), (0, 0)))

    def gathered(value, name):
        with jax.named_scope(name):
            return [value] + [over_mp(value, s) for s in range(1, mp)]

    def packed(parts, *earlier):
        value = parts[0]
        parts = lax.optimization_barrier(tuple(parts) + earlier)[: len(parts)]
        shape = (mp,) + value.shape
        return call(pack_rows, 1, [(idx, None)] + [(p, None) for p in parts], [(shape, value.dtype, None)], [], 1, 0, 0)[0]

    def tied(value, *earlier):
        return lax.optimization_barrier((value,) + earlier)[0]

    in_part = lax.dynamic_index_in_dim(in_weight, core, 1, keepdims=False).T
    out_part = lax.dynamic_index_in_dim(out_weight, core, 0, keepdims=False)
    glu_part = lax.dynamic_index_in_dim(glu_weight, core, 1, keepdims=False).T
    in_send = jnp.concatenate([in_part, params])
    both_part = jnp.concatenate([out_part, glu_part])
    x = tied(x, in_send, both_part)
    in_parts = gathered(in_send, "gather_in")

    chunked = pl.BlockSpec((CHUNKS, per, width), lambda i, idx: (0, i, 0))
    vector = pl.BlockSpec((1, width), lambda i, idx: (0, 0))
    rowed = pl.BlockSpec((STEP_ROWS, width), lambda i, idx: (i, 0))
    big = (tokens, width)
    npar = 8 + mp
    product = 2 * tokens * width * width
    small = ((8, width), F32, None)

    def scratch(*kinds):
        return [((rows, cols), kind) for rows, cols, kind in kinds]

    xhat, norm, rstd = call(
        prepare, steps,
        [(idx, None), (x, chunked), (gain, vector), (bias, vector)],
        [(big, F32, None), (big, BF16, None), ((tokens, 128), F32, None)],
        [], 6, product, 12, None, True,
    )
    in_parts = list(lax.optimization_barrier(tuple(in_parts) + (norm,))[:-1])
    both_own = gathered(tied(both_part, *in_parts[1:]), "gather_out_glu")
    in_own = packed(in_parts, norm)
    in_other = over_core(in_own)
    (cotlow,) = call(lower, steps, [(idx, None), (tied(cot, in_own), chunked)], [(big, BF16, None)], [], 5, 0, 8)
    norm = tied(norm, cotlow)
    src, wt, par, ends, last = call(
        partial(first_scan, chunk, mp), 1,
        [(idx, None), (norm, None), (in_own, None), (in_other, None)],
        [(big, F32, None), ((width, width), BF16, None), ((npar, width), F32, None), ((CHUNKS, width), F32, None), small],
        scratch((CHUNKS, width, F32), (BLOCK, width, F32), (BLOCK, width, F32)), 5, product, 8,
    )
    with jax.named_scope("carry"):
        lasts = [over_mp(last, s) for s in range(1, mp)]
    both_own = packed(both_own, *lasts)
    both_other = over_core(both_own)
    state, act, slope, wc = call(
        partial(readout, mp), 1,
        [(idx, None), (xhat, None), (src, None), (par, None), (ends, None), (gain, vector), (bias, vector), (skp, vector),
         (both_own, None), (both_other, None)] + [(v, None) for v in lasts],
        [(big, BF16, None), (big, BF16, None), (big, F32, None), ((width, width), BF16, None)],
        scratch((CHUNKS, width, F32), (BLOCK, width, BF16), (BLOCK, width, BF16), (BLOCK, width, F32), (BLOCK, width, F32)), 8, product, 8,
    )
    branch, gpre, wg, vec_glu = call(
        partial(gating, mp), 1,
        [(idx, None), (cotlow, None), (act, None), (par, None), (both_own, None), (both_other, None)],
        [(big, BF16, None), ((tokens, 2 * width), BF16, None), ((2 * width, width), BF16, None), small],
        scratch((BLOCK, 2 * width, F32), (BLOCK, 2 * width, F32)),
        10, 2 * product, 8,
    )
    gmix, gs, adj, first, vec_skip = call(
        unmix, 1,
        [(idx, None), (gpre, None), (slope, None), (norm, None), (wg, None), (wc, None), (par, None)],
        [(big, BF16, None), (big, F32, None), ((CHUNKS, width), F32, None), small, small],
        scratch((BLOCK, width, F32), (BLOCK, width, F32), (BLOCK, width, BF16),
                (BLOCK, width, BF16), (BLOCK, width, F32), (BLOCK, width, F32)),
        10, 4 * product, 8,
    )
    with jax.named_scope("carry_back"):
        firsts = [over_mp(first, s) for s in range(1, mp)]
    early_rows = mp * (hid + ns)
    half_rows = early_rows + states
    sums = [((half_rows, width), F32, None), ((half_rows, width), BF16, None)]
    keep, send = call(
        weight_products, 1,
        [(idx, None), (tied(gpre, first), None), (act, None), (state, None), (gmix, None)],
        sums, [], 12, 0, 0,
    )
    firsts[0] = tied(firsts[0], send)
    gdrive, keep, send, vec_lam = call(
        partial(adjoint_scan, mp), 1,
        [(idx, None), (keep, None), (send, None), (gs, None), (state, None), (src, None), (norm, None), (par, None),
         (adj, None)] + [(v, None) for v in firsts],
        [(big, BF16, None)] + sums + [small],
        scratch((width, width, F32), (CHUNKS, width, F32), (BLOCK, width, BF16),
                (BLOCK, width, BF16)), 8, product, 8, {1: 1, 2: 2},
    )
    with jax.named_scope("sum_core"):
        got = over_core(send)
    height = mp * (hid + 2 * ns) // plane
    if ns // plane % 16 == 0 and hid // plane % 16 == 0:
        own_piece, *sends = call(
            partial(split_pieces, mp, plane, (hid, ns, ns)), 1,
            [(idx, None), (keep, None), (got, None)],
            [((height, width), F32, None)] + [((height, width), BF16, None)] * (plane - 1), [], 4, 0, 0,
        )
    else:
        both = keep + got.astype(F32)
        both = [both[: mp * hid], both[mp * hid : early_rows], both[early_rows:]]
        both = jnp.concatenate([v.reshape(mp, plane, -1, width) for v in both], 2).swapaxes(0, 1)
        sends = [lax.dynamic_index_in_dim(both, place ^ s, 0, keepdims=False) for s in range(plane)]
        sends = [v.reshape(-1, width) for v in sends]
        own_piece, sends = sends[0], [v.astype(BF16) for v in sends[1:]]
    with jax.named_scope("sum_plane"):
        pieces = [over_plane(v, s + 1) for s, v in enumerate(sends)]
    gx, y, vec, vec_rows = call(
        norm_back, steps,
        [(idx, None), (cot, None), (tied(gdrive, own_piece), None), (wt, None), (gmix, None), (xhat, None), (rstd, None),
         (gain, vector), (skp, vector), (x, chunked), (branch, None), (vec_skip, None), (vec_glu, None),
         (vec_lam, None)],
        [((CHUNKS, chunk, width), F32, chunked), ((CHUNKS, chunk, width), F32, chunked), small, ((16, width), BF16, None)],
        scratch((BLOCK, width, F32), (BLOCK, width, F32), (STEP_ROWS, width, F32), (8, width, F32)), 18, product, 8,
    )
    pieces[0], own_piece, nu_log, theta_log, me, core, place = lax.optimization_barrier(
        (pieces[0], own_piece, nu_log, theta_log, me, core, place, vec)
    )[:7]
    rows = tree_sum([own_piece] + [p.astype(F32) for p in pieces]).reshape(mp, -1, width)
    with jax.named_scope("sum_mp"):
        got, vecs = [lax.dynamic_index_in_dim(rows, me, 0, keepdims=False)], [vec]
        n = got[0].shape[0]
        for s in range(1, mp):
            send = lax.dynamic_index_in_dim(rows, me ^ s, 0, keepdims=False).astype(BF16)
            buffer = over_mp(jnp.concatenate([send, vec_rows]), s)
            got.append(buffer[:n].astype(F32))
            vecs.append(vector_sum(buffer[n:]))
    piece, vec = tree_sum(got).astype(BF16), tree_sum(vecs)
    with jax.named_scope("spread_plane"):
        vec, vec_rows = vector_rows(vec)
        piece = jnp.concatenate([piece, vec_rows])
        stack = [piece] + [over_plane(piece, s) for s in range(1, plane)]
    vec = tree_sum([vec] + [vector_sum(v[n:]) for v in stack[1:]])
    vec, vec_rows = vector_rows(vec)
    own = jnp.concatenate([v[:n] for v in stack] + [vec_rows])
    with jax.named_scope("spread_core"):
        got = over_core(own)
    line = pl.BlockSpec((1, width), lambda i, idx: (0, 0))
    share = pl.BlockSpec((1, ns), lambda i, idx: (0, 0))
    shared = [((1, width), F32, line)] * 3 + [((1, ns), F32, share)] * 3
    shared.append(((2, hid), F32, pl.BlockSpec((2, hid), lambda i, idx: (0, 0))))
    logs = [(nu_log[None], None), (theta_log[None], None)]
    if ns // plane % 16 == 0 and hid // plane % 16 == 0:
        whole = pl.BlockSpec((2, ns, width), lambda i, idx: (0, 0, 0))
        grad_in, grad_out_weight, grad_glu, *vectors = call(
            partial(finish, hid, ns, plane), 1,
            [(idx, None), (own, None), (got, None)] + logs,
            [((2, ns, width), F32, whole), ((2, ns, width), F32, whole), ((2, hid, width), F32, None)] + shared,
            [], 8, 0, 0,
        )
    else:
        vec = vec + vector_sum(got[plane * n :])
        vectors = call(partial(small_outputs, hid, ns), 1, [(idx, None), (vec, None)] + logs, shared, [], 2, 0, 0)
        pieces = [flip(v[: plane * n].reshape(plane, n, width), place) for v in (own, got)]
        total = flip(jnp.stack(pieces), core).astype(F32)
        nh, nr = hid // plane, ns // plane

        def part(start, size):
            return total[:, :, start : start + size].reshape(2, -1, width)

        grad_glu, grad_out, grad_in = part(0, nh), part(nh, nr), part(nh + nr, nr)
        grad_out_weight = jnp.stack([grad_out[0], -grad_out[1]])
    grad_ln_gain, grad_ln_bias, grad_skip, grad_nu, grad_theta, grad_gamma, grad_glu_bias = vectors
    return (
        y.reshape(block_input.shape),
        gx.reshape(block_input.shape),
        grad_ln_gain[0],
        grad_ln_bias[0],
        grad_nu[0],
        grad_theta[0],
        grad_gamma[0],
        grad_in.transpose(2, 0, 1),
        grad_out_weight,
        grad_skip[0],
        grad_glu.transpose(2, 0, 1),
        grad_glu_bias,
    )


def solution(mesh):
    in_specs = (
        P("dp", "mp", None), P(), P(), P("mp"), P("mp"), P("mp"), P(None, None, "mp"), P(None, "mp", None), P(),
        P(None, None, "mp"), P(None, "mp"), P("dp", "mp", None),
    )
    out_specs = (
        P("dp", "mp", None), P("dp", "mp", None), P(), P(), P("mp"), P("mp"), P("mp"), P(None, None, "mp"),
        P(None, "mp", None), P(), P(None, None, "mp"), P(None, "mp"),
    )
    return jax.shard_map(on_device, mesh=mesh, in_specs=in_specs, out_specs=out_specs, check_vma=False)
```

```python
from functools import partial

import jax
import jax.numpy as jnp
from jax import lax
from jax.experimental import pallas as pl
from jax.experimental.pallas import tpu as pltpu
from jax.sharding import PartitionSpec as P

EPS = 1e-05
F32 = jnp.float32
BF16 = jnp.bfloat16
CHUNKS = 16
STEP_ROWS = 512
BLOCK = 256
PARAM_ROWS = 16
MIB = 1024 * 1024
INV_SQRT2 = 0.7071067811865476
INV_SQRT_2PI = 0.3989422804014327


def nt(a, b):
    return lax.dot_general(a, b, (((1,), (1,)), ((), ())), preferred_element_type=F32)


def nn(a, b):
    return lax.dot_general(a, b, (((1,), (0,)), ((), ())), preferred_element_type=F32)


def tn(a, b):
    return lax.dot_general(a, b, (((0,), (0,)), ((), ())), preferred_element_type=F32)


def cmul(ar, ai, br, bi):
    return ar * br - ai * bi, ar * bi + ai * br


def cpower(re, im, log2):
    for _ in range(log2):
        re, im = cmul(re, im, re, im)
    return re, im


def log2_of(n):
    return n.bit_length() - 1


def block_rows(step, block):
    if isinstance(step, int):
        return slice(block * BLOCK, (block + 1) * BLOCK)
    return pl.ds(pl.multiple_of(step * STEP_ROWS + block * BLOCK, BLOCK), BLOCK)


def tile_rows(step, start):
    if isinstance(step, int):
        return slice(step * STEP_ROWS + start, step * STEP_ROWS + start + 16)
    return pl.ds(pl.multiple_of(step * STEP_ROWS + start, 16), 16)


def alternate(first, second):
    i = j = 0
    while i < len(first) or j < len(second):
        if j >= len(second) or (i < len(first) and i * len(second) <= j * len(first)):
            first[i]()
            i += 1
        else:
            second[j]()
            j += 1


def run(pieces):
    for piece in pieces:
        piece()


def product_nt(out, left, right, size=256):
    def piece(n):
        out[:, n : n + size] = nt(left(), right[n : n + size, :])

    return [partial(piece, n) for n in range(0, right.shape[0], size)]


def product_nn(out, left, right, size=256):
    def piece(n):
        out[:, n : n + size] = nn(left(), right[:, n : n + size])

    return [partial(piece, n) for n in range(0, right.shape[1], size)]


def product_tn(total, left, right, size=256):
    def piece(n):
        total[n : n + size, :] += tn(left(slice(n, n + size)), right())

    return [partial(piece, n) for n in range(0, total.shape[0], size)]


def assemble(dst, own, other, first, rows, me, core, slots, negate_second):
    for slot in range(slots):
        for part in range(2):
            mine = own[me ^ slot, first : first + rows, :]
            theirs = other[me ^ slot, first : first + rows, :]
            value = jnp.where(core == part, mine, theirs)
            start = (part * slots + slot) * rows
            dst[start : start + rows, :] = -value if negate_second and part == 1 else value


def prepare(idx, x_ref, gain_ref, bias_ref, xhat_ref, norm_ref, rstd_ref):
    step = pl.program_id(0)
    width = x_ref.shape[2]
    per = x_ref.shape[1]
    gain, bias = gain_ref[...], bias_ref[...]
    for k in range(0, per, 8):
        rows = jnp.swapaxes(x_ref[:, k : k + 8, :], 0, 1).reshape(8 * CHUNKS, width)
        for r in range(0, 8 * CHUNKS, 16):
            place = tile_rows(step, k * CHUNKS + r)
            part = rows[r : r + 16]
            mean = jnp.mean(part, -1, keepdims=True)
            cen = part - mean
            var = jnp.mean(cen * cen, -1, keepdims=True)
            rstd = lax.rsqrt(var + EPS)
            xhat = cen * rstd
            xhat_ref[place, :] = xhat
            rstd_ref[place, :] = jnp.broadcast_to(rstd, (16, 128))
            norm_ref[place, :] = (xhat * gain + bias).astype(BF16)


def lower(idx, cot_ref, cotlow_ref):
    step = pl.program_id(0)
    width = cot_ref.shape[2]
    for k in range(0, cot_ref.shape[1], 8):
        rows = jnp.swapaxes(cot_ref[:, k : k + 8, :], 0, 1).reshape(8 * CHUNKS, width)
        place = pl.ds(pl.multiple_of(step * STEP_ROWS + k * CHUNKS, 128), 8 * CHUNKS)
        cotlow_ref[place, :] = rows.astype(BF16)


def first_scan(
    chunk, mp, idx, norm_ref, own_ref, other_ref, glu_bias_ref,
    src_ref, wt_ref, par_ref, ends_ref, last_ref, h_ref, drive_a, drive_b,
):
    step = 0
    width = norm_ref.shape[1]
    states = width // 2
    ns = states // mp

    me, core = idx[0], idx[1]
    assemble(wt_ref, own_ref, other_ref, 0, ns, me, core, mp, False)
    total = own_ref[0, ns : ns + PARAM_ROWS, :].astype(F32)
    for s in range(1, mp):
        total = total + own_ref[s, ns : ns + PARAM_ROWS, :].astype(F32)
    decay = total[0:1] + total[2:3] + total[4:5]
    gamma = jnp.exp(total[1:2] + total[3:4] + total[5:6])
    radius = jnp.exp(-jnp.exp(decay[:, :states]))
    turn = jnp.exp(decay[:, states:])
    re, im = radius * jnp.cos(turn), radius * jnp.sin(turn)
    lre, lim = cpower(re, im, log2_of(chunk))
    tre, tim = cpower(lre, lim, log2_of(CHUNKS))
    par_ref[0:1, :] = jnp.concatenate([re, im], 1)
    par_ref[1:2, :] = gamma
    par_ref[2:3, :] = jnp.concatenate([lre, lim], 1)
    par_ref[3:8, :] = jnp.zeros((5, width), F32)
    pre, pim = jnp.ones_like(tre), jnp.zeros_like(tim)
    for s in range(mp):
        par_ref[8 + s : 9 + s, :] = jnp.concatenate([pre, pim], 1)
        pre, pim = cmul(pre, pim, tre, tim)

    gam = par_ref[1:2, :]
    lre, lim = par_ref[0:1, :states], par_ref[0:1, states:]
    h = [jnp.zeros((CHUNKS, states), F32)] * 2

    def drive_pieces(b, drive):
        return product_nt(drive, lambda: norm_ref[block_rows(step, b), :], wt_ref)

    def scan_piece(b, drive, r):
        hre, him = h
        src = drive[r : r + CHUNKS, :] * gam
        src_ref[tile_rows(step, b * BLOCK + r), :] = src
        h[0] = src[:, :states] + lre * hre - lim * him
        h[1] = src[:, states:] + lre * him + lim * hre

    def scan_pieces(b, drive):
        return [partial(scan_piece, b, drive, r) for r in range(0, BLOCK, CHUNKS)]

    blocks = norm_ref.shape[0] // BLOCK
    drives = (drive_a, drive_b)
    run(drive_pieces(0, drive_a))
    for b in range(blocks):
        more = drive_pieces(b + 1, drives[(b + 1) % 2]) if b + 1 < blocks else []
        alternate(more, scan_pieces(b, drives[b % 2]))
    h_ref[:, :states], h_ref[:, states:] = h
    ends_ref[...] = h_ref[...]
    pre, pim = par_ref[2:3, :states], par_ref[2:3, states:]
    re, im = h_ref[0:1, :states], h_ref[0:1, states:]
    for c in range(1, CHUNKS):
        mre, mim = cmul(pre, pim, re, im)
        re, im = mre + h_ref[c : c + 1, :states], mim + h_ref[c : c + 1, states:]
    last_ref[...] = jnp.zeros_like(last_ref)
    last_ref[0:1, :] = jnp.concatenate([re, im], 1)
    hid = glu_bias_ref.shape[1]
    biases = glu_bias_ref[...].astype(F32)
    for j in range(mp):
        last_ref[1:3, j * hid : (j + 1) * hid] = jnp.where(me == j, biases, 0.0)


def gelu_parts(v):
    cdf = 0.5 * (1.0 + lax.erf(v * INV_SQRT2))
    pdf = jnp.exp(-0.5 * v * v) * INV_SQRT_2PI
    return v * cdf, cdf + v * pdf


def readout(mp, idx, xhat_ref, src_ref, par_ref, ends_ref, gain_ref, bias_ref, skip_ref, own_ref, other_ref, *rest):
    others, mine = rest[: mp - 1], rest[mp - 1]
    (state_ref, act_ref, slope_ref, wc_ref, rows_ref, h_ref, low_a, low_b, mix_a, mix_b) = rest[mp:]
    step = 0
    width = xhat_ref.shape[1]
    states = width // 2
    me, core = idx[0], idx[1]

    assemble(wc_ref, own_ref, other_ref, 0, states // mp, me, core, mp, True)
    total = mine[...]
    for other in others:
        total = total + other[...]
    rows_ref[...] = total
    re = jnp.zeros((1, states), F32)
    im = jnp.zeros((1, states), F32)
    for s in range(1, mp):
        j = me ^ s
        power = jnp.maximum(me - 1 - j, 0)
        row = par_ref[pl.ds(8 + power, 1), :]
        sre, sim = cmul(row[:, :states], row[:, states:], others[s - 1][0:1, :states], others[s - 1][0:1, states:])
        keep = (j < me).astype(F32)
        re, im = re + keep * sre, im + keep * sim
    lre, lim = par_ref[2:3, :states], par_ref[2:3, states:]
    for c in range(CHUNKS):
        h_ref[c : c + 1, :states] = re
        h_ref[c : c + 1, states:] = im
        mre, mim = cmul(lre, lim, re, im)
        re, im = mre + ends_ref[c : c + 1, :states], mim + ends_ref[c : c + 1, states:]

    lre, lim = par_ref[0:1, :states], par_ref[0:1, states:]
    h = [h_ref[:, :states], h_ref[:, states:]]

    def scan_piece(b, low, r):
        hre, him = h
        rows = tile_rows(step, b * BLOCK + r)
        hre, him = (
            src_ref[rows, :states] + lre * hre - lim * him,
            src_ref[rows, states:] + lre * him + lim * hre,
        )
        low[r : r + CHUNKS, :states] = hre.astype(BF16)
        low[r : r + CHUNKS, states:] = him.astype(BF16)
        state_ref[rows, :] = low[r : r + CHUNKS, :]
        h[0], h[1] = hre, him

    def gelu_piece(b, mix, r):
        rows = tile_rows(step, b * BLOCK + r)
        for c in range(0, width, 128):
            cols = slice(c, c + 128)
            normed = xhat_ref[rows, cols] * gain_ref[:, cols] + bias_ref[:, cols]
            lru = mix[r : r + 16, cols] + skip_ref[:, cols] * normed
            act, slope = gelu_parts(lru)
            act_ref[rows, cols] = act.astype(BF16)
            slope_ref[rows, cols] = slope

    def scans(b, low):
        return [partial(scan_piece, b, low, r) for r in range(0, BLOCK, CHUNKS)]

    def mixes(low, mix):
        return product_nn(mix, lambda: low[...], wc_ref)

    def gelus(b, mix):
        return [partial(gelu_piece, b, mix, r) for r in range(0, BLOCK, 16)]

    blocks = src_ref.shape[0] // BLOCK
    lows, mix_refs = (low_a, low_b), (mix_a, mix_b)
    run(scans(0, low_a))
    for b in range(blocks):
        other = scans(b + 1, lows[(b + 1) % 2]) if b + 1 < blocks else []
        other = (gelus(b - 1, mix_refs[(b - 1) % 2]) if b else []) + other
        alternate(mixes(lows[b % 2], mix_refs[b % 2]), other)
    run(gelus(blocks - 1, mix_refs[(blocks - 1) % 2]))


def gating(mp, idx, cotlow_ref, act_ref, rows_ref, own_ref, other_ref,
           br_ref, gpre_ref, wg_ref, vec_ref, pre_a, pre_b):
    width = act_ref.shape[1]
    core = idx[1]
    assemble(wg_ref, own_ref, other_ref, width // 2 // mp, width // mp, idx[0], core, mp, False)
    vec_ref[...] = jnp.zeros_like(vec_ref)
    blocks = act_ref.shape[0] // BLOCK
    buffers = (pre_a, pre_b)

    def pre_pieces(b):
        return product_nt(buffers[b % 2], lambda: act_ref[b * BLOCK : (b + 1) * BLOCK, :], wg_ref) if b < blocks else []

    sums = {}

    def gate_piece(b, start, c):
        pre = buffers[b % 2]
        cols = slice(c, c + 128)
        gate_cols = slice(width + c, width + c + 128)
        for r in range(start, start + 64, 16):
            rows = slice(b * BLOCK + r, b * BLOCK + r + 16)
            value = pre[r : r + 16, cols] + rows_ref[1:2, cols]
            gate = pre[r : r + 16, gate_cols] + rows_ref[2:3, cols]
            sig = 0.5 * jnp.tanh(0.5 * gate) + 0.5
            branch = value * sig
            br_ref[rows, cols] = branch.astype(BF16)
            g = cotlow_ref[rows, cols].astype(F32)
            g_value = g * sig
            g_gate = g * branch * (1.0 - sig)
            gpre_ref[rows, cols] = g_value.astype(BF16)
            gpre_ref[rows, gate_cols] = g_gate.astype(BF16)
            for key, part in ((("value", c), g_value), (("gate", c), g_gate)):
                sums[key] = sums[key] + part if key in sums else part

    def gate_pieces(b):
        return [partial(gate_piece, b, start, c) for start in range(0, BLOCK, 64) for c in range(0, width, 128)]

    run(pre_pieces(0))
    for b in range(blocks):
        alternate(pre_pieces(b + 1), gate_pieces(b))
        for c in range(0, width, 128):
            vec_ref[1:2, c : c + 128] += jnp.sum(sums.pop(("value", c)), 0, keepdims=True)
            vec_ref[2:3, c : c + 128] += jnp.sum(sums.pop(("gate", c)), 0, keepdims=True)


def weight_products(idx, gpre_ref, act_ref, state_ref, gmix_ref, keep_ref, send_ref):
    core = idx[1]

    def product(left_ref, right_ref, first):
        columns = left_ref.shape[1]
        size = columns // 2
        for n in range(0, columns, 256):
            total = tn(left_ref[:, n : n + 256], right_ref[...])
            here = slice(first + n % size, first + n % size + 256)

            @pl.when(core == n // size)
            def _():
                keep_ref[here, :] = total

            @pl.when(core != n // size)
            def _():
                send_ref[here, :] = total.astype(BF16)

    product(gpre_ref, act_ref, 0)
    product(state_ref, gmix_ref, gpre_ref.shape[1] // 2)


def unmix(idx, gpre_ref, slope_ref, norm_ref, wg_ref, wc_ref, par_ref,
          gmix_ref, gs_ref, adj_ref, first_ref, vec_ref, ga_a, ga_b, gmix_a, gmix_b, gs_a, gs_b):
    step = 0
    width = norm_ref.shape[1]
    states = width // 2
    core = idx[1]

    vec_ref[...] = jnp.zeros_like(vec_ref)
    sums = {}

    def act_pieces(b, ga):
        return product_nn(ga, lambda: gpre_ref[block_rows(step, b), :], wg_ref)

    def lru_piece(b, ga, gmix, r):
        rows = tile_rows(step, b * BLOCK + r)
        for c in range(0, width, 128):
            cols = slice(c, c + 128)
            g_lru = ga[r : r + 16, cols] * slope_ref[rows, cols]
            low = g_lru.astype(BF16)
            gmix[r : r + 16, cols] = low
            gmix_ref[rows, cols] = low
            part = g_lru * norm_ref[rows, cols].astype(F32)
            sums[c] = sums[c] + part if c in sums else part

    def lru_pieces(b, ga, gmix):
        return [partial(lru_piece, b, ga, gmix, r) for r in range(0, BLOCK, 16)]

    def mix_pieces(b, gs, gmix):
        return product_nt(gs, lambda: gmix[...], wc_ref)

    lre, lim = par_ref[0:1, :states], par_ref[0:1, states:]
    power = [jnp.ones((8, states), F32), jnp.zeros((8, states), F32)]
    are = [jnp.zeros((8, states), F32) for _ in range(0, CHUNKS, 8)]
    aim = [jnp.zeros((8, states), F32) for _ in range(0, CHUNKS, 8)]

    def end_piece(b, gs, r):
        pre, pim = power
        for n, c in enumerate(range(0, CHUNKS, 8)):
            gre, gim = gs[r + c : r + c + 8, :states], gs[r + c : r + c + 8, states:]
            mre, mim = cmul(pre, pim, gre, gim)
            are[n], aim[n] = are[n] + mre, aim[n] + mim
        gs_ref[tile_rows(step, b * BLOCK + r), :] = gs[r : r + CHUNKS, :]
        power[0], power[1] = pre * lre + pim * lim, pim * lre - pre * lim

    def end_pieces(b, gs):
        return [partial(end_piece, b, gs, r) for r in range(0, BLOCK, CHUNKS)]

    blocks = gpre_ref.shape[0] // BLOCK
    gas, gmixes, gss = (ga_a, ga_b), (gmix_a, gmix_b), (gs_a, gs_b)
    run(act_pieces(0, ga_a))
    for b in range(blocks + 2):
        products = act_pieces(b + 1, gas[(b + 1) % 2]) if b + 1 < blocks else []
        products += mix_pieces(b - 1, gss[(b - 1) % 2], gmixes[(b - 1) % 2]) if 0 <= b - 1 < blocks else []
        other = lru_pieces(b, gas[b % 2], gmixes[b % 2]) if b < blocks else []
        other += end_pieces(b - 2, gss[b % 2]) if b >= 2 else []
        alternate(products, other)
    for c in range(0, width, 128):
        vec_ref[0:1, c : c + 128] += jnp.sum(sums[c], 0, keepdims=True)
    for n, c in enumerate(range(0, CHUNKS, 8)):
        adj_ref[c : c + 8, :states] = are[n]
        adj_ref[c : c + 8, states:] = aim[n]
    lre, lim = par_ref[2:3, :states], -par_ref[2:3, states:]
    last = CHUNKS - 1
    re, im = adj_ref[last : last + 1, :states], adj_ref[last : last + 1, states:]
    for c in range(CHUNKS - 2, -1, -1):
        mre, mim = cmul(lre, lim, re, im)
        re, im = mre + adj_ref[c : c + 1, :states], mim + adj_ref[c : c + 1, states:]
    first_ref[...] = jnp.broadcast_to(jnp.concatenate([re, im], 1), first_ref.shape)


def adjoint_scan(mp, idx, gs_ref, state_ref, src_ref, norm_ref, par_ref, adj_ref, *rest):
    others = rest[: mp - 1]
    (gdrive_ref, keep_ref, send_ref, vec_ref, acc_ref, h_ref, gdrive_a, gdrive_b) = rest[mp - 1 :]
    step = 0
    width = gs_ref.shape[1]
    states = width // 2
    me, core = idx[0], idx[1]

    re = jnp.zeros((1, states), F32)
    im = jnp.zeros((1, states), F32)
    for s in range(1, mp):
        j = me ^ s
        power = jnp.maximum(j - me - 1, 0)
        row = par_ref[pl.ds(8 + power, 1), :]
        sre, sim = cmul(row[:, :states], -row[:, states:], others[s - 1][0:1, :states], others[s - 1][0:1, states:])
        keep = (j > me).astype(F32)
        re, im = re + keep * sre, im + keep * sim
    lre, lim = par_ref[2:3, :states], -par_ref[2:3, states:]
    for c in range(CHUNKS - 1, -1, -1):
        h_ref[c : c + 1, :states] = re
        h_ref[c : c + 1, states:] = im
        mre, mim = cmul(lre, lim, re, im)
        re, im = mre + adj_ref[c : c + 1, :states], mim + adj_ref[c : c + 1, states:]
    acc_ref[...] = jnp.zeros_like(acc_ref)

    lre, lim = par_ref[0:1, :states], par_ref[0:1, states:]
    gam = par_ref[1:2, :states]
    h = [h_ref[:, :states], h_ref[:, states:]]
    sums = [jnp.zeros((CHUNKS, states), F32)] * 3

    def scan_piece(b, gdrive, r):
        hre, him = h
        rows = tile_rows(step, b * BLOCK + r)
        tre, tim = state_ref[rows, :states].astype(F32), state_ref[rows, states:].astype(F32)
        sums[0] = sums[0] + (hre * tre + him * tim)
        sums[1] = sums[1] + (him * tre - hre * tim)
        hre, him = (
            gs_ref[rows, :states] + lre * hre + lim * him,
            gs_ref[rows, states:] + lre * him - lim * hre,
        )
        sums[2] = sums[2] + (hre * src_ref[rows, :states] + him * src_ref[rows, states:])
        gdrive[r : r + CHUNKS, :states] = (hre * gam).astype(BF16)
        gdrive[r : r + CHUNKS, states:] = (him * gam).astype(BF16)
        gdrive_ref[rows, :] = gdrive[r : r + CHUNKS, :]
        h[0], h[1] = hre, him

    def scans(b, gdrive):
        return [partial(scan_piece, b, gdrive, r) for r in range(BLOCK - CHUNKS, -1, -CHUNKS)]

    def weight_pieces(b, gdrive):
        return product_tn(acc_ref, lambda cols: gdrive[:, cols], lambda: norm_ref[block_rows(step, b), :])

    last = gs_ref.shape[0] // BLOCK - 1
    buffers = (gdrive_a, gdrive_b)
    run(scans(last, buffers[last % 2]))
    for b in range(last - 1, -1, -1):
        alternate(weight_pieces(b + 1, buffers[(b + 1) % 2]), scans(b, buffers[b % 2]))
    run(weight_pieces(0, buffers[0]))
    keep_ref[...] = acc_ref[pl.ds(core * states, states), :]
    send_ref[...] = acc_ref[pl.ds((1 - core) * states, states), :].astype(BF16)
    sre, sim, sgam = [jnp.sum(v, 0, keepdims=True) for v in sums]
    vec_ref[0:1, :] = jnp.concatenate([sre, sim], 1)
    vec_ref[1:2, :] = jnp.concatenate([sgam, jnp.zeros((1, states), F32)], 1)
    vec_ref[2:8, :] = jnp.zeros((6, width), F32)


def norm_back(idx, cot_ref, gdrive_ref, wt_ref, gmix_ref, xhat_ref, rstd_ref, gain_ref, skip_ref, x_ref, br_ref,
              vec_skip_ref, vec_glu_ref, vec_lam_ref, gx_ref, y_ref, parts_ref, send_ref, gn_a, gn_b, dx_ref, vec_ref):
    step = pl.program_id(0)
    width = cot_ref.shape[2]
    per = STEP_ROWS // CHUNKS

    @pl.when(step == 0)
    def _():
        vec_ref[...] = jnp.zeros_like(vec_ref)

    def normed_pieces(block, gn):
        rows = pl.ds(pl.multiple_of(block * BLOCK, BLOCK), BLOCK)
        return product_nn(gn, lambda: gdrive_ref[rows, :], wt_ref)

    @pl.when(step == 0)
    def _():
        run(normed_pieces(0, gn_a))

    sums = [jnp.zeros((16, width), F32), jnp.zeros((16, width), F32)]

    def norm_piece(b, gn, r):
        rows = tile_rows(step, b * BLOCK + r)
        xhat = xhat_ref[rows, :]
        g = gn[r : r + 16, :] + skip_ref[...] * gmix_ref[rows, :].astype(F32)
        sums[0] = sums[0] + g * xhat
        sums[1] = sums[1] + g
        gh = g * gain_ref[...]
        first = jnp.mean(gh, -1, keepdims=True)
        second = jnp.mean(gh * xhat, -1, keepdims=True)
        rstd = jnp.concatenate([rstd_ref[rows, :]] * (width // 128), 1)
        dx_ref[b * BLOCK + r : b * BLOCK + r + 16, :] = rstd * (gh - first - xhat * second)

    def norm_pieces(b, gn):
        return [partial(norm_piece, b, gn, r) for r in range(0, BLOCK, 16)]

    def output_piece(k):
        rows = dx_ref[k * CHUNKS : (k + 8) * CHUNKS, :].reshape(8, CHUNKS, width)
        place = pl.ds(pl.multiple_of(step * per + k, 8), 8)
        gx_ref[:, k : k + 8, :] = cot_ref[:, place, :] + jnp.swapaxes(rows, 0, 1)

    def branch_piece(k):
        here = pl.ds(pl.multiple_of(step * STEP_ROWS + k * CHUNKS, 128), 8 * CHUNKS)
        rows = br_ref[here, :].astype(F32).reshape(8, CHUNKS, width)
        y_ref[:, k : k + 8, :] = x_ref[:, k : k + 8, :] + jnp.swapaxes(rows, 0, 1)

    after = jnp.minimum(2 * step + 2, gdrive_ref.shape[0] // BLOCK - 1)
    outputs = [partial(output_piece, k) for k in range(0, per, 8)]
    run([partial(branch_piece, k) for k in range(0, per, 8)])
    alternate(normed_pieces(2 * step + 1, gn_b), norm_pieces(0, gn_a))
    alternate(normed_pieces(after, gn_a), outputs[: len(outputs) // 2] + norm_pieces(1, gn_b) + outputs[len(outputs) // 2 :])
    vec_ref[0:1, :] += jnp.sum(sums[0], 0, keepdims=True)
    vec_ref[1:2, :] += jnp.sum(sums[1], 0, keepdims=True)

    @pl.when(step == pl.num_programs(0) - 1)
    def _():
        rows = [vec_skip_ref[0:1, :], vec_glu_ref[1:3, :], vec_ref[0:2, :], vec_lam_ref[0:2, :], jnp.zeros((1, width), F32)]
        vec = jnp.concatenate(rows, 0)
        high = vec.astype(BF16)
        low = (vec - high.astype(F32)).astype(BF16)
        parts_ref[...] = high.astype(F32) + low.astype(F32)
        send_ref[...] = jnp.concatenate([high.astype(F32), low.astype(F32)], 0).astype(BF16)


def pack_rows(idx, *refs):
    *parts, out = refs
    for i, part in enumerate(parts):
        out[i] = part[...]


def split_pieces(slots, count, hid, ns, idx, keep_ref, got_ref, in_keep_ref, in_got_ref, own_ref, *sends):
    place = idx[2]
    parts = ((keep_ref, got_ref, 0, hid), (keep_ref, got_ref, slots * hid, ns), (in_keep_ref, in_got_ref, 0, ns))
    height = (hid + 2 * ns) // count
    for slot in range(slots):
        for s in range(count):
            low = slot * height
            for keep, got, base, size in parts:
                rows = size // count
                start = pl.multiple_of(base + slot * size + (place ^ s) * rows, rows)
                piece = keep[pl.ds(start, rows), :] + got[pl.ds(start, rows), :].astype(F32)
                if s == 0:
                    own_ref[low : low + rows, :] = piece
                else:
                    sends[s - 1][low : low + rows, :] = piece.astype(BF16)
                low += rows


def finish(hid, ns, count, idx, own_ref, got_ref, nu_ref, theta_ref, in_ref, out_ref, glu_ref, *rest):
    core, place = idx[1], idx[2]
    height = (hid + 2 * ns) // count
    for part in range(2):
        for i in range(count):
            here = pl.ds(pl.multiple_of((i ^ place) * height, 16), height)
            rows = jnp.where(core == part, own_ref[here, :], got_ref[here, :]).astype(F32)
            low = 0
            for ref, size in ((glu_ref, hid // count), (out_ref, ns // count), (in_ref, ns // count)):
                value = rows[low : low + size]
                ref[part, i * size : (i + 1) * size, :] = -value if ref is out_ref and part == 1 else value
                low += size
    first = count * height
    both = [ref[first : first + 16, :].astype(F32) for ref in (own_ref, got_ref)]
    vec = (both[0][:8] + both[0][8:]) + (both[1][:8] + both[1][8:])
    vector_outputs(hid, ns, idx, vec, nu_ref, theta_ref, *rest)


def vector_outputs(hid, ns, idx, vec, nu_ref, theta_ref, gain_ref, bias_ref, skip_ref, nu_out, theta_out, gamma_out, glu_ref):
    me = idx[0]
    width = vec.shape[1]
    states = width // 2
    skip_ref[...] = vec[0:1, :]
    gain_ref[...] = vec[3:4, :]
    bias_ref[...] = vec[4:5, :]

    def share(rows, start, size, count):
        total = jnp.zeros((rows.shape[0], size), F32)
        for j in range(count):
            total = total + jnp.where(me == j, rows[:, start + j * size : start + (j + 1) * size], 0.0)
        return total

    glu_ref[...] = share(vec[1:3, :], 0, hid, width // hid)
    re = share(vec[5:6, :], 0, ns, states // ns)
    im = share(vec[5:6, :], states, ns, states // ns)
    gamma_out[...] = share(vec[6:7, :], 0, ns, states // ns)
    speed, turn = jnp.exp(nu_ref[...]), jnp.exp(theta_ref[...])
    radius = jnp.exp(-speed)
    cos, sin = radius * jnp.cos(turn), radius * jnp.sin(turn)
    nu_out[...] = -speed * (cos * re + sin * im)
    theta_out[...] = turn * (cos * im - sin * re)


def small_outputs(hid, ns, idx, vec_ref, *rest):
    vector_outputs(hid, ns, idx, vec_ref[...], *rest)


def call(kernel, steps, ins, outs, scratch, mib, flops, moved, in_place=None, first=False):
    def in_hbm(array, block):
        return array if block is None or (array.size < 65536 and not first) else pltpu.with_memory_space_constraint(array, pltpu.HBM)

    def spec(block):
        return pl.BlockSpec(memory_space=pltpu.VMEM) if block is None else block

    return pl.pallas_call(
        kernel,
        grid_spec=pltpu.PrefetchScalarGridSpec(
            num_scalar_prefetch=1,
            grid=(steps,),
            in_specs=[spec(block) for _, block in ins[1:]],
            out_specs=[spec(block) for _, _, block in outs],
            scratch_shapes=[pltpu.VMEM(*s) for s in scratch],
        ),
        out_shape=[jax.ShapeDtypeStruct(s, t) if block is None else pltpu.HBM(s, t) for s, t, block in outs],
        input_output_aliases=in_place or {},
        compiler_params=pltpu.CompilerParams(vmem_limit_bytes=mib * MIB),
        cost_estimate=pl.CostEstimate(flops=flops, bytes_accessed=moved * MIB, transcendentals=0),
    )(*[in_hbm(a, block) for a, block in ins])


def xor_pairs(n, s):
    return [(i, i ^ s) for i in range(n)]


def from_each(value, axis, n):
    return [value] + [lax.ppermute(value, axis, xor_pairs(n, s)) for s in range(1, n)]


def tree_sum(parts):
    parts = list(parts)
    while len(parts) > 1:
        parts = [parts[i] + parts[i + 1] for i in range(0, len(parts), 2)]
    return parts[0]


def high_low(v):
    high = lax.reduce_precision(v, 8, 7)
    return high, lax.reduce_precision(v - high, 8, 7)


def vector_rows(v):
    high, low = high_low(v)
    return high + low, jnp.concatenate([high, low]).astype(BF16)


def vector_sum(rows):
    n = rows.shape[0] // 2
    return rows[:n].astype(F32) + rows[n:].astype(F32)


def flip(stack, position):
    n = stack.shape[0]
    for b in range(log2_of(n)):
        pairs = stack.reshape((n >> (b + 1), 2, 1 << b) + stack.shape[1:])
        pairs = jnp.where((position >> b) & 1 == 1, pairs[:, ::-1], pairs)
        stack = pairs.reshape(stack.shape)
    return stack


def on_device(
    block_input, ln_gain, ln_bias, nu_log, theta_log, gamma_log, in_weight, out_weight, skip, glu_weight, glu_bias,
    out_cotangent,
):
    mp = lax.axis_size("mp")
    dp = lax.axis_size("dp")
    plane = dp // 2
    me = lax.axis_index("mp")
    dpi = lax.axis_index("dp")
    core = dpi & 1
    place = dpi >> 1
    idx = jnp.stack([me, core, place]).astype(jnp.int32)
    tokens, width = block_input.shape[1:]
    ns = nu_log.shape[0]
    states = ns * mp
    hid = glu_weight.shape[2]
    chunk = tokens // CHUNKS
    per = STEP_ROWS // CHUNKS
    steps = tokens // STEP_ROWS
    x = block_input.reshape(CHUNKS, chunk, width)
    cot = out_cotangent.reshape(CHUNKS, chunk, width)
    gain, bias, skp = ln_gain[None], ln_bias[None], skip[None]

    def over_core(v):
        return lax.ppermute(v, "dp", xor_pairs(dp, 1))

    def over_plane(v, s):
        return lax.ppermute(v, "dp", xor_pairs(dp, 2 * s))

    def over_mp(v, s):
        return lax.ppermute(v, "mp", xor_pairs(mp, s))

    here = (jnp.arange(mp) == me).astype(F32)[:, None]

    def placed(v):
        return (here * v[None]).reshape(-1)

    def thirds(v):
        high, rest = high_low(v)
        return [high, rest, lax.reduce_precision(v - high - rest, 8, 7)]

    first_rows = [placed(nu_log), placed(gamma_log)], [placed(theta_log), placed(gamma_log)]
    first_rows = jnp.concatenate([jnp.stack(v) for v in first_rows], 1)
    first_rows = lax.optimization_barrier(first_rows)
    params = jnp.concatenate(thirds(first_rows)).astype(BF16)
    params = jnp.pad(params, ((0, PARAM_ROWS - params.shape[0]), (0, 0)))

    def gathered(value, name):
        with jax.named_scope(name):
            return [value] + [over_mp(value, s) for s in range(1, mp)]

    def packed(parts, *earlier):
        value = parts[0]
        parts = lax.optimization_barrier(tuple(parts) + earlier)[: len(parts)]
        shape = (mp,) + value.shape
        return call(pack_rows, 1, [(idx, None)] + [(p, None) for p in parts], [(shape, value.dtype, None)], [], 1, 0, 0)[0]

    def tied(value, *earlier):
        return lax.optimization_barrier((value,) + earlier)[0]

    in_part = lax.dynamic_index_in_dim(in_weight, core, 1, keepdims=False).T
    out_part = lax.dynamic_index_in_dim(out_weight, core, 0, keepdims=False)
    glu_part = lax.dynamic_index_in_dim(glu_weight, core, 1, keepdims=False).T
    in_send = jnp.concatenate([in_part, params])
    both_part = jnp.concatenate([out_part, glu_part])
    x = tied(x, in_send, both_part)
    in_parts = gathered(in_send, "gather_in")

    chunked = pl.BlockSpec((CHUNKS, per, width), lambda i, idx: (0, i, 0))
    vector = pl.BlockSpec((1, width), lambda i, idx: (0, 0))
    rowed = pl.BlockSpec((STEP_ROWS, width), lambda i, idx: (i, 0))
    big = (tokens, width)
    npar = 8 + mp
    product = 2 * tokens * width * width
    small = ((8, width), F32, None)

    def scratch(*kinds):
        return [((rows, cols), kind) for rows, cols, kind in kinds]

    xhat, norm, rstd = call(
        prepare, steps,
        [(idx, None), (x, chunked), (gain, vector), (bias, vector)],
        [(big, F32, None), (big, BF16, None), ((tokens, 128), F32, None)],
        [], 6, product, 12, None, True,
    )
    in_parts = list(lax.optimization_barrier(tuple(in_parts) + (norm,))[:-1])
    both_own = gathered(tied(both_part, *in_parts[1:]), "gather_out_glu")
    in_own = packed(in_parts, norm)
    in_other = over_core(in_own)
    (cotlow,) = call(lower, steps, [(idx, None), (tied(cot, in_own), chunked)], [(big, BF16, None)], [], 5, 0, 8)
    norm = tied(norm, cotlow)
    src, wt, par, ends, last = call(
        partial(first_scan, chunk, mp), 1,
        [(idx, None), (norm, None), (in_own, None), (in_other, None), (glu_bias, None)],
        [(big, F32, None), ((width, width), BF16, None), ((npar, width), F32, None), ((CHUNKS, width), F32, None), small],
        scratch((CHUNKS, width, F32), (BLOCK, width, F32), (BLOCK, width, F32)), 5, product, 8,
    )
    with jax.named_scope("carry"):
        lasts = [over_mp(last, s) for s in range(1, mp)]
    both_own = packed(both_own, *lasts)
    both_other = over_core(both_own)
    state, act, slope, wc, bias_rows = call(
        partial(readout, mp), 1,
        [(idx, None), (xhat, None), (src, None), (par, None), (ends, None), (gain, vector), (bias, vector), (skp, vector),
         (both_own, None), (both_other, None)] + [(v, None) for v in lasts + [last]],
        [(big, BF16, None), (big, BF16, None), (big, F32, None), ((width, width), BF16, None), small],
        scratch((CHUNKS, width, F32), (BLOCK, width, BF16), (BLOCK, width, BF16), (BLOCK, width, F32), (BLOCK, width, F32)), 8, product, 8,
    )
    branch, gpre, wg, vec_glu = call(
        partial(gating, mp), 1,
        [(idx, None), (cotlow, None), (act, None), (bias_rows, None), (both_own, None), (both_other, None)],
        [(big, BF16, None), ((tokens, 2 * width), BF16, None), ((2 * width, width), BF16, None), small],
        scratch((BLOCK, 2 * width, F32), (BLOCK, 2 * width, F32)),
        10, 2 * product, 8,
    )
    gmix, gs, adj, first, vec_skip = call(
        unmix, 1,
        [(idx, None), (gpre, None), (slope, None), (norm, None), (wg, None), (wc, None), (par, None)],
        [(big, BF16, None), (big, F32, None), ((CHUNKS, width), F32, None), small, small],
        scratch((BLOCK, width, F32), (BLOCK, width, F32), (BLOCK, width, BF16),
                (BLOCK, width, BF16), (BLOCK, width, F32), (BLOCK, width, F32)),
        10, 4 * product, 8,
    )
    with jax.named_scope("carry_back"):
        firsts = [over_mp(first, s) for s in range(1, mp)]
    early_rows = mp * (hid + ns)
    sums = [((early_rows, width), F32, None), ((early_rows, width), BF16, None)]
    keep, send = call(
        weight_products, 1,
        [(idx, None), (tied(gpre, first), None), (act, None), (state, None), (gmix, None)],
        sums, [], 12, 0, 0,
    )
    firsts[0] = tied(firsts[0], send)
    with jax.named_scope("sum_early_core"):
        got = over_core(tied(send, *firsts))
    gdrive, in_keep, in_send, vec_lam = call(
        partial(adjoint_scan, mp), 1,
        [(idx, None), (gs, None), (state, None), (src, None), (norm, None), (par, None),
         (adj, None)] + [(v, None) for v in firsts],
        [(big, BF16, None), ((states, width), F32, None), ((states, width), BF16, None), small],
        scratch((width, width, F32), (CHUNKS, width, F32), (BLOCK, width, BF16),
                (BLOCK, width, BF16)), 8, product, 8,
    )
    with jax.named_scope("sum_in_core"):
        in_got = over_core(in_send)
    got = tied(got, gdrive)
    height = mp * (hid + 2 * ns) // plane
    if ns // plane % 16 == 0 and hid // plane % 16 == 0:
        own_piece, *sends = call(
            partial(split_pieces, mp, plane, hid, ns), 1,
            [(idx, None), (keep, None), (got, None), (in_keep, None), (in_got, None)],
            [((height, width), F32, None)] + [((height, width), BF16, None)] * (plane - 1), [], 4, 0, 0,
        )
    else:
        both = keep + got.astype(F32)
        both = [both[: mp * hid], both[mp * hid :], in_keep + in_got.astype(F32)]
        both = jnp.concatenate([v.reshape(mp, plane, -1, width) for v in both], 2).swapaxes(0, 1)
        sends = [lax.dynamic_index_in_dim(both, place ^ s, 0, keepdims=False) for s in range(plane)]
        sends = [v.reshape(-1, width) for v in sends]
        own_piece, sends = sends[0], [v.astype(BF16) for v in sends[1:]]
    with jax.named_scope("sum_plane"):
        pieces = [over_plane(v, s + 1) for s, v in enumerate(sends)]
    gx, y, vec, vec_rows = call(
        norm_back, steps,
        [(idx, None), (cot, None), (tied(gdrive, own_piece), None), (wt, None), (gmix, None), (xhat, None), (rstd, None),
         (gain, vector), (skp, vector), (x, chunked), (branch, None), (vec_skip, None), (vec_glu, None),
         (vec_lam, None)],
        [((CHUNKS, chunk, width), F32, chunked), ((CHUNKS, chunk, width), F32, chunked), small, ((16, width), BF16, None)],
        scratch((BLOCK, width, F32), (BLOCK, width, F32), (STEP_ROWS, width, F32), (8, width, F32)), 18, product, 8,
    )
    pieces[0], own_piece, nu_log, theta_log, me, core, place = lax.optimization_barrier(
        (pieces[0], own_piece, nu_log, theta_log, me, core, place, vec)
    )[:7]
    rows = tree_sum([own_piece] + [p.astype(F32) for p in pieces]).reshape(mp, -1, width)
    with jax.named_scope("sum_mp"):
        got, vecs = [lax.dynamic_index_in_dim(rows, me, 0, keepdims=False)], [vec]
        n = got[0].shape[0]
        for s in range(1, mp):
            send = lax.dynamic_index_in_dim(rows, me ^ s, 0, keepdims=False).astype(BF16)
            buffer = over_mp(jnp.concatenate([send, vec_rows]), s)
            got.append(buffer[:n].astype(F32))
            vecs.append(vector_sum(buffer[n:]))
    piece, vec = tree_sum(got).astype(BF16), tree_sum(vecs)
    with jax.named_scope("spread_plane"):
        vec, vec_rows = vector_rows(vec)
        piece = jnp.concatenate([piece, vec_rows])
        stack = [piece] + [over_plane(piece, s) for s in range(1, plane)]
    vec = tree_sum([vec] + [vector_sum(v[n:]) for v in stack[1:]])
    vec, vec_rows = vector_rows(vec)
    own = jnp.concatenate([v[:n] for v in stack] + [vec_rows])
    with jax.named_scope("spread_core"):
        got = over_core(own)
    line = pl.BlockSpec((1, width), lambda i, idx: (0, 0))
    share = pl.BlockSpec((1, ns), lambda i, idx: (0, 0))
    shared = [((1, width), F32, line)] * 3 + [((1, ns), F32, share)] * 3
    shared.append(((2, hid), F32, pl.BlockSpec((2, hid), lambda i, idx: (0, 0))))
    logs = [(nu_log[None], None), (theta_log[None], None)]
    if ns // plane % 16 == 0 and hid // plane % 16 == 0:
        whole = pl.BlockSpec((2, ns, width), lambda i, idx: (0, 0, 0))
        grad_in, grad_out_weight, grad_glu, *vectors = call(
            partial(finish, hid, ns, plane), 1,
            [(idx, None), (own, None), (got, None)] + logs,
            [((2, ns, width), F32, whole), ((2, ns, width), F32, whole), ((2, hid, width), F32, None)] + shared,
            [], 8, 0, 0,
        )
    else:
        vec = vec + vector_sum(got[plane * n :])
        vectors = call(partial(small_outputs, hid, ns), 1, [(idx, None), (vec, None)] + logs, shared, [], 2, 0, 0)
        pieces = [flip(v[: plane * n].reshape(plane, n, width), place) for v in (own, got)]
        total = flip(jnp.stack(pieces), core).astype(F32)
        nh, nr = hid // plane, ns // plane

        def part(start, size):
            return total[:, :, start : start + size].reshape(2, -1, width)

        grad_glu, grad_out, grad_in = part(0, nh), part(nh, nr), part(nh + nr, nr)
        grad_out_weight = jnp.stack([grad_out[0], -grad_out[1]])
    grad_ln_gain, grad_ln_bias, grad_skip, grad_nu, grad_theta, grad_gamma, grad_glu_bias = vectors
    return (
        y.reshape(block_input.shape),
        gx.reshape(block_input.shape),
        grad_ln_gain[0],
        grad_ln_bias[0],
        grad_nu[0],
        grad_theta[0],
        grad_gamma[0],
        grad_in.transpose(2, 0, 1),
        grad_out_weight,
        grad_skip[0],
        grad_glu.transpose(2, 0, 1),
        grad_glu_bias,
    )


def solution(mesh):
    in_specs = (
        P("dp", "mp", None), P(), P(), P("mp"), P("mp"), P("mp"), P(None, None, "mp"), P(None, "mp", None), P(),
        P(None, None, "mp"), P(None, "mp"), P("dp", "mp", None),
    )
    out_specs = (
        P("dp", "mp", None), P("dp", "mp", None), P(), P(), P("mp"), P("mp"), P("mp"), P(None, None, "mp"),
        P(None, "mp", None), P(), P(None, None, "mp"), P(None, "mp"),
    )
    return jax.shard_map(on_device, mesh=mesh, in_specs=in_specs, out_specs=out_specs, check_vma=False)
```

```python
from functools import partial

import jax
import jax.numpy as jnp
from jax import lax
from jax.experimental import pallas as pl
from jax.experimental.pallas import tpu as pltpu
from jax.sharding import PartitionSpec as P

EPS = 1e-05
F32 = jnp.float32
BF16 = jnp.bfloat16
CHUNKS = 16
STEP_ROWS = 512
BLOCK = 256
PARAM_ROWS = 16
MIB = 1024 * 1024
INV_SQRT2 = 0.7071067811865476
INV_SQRT_2PI = 0.3989422804014327


def nt(a, b):
    return lax.dot_general(a, b, (((1,), (1,)), ((), ())), preferred_element_type=F32)


def nn(a, b):
    return lax.dot_general(a, b, (((1,), (0,)), ((), ())), preferred_element_type=F32)


def tn(a, b):
    return lax.dot_general(a, b, (((0,), (0,)), ((), ())), preferred_element_type=F32)


def cmul(ar, ai, br, bi):
    return ar * br - ai * bi, ar * bi + ai * br


def cpower(re, im, log2):
    for _ in range(log2):
        re, im = cmul(re, im, re, im)
    return re, im


def log2_of(n):
    return n.bit_length() - 1


def block_rows(step, block):
    if isinstance(step, int):
        return slice(block * BLOCK, (block + 1) * BLOCK)
    return pl.ds(pl.multiple_of(step * STEP_ROWS + block * BLOCK, BLOCK), BLOCK)


def tile_rows(step, start):
    if isinstance(step, int):
        return slice(step * STEP_ROWS + start, step * STEP_ROWS + start + 16)
    return pl.ds(pl.multiple_of(step * STEP_ROWS + start, 16), 16)


def alternate(first, second):
    i = j = 0
    while i < len(first) or j < len(second):
        if j >= len(second) or (i < len(first) and i * len(second) <= j * len(first)):
            first[i]()
            i += 1
        else:
            second[j]()
            j += 1


def run(pieces):
    for piece in pieces:
        piece()


def product_nt(out, left, right, size=256):
    def piece(n):
        out[:, n : n + size] = nt(left(), right[n : n + size, :])

    return [partial(piece, n) for n in range(0, right.shape[0], size)]


def product_nn(out, left, right, size=256):
    def piece(n):
        out[:, n : n + size] = nn(left(), right[:, n : n + size])

    return [partial(piece, n) for n in range(0, right.shape[1], size)]


def product_tn(total, left, right, size=256):
    def piece(n):
        total[n : n + size, :] += tn(left(slice(n, n + size)), right())

    return [partial(piece, n) for n in range(0, total.shape[0], size)]


def assemble(dst, own, other, first, rows, me, core, slots, negate_second):
    for slot in range(slots):
        for part in range(2):
            mine = own[me ^ slot, first : first + rows, :]
            theirs = other[me ^ slot, first : first + rows, :]
            value = jnp.where(core == part, mine, theirs)
            start = (part * slots + slot) * rows
            dst[start : start + rows, :] = -value if negate_second and part == 1 else value


def prepare(idx, x_ref, gain_ref, bias_ref, xhat_ref, norm_ref, rstd_ref):
    step = pl.program_id(0)
    width = x_ref.shape[2]
    per = x_ref.shape[1]
    gain, bias = gain_ref[...], bias_ref[...]
    for k in range(0, per, 8):
        rows = jnp.swapaxes(x_ref[:, k : k + 8, :], 0, 1).reshape(8 * CHUNKS, width)
        for r in range(0, 8 * CHUNKS, 16):
            place = tile_rows(step, k * CHUNKS + r)
            part = rows[r : r + 16]
            mean = jnp.mean(part, -1, keepdims=True)
            cen = part - mean
            var = jnp.mean(cen * cen, -1, keepdims=True)
            rstd = lax.rsqrt(var + EPS)
            xhat = cen * rstd
            xhat_ref[place, :] = xhat
            rstd_ref[place, :] = jnp.broadcast_to(rstd, (16, 128))
            norm_ref[place, :] = (xhat * gain + bias).astype(BF16)


def lower(idx, cot_ref, cotlow_ref):
    step = pl.program_id(0)
    width = cot_ref.shape[2]
    for k in range(0, cot_ref.shape[1], 8):
        rows = jnp.swapaxes(cot_ref[:, k : k + 8, :], 0, 1).reshape(8 * CHUNKS, width)
        place = pl.ds(pl.multiple_of(step * STEP_ROWS + k * CHUNKS, 128), 8 * CHUNKS)
        cotlow_ref[place, :] = rows.astype(BF16)


def first_scan(
    chunk, mp, idx, norm_ref, own_ref, other_ref, glu_bias_ref,
    src_ref, wt_ref, par_ref, ends_ref, last_ref, h_ref, drive_a, drive_b,
):
    step = 0
    width = norm_ref.shape[1]
    states = width // 2
    ns = states // mp

    me, core = idx[0], idx[1]
    assemble(wt_ref, own_ref, other_ref, 0, ns, me, core, mp, False)
    total = own_ref[0, ns : ns + PARAM_ROWS, :].astype(F32)
    for s in range(1, mp):
        total = total + own_ref[s, ns : ns + PARAM_ROWS, :].astype(F32)
    decay = total[0:1] + total[2:3] + total[4:5]
    gamma = jnp.exp(total[1:2] + total[3:4] + total[5:6])
    radius = jnp.exp(-jnp.exp(decay[:, :states]))
    turn = jnp.exp(decay[:, states:])
    re, im = radius * jnp.cos(turn), radius * jnp.sin(turn)
    lre, lim = cpower(re, im, log2_of(chunk))
    tre, tim = cpower(lre, lim, log2_of(CHUNKS))
    par_ref[0:1, :] = jnp.concatenate([re, im], 1)
    par_ref[1:2, :] = gamma
    par_ref[2:3, :] = jnp.concatenate([lre, lim], 1)
    par_ref[3:8, :] = jnp.zeros((5, width), F32)
    pre, pim = jnp.ones_like(tre), jnp.zeros_like(tim)
    for s in range(mp):
        par_ref[8 + s : 9 + s, :] = jnp.concatenate([pre, pim], 1)
        pre, pim = cmul(pre, pim, tre, tim)

    gam = par_ref[1:2, :]
    lre, lim = par_ref[0:1, :states], par_ref[0:1, states:]
    h = [jnp.zeros((CHUNKS, states), F32)] * 2

    def drive_pieces(b, drive):
        return product_nt(drive, lambda: norm_ref[block_rows(step, b), :], wt_ref)

    def scan_piece(b, drive, r):
        hre, him = h
        src = drive[r : r + CHUNKS, :] * gam
        src_ref[tile_rows(step, b * BLOCK + r), :] = src
        h[0] = src[:, :states] + lre * hre - lim * him
        h[1] = src[:, states:] + lre * him + lim * hre

    def scan_pieces(b, drive):
        return [partial(scan_piece, b, drive, r) for r in range(0, BLOCK, CHUNKS)]

    blocks = norm_ref.shape[0] // BLOCK
    drives = (drive_a, drive_b)
    run(drive_pieces(0, drive_a))
    for b in range(blocks):
        more = drive_pieces(b + 1, drives[(b + 1) % 2]) if b + 1 < blocks else []
        alternate(more, scan_pieces(b, drives[b % 2]))
    h_ref[:, :states], h_ref[:, states:] = h
    ends_ref[...] = h_ref[...]
    pre, pim = par_ref[2:3, :states], par_ref[2:3, states:]
    re, im = h_ref[0:1, :states], h_ref[0:1, states:]
    for c in range(1, CHUNKS):
        mre, mim = cmul(pre, pim, re, im)
        re, im = mre + h_ref[c : c + 1, :states], mim + h_ref[c : c + 1, states:]
    last_ref[...] = jnp.zeros_like(last_ref)
    last_ref[0:1, :] = jnp.concatenate([re, im], 1)
    hid = glu_bias_ref.shape[1]
    biases = glu_bias_ref[...].astype(F32)
    for j in range(mp):
        last_ref[1:3, j * hid : (j + 1) * hid] = jnp.where(me == j, biases, 0.0)


def gelu_parts(v):
    cdf = 0.5 * (1.0 + lax.erf(v * INV_SQRT2))
    pdf = jnp.exp(-0.5 * v * v) * INV_SQRT_2PI
    return v * cdf, cdf + v * pdf


def readout(mp, idx, xhat_ref, src_ref, par_ref, ends_ref, gain_ref, bias_ref, skip_ref, own_ref, other_ref, *rest):
    others, mine = rest[: mp - 1], rest[mp - 1]
    (state_ref, act_ref, slope_ref, wc_ref, rows_ref, h_ref, low_a, low_b, mix_a, mix_b) = rest[mp:]
    step = 0
    width = xhat_ref.shape[1]
    states = width // 2
    me, core = idx[0], idx[1]

    assemble(wc_ref, own_ref, other_ref, 0, states // mp, me, core, mp, True)
    total = mine[...]
    for other in others:
        total = total + other[...]
    rows_ref[...] = total
    re = jnp.zeros((1, states), F32)
    im = jnp.zeros((1, states), F32)
    for s in range(1, mp):
        j = me ^ s
        power = jnp.maximum(me - 1 - j, 0)
        row = par_ref[pl.ds(8 + power, 1), :]
        sre, sim = cmul(row[:, :states], row[:, states:], others[s - 1][0:1, :states], others[s - 1][0:1, states:])
        keep = (j < me).astype(F32)
        re, im = re + keep * sre, im + keep * sim
    lre, lim = par_ref[2:3, :states], par_ref[2:3, states:]
    for c in range(CHUNKS):
        h_ref[c : c + 1, :states] = re
        h_ref[c : c + 1, states:] = im
        mre, mim = cmul(lre, lim, re, im)
        re, im = mre + ends_ref[c : c + 1, :states], mim + ends_ref[c : c + 1, states:]

    lre, lim = par_ref[0:1, :states], par_ref[0:1, states:]
    h = [h_ref[:, :states], h_ref[:, states:]]

    def scan_piece(b, low, r):
        hre, him = h
        rows = tile_rows(step, b * BLOCK + r)
        hre, him = (
            src_ref[rows, :states] + lre * hre - lim * him,
            src_ref[rows, states:] + lre * him + lim * hre,
        )
        low[r : r + CHUNKS, :states] = hre.astype(BF16)
        low[r : r + CHUNKS, states:] = him.astype(BF16)
        state_ref[rows, :] = low[r : r + CHUNKS, :]
        h[0], h[1] = hre, him

    def gelu_piece(b, mix, r):
        rows = tile_rows(step, b * BLOCK + r)
        for c in range(0, width, 128):
            cols = slice(c, c + 128)
            normed = xhat_ref[rows, cols] * gain_ref[:, cols] + bias_ref[:, cols]
            lru = mix[r : r + 16, cols] + skip_ref[:, cols] * normed
            act, slope = gelu_parts(lru)
            act_ref[rows, cols] = act.astype(BF16)
            slope_ref[rows, cols] = slope

    def scans(b, low):
        return [partial(scan_piece, b, low, r) for r in range(0, BLOCK, CHUNKS)]

    def mixes(low, mix):
        return product_nn(mix, lambda: low[...], wc_ref)

    def gelus(b, mix):
        return [partial(gelu_piece, b, mix, r) for r in range(0, BLOCK, 16)]

    blocks = src_ref.shape[0] // BLOCK
    lows, mix_refs = (low_a, low_b), (mix_a, mix_b)
    run(scans(0, low_a))
    for b in range(blocks):
        other = scans(b + 1, lows[(b + 1) % 2]) if b + 1 < blocks else []
        other = (gelus(b - 1, mix_refs[(b - 1) % 2]) if b else []) + other
        alternate(mixes(lows[b % 2], mix_refs[b % 2]), other)
    run(gelus(blocks - 1, mix_refs[(blocks - 1) % 2]))


def gating(mp, idx, cotlow_ref, act_ref, rows_ref, own_ref, other_ref,
           br_ref, gpre_ref, wg_ref, vec_ref, pre_a, pre_b):
    width = act_ref.shape[1]
    core = idx[1]
    assemble(wg_ref, own_ref, other_ref, width // 2 // mp, width // mp, idx[0], core, mp, False)
    vec_ref[...] = jnp.zeros_like(vec_ref)
    blocks = act_ref.shape[0] // BLOCK
    buffers = (pre_a, pre_b)

    def pre_pieces(b):
        return product_nt(buffers[b % 2], lambda: act_ref[b * BLOCK : (b + 1) * BLOCK, :], wg_ref) if b < blocks else []

    sums = {}

    def gate_piece(b, start, c):
        pre = buffers[b % 2]
        cols = slice(c, c + 128)
        gate_cols = slice(width + c, width + c + 128)
        for r in range(start, start + 64, 16):
            rows = slice(b * BLOCK + r, b * BLOCK + r + 16)
            value = pre[r : r + 16, cols] + rows_ref[1:2, cols]
            gate = pre[r : r + 16, gate_cols] + rows_ref[2:3, cols]
            sig = 0.5 * jnp.tanh(0.5 * gate) + 0.5
            branch = value * sig
            br_ref[rows, cols] = branch.astype(BF16)
            g = cotlow_ref[rows, cols].astype(F32)
            g_value = g * sig
            g_gate = g * branch * (1.0 - sig)
            gpre_ref[rows, cols] = g_value.astype(BF16)
            gpre_ref[rows, gate_cols] = g_gate.astype(BF16)
            for key, part in ((("value", c), g_value), (("gate", c), g_gate)):
                sums[key] = sums[key] + part if key in sums else part

    def gate_pieces(b):
        return [partial(gate_piece, b, start, c) for start in range(0, BLOCK, 64) for c in range(0, width, 128)]

    run(pre_pieces(0))
    for b in range(blocks):
        alternate(pre_pieces(b + 1), gate_pieces(b))
        for c in range(0, width, 128):
            vec_ref[1:2, c : c + 128] += jnp.sum(sums.pop(("value", c)), 0, keepdims=True)
            vec_ref[2:3, c : c + 128] += jnp.sum(sums.pop(("gate", c)), 0, keepdims=True)


def weight_products(idx, gpre_ref, act_ref, state_ref, gmix_ref, keep_ref, send_ref):
    core = idx[1]

    def product(left_ref, right_ref, first):
        columns = left_ref.shape[1]
        size = columns // 2
        for n in range(0, columns, 256):
            total = tn(left_ref[:, n : n + 256], right_ref[...])
            here = slice(first + n % size, first + n % size + 256)

            @pl.when(core == n // size)
            def _():
                keep_ref[here, :] = total

            @pl.when(core != n // size)
            def _():
                send_ref[here, :] = total.astype(BF16)

    product(gpre_ref, act_ref, 0)
    product(state_ref, gmix_ref, gpre_ref.shape[1] // 2)


def unmix(idx, gpre_ref, slope_ref, norm_ref, wg_ref, wc_ref, par_ref,
          gmix_ref, gs_ref, adj_ref, first_ref, vec_ref, ga_a, ga_b, gmix_a, gmix_b, gs_a, gs_b):
    step = 0
    width = norm_ref.shape[1]
    states = width // 2
    core = idx[1]

    vec_ref[...] = jnp.zeros_like(vec_ref)
    sums = {}

    def act_pieces(b, ga):
        return product_nn(ga, lambda: gpre_ref[block_rows(step, b), :], wg_ref)

    def lru_piece(b, ga, gmix, r):
        rows = tile_rows(step, b * BLOCK + r)
        for c in range(0, width, 128):
            cols = slice(c, c + 128)
            g_lru = ga[r : r + 16, cols] * slope_ref[rows, cols]
            low = g_lru.astype(BF16)
            gmix[r : r + 16, cols] = low
            gmix_ref[rows, cols] = low
            part = g_lru * norm_ref[rows, cols].astype(F32)
            sums[c] = sums[c] + part if c in sums else part

    def lru_pieces(b, ga, gmix):
        return [partial(lru_piece, b, ga, gmix, r) for r in range(0, BLOCK, 16)]

    def mix_pieces(b, gs, gmix):
        return product_nt(gs, lambda: gmix[...], wc_ref)

    lre, lim = par_ref[0:1, :states], par_ref[0:1, states:]
    power = [jnp.ones((8, states), F32), jnp.zeros((8, states), F32)]
    are = [jnp.zeros((8, states), F32) for _ in range(0, CHUNKS, 8)]
    aim = [jnp.zeros((8, states), F32) for _ in range(0, CHUNKS, 8)]

    def end_piece(b, gs, r):
        pre, pim = power
        for n, c in enumerate(range(0, CHUNKS, 8)):
            gre, gim = gs[r + c : r + c + 8, :states], gs[r + c : r + c + 8, states:]
            mre, mim = cmul(pre, pim, gre, gim)
            are[n], aim[n] = are[n] + mre, aim[n] + mim
        gs_ref[tile_rows(step, b * BLOCK + r), :] = gs[r : r + CHUNKS, :]
        power[0], power[1] = pre * lre + pim * lim, pim * lre - pre * lim

    def end_pieces(b, gs):
        return [partial(end_piece, b, gs, r) for r in range(0, BLOCK, CHUNKS)]

    blocks = gpre_ref.shape[0] // BLOCK
    gas, gmixes, gss = (ga_a, ga_b), (gmix_a, gmix_b), (gs_a, gs_b)
    run(act_pieces(0, ga_a))
    for b in range(blocks + 2):
        products = act_pieces(b + 1, gas[(b + 1) % 2]) if b + 1 < blocks else []
        products += mix_pieces(b - 1, gss[(b - 1) % 2], gmixes[(b - 1) % 2]) if 0 <= b - 1 < blocks else []
        other = lru_pieces(b, gas[b % 2], gmixes[b % 2]) if b < blocks else []
        other += end_pieces(b - 2, gss[b % 2]) if b >= 2 else []
        alternate(products, other)
    for c in range(0, width, 128):
        vec_ref[0:1, c : c + 128] += jnp.sum(sums[c], 0, keepdims=True)
    for n, c in enumerate(range(0, CHUNKS, 8)):
        adj_ref[c : c + 8, :states] = are[n]
        adj_ref[c : c + 8, states:] = aim[n]
    lre, lim = par_ref[2:3, :states], -par_ref[2:3, states:]
    last = CHUNKS - 1
    re, im = adj_ref[last : last + 1, :states], adj_ref[last : last + 1, states:]
    for c in range(CHUNKS - 2, -1, -1):
        mre, mim = cmul(lre, lim, re, im)
        re, im = mre + adj_ref[c : c + 1, :states], mim + adj_ref[c : c + 1, states:]
    first_ref[...] = jnp.broadcast_to(jnp.concatenate([re, im], 1), first_ref.shape)


def adjoint_scan(mp, idx, gs_ref, state_ref, src_ref, norm_ref, par_ref, adj_ref, *rest):
    others = rest[: mp - 1]
    (gdrive_ref, keep_ref, send_ref, vec_ref, acc_ref, h_ref, gdrive_a, gdrive_b) = rest[mp - 1 :]
    step = 0
    width = gs_ref.shape[1]
    states = width // 2
    me, core = idx[0], idx[1]

    re = jnp.zeros((1, states), F32)
    im = jnp.zeros((1, states), F32)
    for s in range(1, mp):
        j = me ^ s
        power = jnp.maximum(j - me - 1, 0)
        row = par_ref[pl.ds(8 + power, 1), :]
        sre, sim = cmul(row[:, :states], -row[:, states:], others[s - 1][0:1, :states], others[s - 1][0:1, states:])
        keep = (j > me).astype(F32)
        re, im = re + keep * sre, im + keep * sim
    lre, lim = par_ref[2:3, :states], -par_ref[2:3, states:]
    for c in range(CHUNKS - 1, -1, -1):
        h_ref[c : c + 1, :states] = re
        h_ref[c : c + 1, states:] = im
        mre, mim = cmul(lre, lim, re, im)
        re, im = mre + adj_ref[c : c + 1, :states], mim + adj_ref[c : c + 1, states:]
    acc_ref[...] = jnp.zeros_like(acc_ref)

    lre, lim = par_ref[0:1, :states], par_ref[0:1, states:]
    gam = par_ref[1:2, :states]
    h = [h_ref[:, :states], h_ref[:, states:]]
    sums = [jnp.zeros((CHUNKS, states), F32)] * 3

    def scan_piece(b, gdrive, r):
        hre, him = h
        rows = tile_rows(step, b * BLOCK + r)
        tre, tim = state_ref[rows, :states].astype(F32), state_ref[rows, states:].astype(F32)
        sums[0] = sums[0] + (hre * tre + him * tim)
        sums[1] = sums[1] + (him * tre - hre * tim)
        hre, him = (
            gs_ref[rows, :states] + lre * hre + lim * him,
            gs_ref[rows, states:] + lre * him - lim * hre,
        )
        sums[2] = sums[2] + (hre * src_ref[rows, :states] + him * src_ref[rows, states:])
        gdrive[r : r + CHUNKS, :states] = (hre * gam).astype(BF16)
        gdrive[r : r + CHUNKS, states:] = (him * gam).astype(BF16)
        gdrive_ref[rows, :] = gdrive[r : r + CHUNKS, :]
        h[0], h[1] = hre, him

    def scans(b, gdrive):
        return [partial(scan_piece, b, gdrive, r) for r in range(BLOCK - CHUNKS, -1, -CHUNKS)]

    def weight_pieces(b, gdrive):
        return product_tn(acc_ref, lambda cols: gdrive[:, cols], lambda: norm_ref[block_rows(step, b), :])

    last = gs_ref.shape[0] // BLOCK - 1
    buffers = (gdrive_a, gdrive_b)
    run(scans(last, buffers[last % 2]))
    for b in range(last - 1, -1, -1):
        alternate(weight_pieces(b + 1, buffers[(b + 1) % 2]), scans(b, buffers[b % 2]))
    run(weight_pieces(0, buffers[0]))
    keep_ref[...] = acc_ref[pl.ds(core * states, states), :]
    send_ref[...] = acc_ref[pl.ds((1 - core) * states, states), :].astype(BF16)
    sre, sim, sgam = [jnp.sum(v, 0, keepdims=True) for v in sums]
    vec_ref[0:1, :] = jnp.concatenate([sre, sim], 1)
    vec_ref[1:2, :] = jnp.concatenate([sgam, jnp.zeros((1, states), F32)], 1)
    vec_ref[2:8, :] = jnp.zeros((6, width), F32)


def norm_back(idx, cot_ref, gdrive_ref, wt_ref, gmix_ref, xhat_ref, rstd_ref, gain_ref, skip_ref, x_ref, br_ref,
              vec_skip_ref, vec_glu_ref, vec_lam_ref, gx_ref, y_ref, parts_ref, send_ref, gn_a, gn_b, dx_ref, vec_ref):
    step = pl.program_id(0)
    width = cot_ref.shape[2]
    per = STEP_ROWS // CHUNKS

    @pl.when(step == 0)
    def _():
        vec_ref[...] = jnp.zeros_like(vec_ref)

    def normed_pieces(block, gn):
        rows = pl.ds(pl.multiple_of(block * BLOCK, BLOCK), BLOCK)
        return product_nn(gn, lambda: gdrive_ref[rows, :], wt_ref)

    @pl.when(step == 0)
    def _():
        run(normed_pieces(0, gn_a))

    sums = [jnp.zeros((16, width), F32), jnp.zeros((16, width), F32)]

    def norm_piece(b, gn, r):
        rows = tile_rows(step, b * BLOCK + r)
        xhat = xhat_ref[rows, :]
        g = gn[r : r + 16, :] + skip_ref[...] * gmix_ref[rows, :].astype(F32)
        sums[0] = sums[0] + g * xhat
        sums[1] = sums[1] + g
        gh = g * gain_ref[...]
        first = jnp.mean(gh, -1, keepdims=True)
        second = jnp.mean(gh * xhat, -1, keepdims=True)
        rstd = jnp.concatenate([rstd_ref[rows, :]] * (width // 128), 1)
        dx_ref[b * BLOCK + r : b * BLOCK + r + 16, :] = rstd * (gh - first - xhat * second)

    def norm_pieces(b, gn):
        return [partial(norm_piece, b, gn, r) for r in range(0, BLOCK, 16)]

    def output_piece(k):
        rows = dx_ref[k * CHUNKS : (k + 8) * CHUNKS, :].reshape(8, CHUNKS, width)
        place = pl.ds(pl.multiple_of(step * per + k, 8), 8)
        gx_ref[:, k : k + 8, :] = cot_ref[:, place, :] + jnp.swapaxes(rows, 0, 1)

    def branch_piece(k):
        here = pl.ds(pl.multiple_of(step * STEP_ROWS + k * CHUNKS, 128), 8 * CHUNKS)
        rows = br_ref[here, :].astype(F32).reshape(8, CHUNKS, width)
        y_ref[:, k : k + 8, :] = x_ref[:, k : k + 8, :] + jnp.swapaxes(rows, 0, 1)

    after = jnp.minimum(2 * step + 2, gdrive_ref.shape[0] // BLOCK - 1)
    outputs = [partial(output_piece, k) for k in range(0, per, 8)]
    run([partial(branch_piece, k) for k in range(0, per, 8)])
    alternate(normed_pieces(2 * step + 1, gn_b), norm_pieces(0, gn_a))
    alternate(normed_pieces(after, gn_a), outputs[: len(outputs) // 2] + norm_pieces(1, gn_b) + outputs[len(outputs) // 2 :])
    vec_ref[0:1, :] += jnp.sum(sums[0], 0, keepdims=True)
    vec_ref[1:2, :] += jnp.sum(sums[1], 0, keepdims=True)

    @pl.when(step == pl.num_programs(0) - 1)
    def _():
        rows = [vec_skip_ref[0:1, :], vec_glu_ref[1:3, :], vec_ref[0:2, :], vec_lam_ref[0:2, :], jnp.zeros((1, width), F32)]
        vec = jnp.concatenate(rows, 0)
        high = vec.astype(BF16)
        low = (vec - high.astype(F32)).astype(BF16)
        parts_ref[...] = high.astype(F32) + low.astype(F32)
        send_ref[...] = jnp.concatenate([high.astype(F32), low.astype(F32)], 0).astype(BF16)


def pack_rows(idx, *refs):
    *parts, out = refs
    for i, part in enumerate(parts):
        out[i] = part[...]


def split_pieces(slots, count, hid, ns, idx, keep_ref, got_ref, in_keep_ref, in_got_ref, own_ref, *sends):
    place = idx[2]
    parts = ((keep_ref, got_ref, 0, hid), (keep_ref, got_ref, slots * hid, ns), (in_keep_ref, in_got_ref, 0, ns))
    height = (hid + 2 * ns) // count
    for slot in range(slots):
        for s in range(count):
            low = slot * height
            for keep, got, base, size in parts:
                rows = size // count
                start = pl.multiple_of(base + slot * size + (place ^ s) * rows, rows)
                piece = keep[pl.ds(start, rows), :] + got[pl.ds(start, rows), :].astype(F32)
                if s == 0:
                    own_ref[low : low + rows, :] = piece
                else:
                    sends[s - 1][low : low + rows, :] = piece.astype(BF16)
                low += rows


def finish(hid, ns, count, idx, own_ref, got_ref, nu_ref, theta_ref, in_ref, out_ref, glu_ref, *rest):
    *rest, rows_ref = rest
    core, place = idx[1], idx[2]
    height = (hid + 2 * ns) // count
    for part in range(2):
        for i in range(count):
            here = pl.ds(pl.multiple_of((i ^ place) * height, 16), height)
            rows = jnp.where(core == part, own_ref[here, :], got_ref[here, :]).astype(F32)
            low = 0
            for ref, size in ((rows_ref, hid // count), (out_ref, ns // count), (in_ref, ns // count)):
                value = rows[low : low + size]
                ref[part, i * size : (i + 1) * size, :] = -value if ref is out_ref and part == 1 else value
                low += size
        glu_ref[:, part, :] = rows_ref[part].T
    first = count * height
    both = [ref[first : first + 16, :].astype(F32) for ref in (own_ref, got_ref)]
    vec = (both[0][:8] + both[0][8:]) + (both[1][:8] + both[1][8:])
    vector_outputs(hid, ns, idx, vec, nu_ref, theta_ref, *rest)


def vector_outputs(hid, ns, idx, vec, nu_ref, theta_ref, gain_ref, bias_ref, skip_ref, nu_out, theta_out, gamma_out, glu_ref):
    me = idx[0]
    width = vec.shape[1]
    states = width // 2
    skip_ref[...] = vec[0:1, :]
    gain_ref[...] = vec[3:4, :]
    bias_ref[...] = vec[4:5, :]

    def share(rows, start, size, count):
        total = jnp.zeros((rows.shape[0], size), F32)
        for j in range(count):
            total = total + jnp.where(me == j, rows[:, start + j * size : start + (j + 1) * size], 0.0)
        return total

    glu_ref[...] = share(vec[1:3, :], 0, hid, width // hid)
    re = share(vec[5:6, :], 0, ns, states // ns)
    im = share(vec[5:6, :], states, ns, states // ns)
    gamma_out[...] = share(vec[6:7, :], 0, ns, states // ns)
    speed, turn = jnp.exp(nu_ref[...]), jnp.exp(theta_ref[...])
    radius = jnp.exp(-speed)
    cos, sin = radius * jnp.cos(turn), radius * jnp.sin(turn)
    nu_out[...] = -speed * (cos * re + sin * im)
    theta_out[...] = turn * (cos * im - sin * re)


def small_outputs(hid, ns, idx, vec_ref, *rest):
    vector_outputs(hid, ns, idx, vec_ref[...], *rest)


def call(kernel, steps, ins, outs, scratch, mib, flops, moved, in_place=None, first=False):
    def in_hbm(array, block):
        return array if block is None or (array.size < 65536 and not first) else pltpu.with_memory_space_constraint(array, pltpu.HBM)

    def spec(block):
        return pl.BlockSpec(memory_space=pltpu.VMEM) if block is None else block

    return pl.pallas_call(
        kernel,
        grid_spec=pltpu.PrefetchScalarGridSpec(
            num_scalar_prefetch=1,
            grid=(steps,),
            in_specs=[spec(block) for _, block in ins[1:]],
            out_specs=[spec(block) for _, _, block in outs],
            scratch_shapes=[pltpu.VMEM(*s) for s in scratch],
        ),
        out_shape=[jax.ShapeDtypeStruct(s, t) if block is None else pltpu.HBM(s, t) for s, t, block in outs],
        input_output_aliases=in_place or {},
        compiler_params=pltpu.CompilerParams(vmem_limit_bytes=mib * MIB),
        cost_estimate=pl.CostEstimate(flops=flops, bytes_accessed=moved * MIB, transcendentals=0),
    )(*[in_hbm(a, block) for a, block in ins])


def xor_pairs(n, s):
    return [(i, i ^ s) for i in range(n)]


def from_each(value, axis, n):
    return [value] + [lax.ppermute(value, axis, xor_pairs(n, s)) for s in range(1, n)]


def tree_sum(parts):
    parts = list(parts)
    while len(parts) > 1:
        parts = [parts[i] + parts[i + 1] for i in range(0, len(parts), 2)]
    return parts[0]


def high_low(v):
    high = lax.reduce_precision(v, 8, 7)
    return high, lax.reduce_precision(v - high, 8, 7)


def vector_rows(v):
    high, low = high_low(v)
    return high + low, jnp.concatenate([high, low]).astype(BF16)


def vector_sum(rows):
    n = rows.shape[0] // 2
    return rows[:n].astype(F32) + rows[n:].astype(F32)


def flip(stack, position):
    n = stack.shape[0]
    for b in range(log2_of(n)):
        pairs = stack.reshape((n >> (b + 1), 2, 1 << b) + stack.shape[1:])
        pairs = jnp.where((position >> b) & 1 == 1, pairs[:, ::-1], pairs)
        stack = pairs.reshape(stack.shape)
    return stack


def on_device(
    block_input, ln_gain, ln_bias, nu_log, theta_log, gamma_log, in_weight, out_weight, skip, glu_weight, glu_bias,
    out_cotangent,
):
    mp = lax.axis_size("mp")
    dp = lax.axis_size("dp")
    plane = dp // 2
    me = lax.axis_index("mp")
    dpi = lax.axis_index("dp")
    core = dpi & 1
    place = dpi >> 1
    idx = jnp.stack([me, core, place]).astype(jnp.int32)
    tokens, width = block_input.shape[1:]
    ns = nu_log.shape[0]
    states = ns * mp
    hid = glu_weight.shape[2]
    chunk = tokens // CHUNKS
    per = STEP_ROWS // CHUNKS
    steps = tokens // STEP_ROWS
    x = block_input.reshape(CHUNKS, chunk, width)
    cot = out_cotangent.reshape(CHUNKS, chunk, width)
    gain, bias, skp = ln_gain[None], ln_bias[None], skip[None]

    def over_core(v):
        return lax.ppermute(v, "dp", xor_pairs(dp, 1))

    def over_plane(v, s):
        return lax.ppermute(v, "dp", xor_pairs(dp, 2 * s))

    def over_mp(v, s):
        return lax.ppermute(v, "mp", xor_pairs(mp, s))

    here = (jnp.arange(mp) == me).astype(F32)[:, None]

    def placed(v):
        return (here * v[None]).reshape(-1)

    def thirds(v):
        high, rest = high_low(v)
        return [high, rest, lax.reduce_precision(v - high - rest, 8, 7)]

    first_rows = [placed(nu_log), placed(gamma_log)], [placed(theta_log), placed(gamma_log)]
    first_rows = jnp.concatenate([jnp.stack(v) for v in first_rows], 1)
    first_rows = lax.optimization_barrier(first_rows)
    params = jnp.concatenate(thirds(first_rows)).astype(BF16)
    params = jnp.pad(params, ((0, PARAM_ROWS - params.shape[0]), (0, 0)))

    def gathered(value, name):
        with jax.named_scope(name):
            return [value] + [over_mp(value, s) for s in range(1, mp)]

    def packed(parts, *earlier):
        value = parts[0]
        parts = lax.optimization_barrier(tuple(parts) + earlier)[: len(parts)]
        shape = (mp,) + value.shape
        return call(pack_rows, 1, [(idx, None)] + [(p, None) for p in parts], [(shape, value.dtype, None)], [], 1, 0, 0)[0]

    def tied(value, *earlier):
        return lax.optimization_barrier((value,) + earlier)[0]

    in_part = lax.dynamic_index_in_dim(in_weight, core, 1, keepdims=False).T
    out_part = lax.dynamic_index_in_dim(out_weight, core, 0, keepdims=False)
    glu_part = lax.dynamic_index_in_dim(glu_weight, core, 1, keepdims=False).T
    in_send = jnp.concatenate([in_part, params])
    both_part = jnp.concatenate([out_part, glu_part])
    x = tied(x, in_send, both_part)
    in_parts = gathered(in_send, "gather_in")

    chunked = pl.BlockSpec((CHUNKS, per, width), lambda i, idx: (0, i, 0))
    vector = pl.BlockSpec((1, width), lambda i, idx: (0, 0))
    rowed = pl.BlockSpec((STEP_ROWS, width), lambda i, idx: (i, 0))
    big = (tokens, width)
    npar = 8 + mp
    product = 2 * tokens * width * width
    small = ((8, width), F32, None)

    def scratch(*kinds):
        return [((rows, cols), kind) for rows, cols, kind in kinds]

    xhat, norm, rstd = call(
        prepare, steps,
        [(idx, None), (x, chunked), (gain, vector), (bias, vector)],
        [(big, F32, None), (big, BF16, None), ((tokens, 128), F32, None)],
        [], 6, product, 12, None, True,
    )
    in_parts = list(lax.optimization_barrier(tuple(in_parts) + (norm,))[:-1])
    both_own = gathered(tied(both_part, *in_parts[1:]), "gather_out_glu")
    in_own = packed(in_parts, norm)
    in_other = over_core(in_own)
    (cotlow,) = call(lower, steps, [(idx, None), (tied(cot, in_own), chunked)], [(big, BF16, None)], [], 5, 0, 8)
    norm = tied(norm, cotlow)
    src, wt, par, ends, last = call(
        partial(first_scan, chunk, mp), 1,
        [(idx, None), (norm, None), (in_own, None), (in_other, None), (glu_bias, None)],
        [(big, F32, None), ((width, width), BF16, None), ((npar, width), F32, None), ((CHUNKS, width), F32, None), small],
        scratch((CHUNKS, width, F32), (BLOCK, width, F32), (BLOCK, width, F32)), 5, product, 8,
    )
    with jax.named_scope("carry"):
        lasts = [over_mp(last, s) for s in range(1, mp)]
    both_own = packed(both_own, *lasts)
    both_other = over_core(both_own)
    state, act, slope, wc, bias_rows = call(
        partial(readout, mp), 1,
        [(idx, None), (xhat, None), (src, None), (par, None), (ends, None), (gain, vector), (bias, vector), (skp, vector),
         (both_own, None), (both_other, None)] + [(v, None) for v in lasts + [last]],
        [(big, BF16, None), (big, BF16, None), (big, F32, None), ((width, width), BF16, None), small],
        scratch((CHUNKS, width, F32), (BLOCK, width, BF16), (BLOCK, width, BF16), (BLOCK, width, F32), (BLOCK, width, F32)), 8, product, 8,
    )
    branch, gpre, wg, vec_glu = call(
        partial(gating, mp), 1,
        [(idx, None), (cotlow, None), (act, None), (bias_rows, None), (both_own, None), (both_other, None)],
        [(big, BF16, None), ((tokens, 2 * width), BF16, None), ((2 * width, width), BF16, None), small],
        scratch((BLOCK, 2 * width, F32), (BLOCK, 2 * width, F32)),
        10, 2 * product, 8,
    )
    gmix, gs, adj, first, vec_skip = call(
        unmix, 1,
        [(idx, None), (gpre, None), (slope, None), (norm, None), (wg, None), (wc, None), (par, None)],
        [(big, BF16, None), (big, F32, None), ((CHUNKS, width), F32, None), small, small],
        scratch((BLOCK, width, F32), (BLOCK, width, F32), (BLOCK, width, BF16),
                (BLOCK, width, BF16), (BLOCK, width, F32), (BLOCK, width, F32)),
        10, 4 * product, 8,
    )
    with jax.named_scope("carry_back"):
        firsts = [over_mp(first, s) for s in range(1, mp)]
    early_rows = mp * (hid + ns)
    sums = [((early_rows, width), F32, None), ((early_rows, width), BF16, None)]
    keep, send = call(
        weight_products, 1,
        [(idx, None), (tied(gpre, first), None), (act, None), (state, None), (gmix, None)],
        sums, [], 12, 0, 0,
    )
    firsts[0] = tied(firsts[0], send)
    with jax.named_scope("sum_early_core"):
        got = over_core(tied(send, *firsts))
    gdrive, in_keep, in_send, vec_lam = call(
        partial(adjoint_scan, mp), 1,
        [(idx, None), (gs, None), (state, None), (src, None), (norm, None), (par, None),
         (adj, None)] + [(v, None) for v in firsts],
        [(big, BF16, None), ((states, width), F32, None), ((states, width), BF16, None), small],
        scratch((width, width, F32), (CHUNKS, width, F32), (BLOCK, width, BF16),
                (BLOCK, width, BF16)), 8, product, 8,
    )
    with jax.named_scope("sum_in_core"):
        in_got = over_core(in_send)
    got = tied(got, gdrive)
    height = mp * (hid + 2 * ns) // plane
    if ns // plane % 16 == 0 and hid // plane % 16 == 0:
        own_piece, *sends = call(
            partial(split_pieces, mp, plane, hid, ns), 1,
            [(idx, None), (keep, None), (got, None), (in_keep, None), (in_got, None)],
            [((height, width), F32, None)] + [((height, width), BF16, None)] * (plane - 1), [], 4, 0, 0,
        )
    else:
        both = keep + got.astype(F32)
        both = [both[: mp * hid], both[mp * hid :], in_keep + in_got.astype(F32)]
        both = jnp.concatenate([v.reshape(mp, plane, -1, width) for v in both], 2).swapaxes(0, 1)
        sends = [lax.dynamic_index_in_dim(both, place ^ s, 0, keepdims=False) for s in range(plane)]
        sends = [v.reshape(-1, width) for v in sends]
        own_piece, sends = sends[0], [v.astype(BF16) for v in sends[1:]]
    with jax.named_scope("sum_plane"):
        pieces = [over_plane(v, s + 1) for s, v in enumerate(sends)]
    gx, y, vec, vec_rows = call(
        norm_back, steps,
        [(idx, None), (cot, None), (tied(gdrive, own_piece), None), (wt, None), (gmix, None), (xhat, None), (rstd, None),
         (gain, vector), (skp, vector), (x, chunked), (branch, None), (vec_skip, None), (vec_glu, None),
         (vec_lam, None)],
        [((CHUNKS, chunk, width), F32, chunked), ((CHUNKS, chunk, width), F32, chunked), small, ((16, width), BF16, None)],
        scratch((BLOCK, width, F32), (BLOCK, width, F32), (STEP_ROWS, width, F32), (8, width, F32)), 18, product, 8,
    )
    pieces[0], own_piece, nu_log, theta_log, me, core, place = lax.optimization_barrier(
        (pieces[0], own_piece, nu_log, theta_log, me, core, place, vec)
    )[:7]
    rows = tree_sum([own_piece] + [p.astype(F32) for p in pieces]).reshape(mp, -1, width)
    with jax.named_scope("sum_mp"):
        got, vecs = [lax.dynamic_index_in_dim(rows, me, 0, keepdims=False)], [vec]
        n = got[0].shape[0]
        for s in range(1, mp):
            send = lax.dynamic_index_in_dim(rows, me ^ s, 0, keepdims=False).astype(BF16)
            buffer = over_mp(jnp.concatenate([send, vec_rows]), s)
            got.append(buffer[:n].astype(F32))
            vecs.append(vector_sum(buffer[n:]))
    piece, vec = tree_sum(got).astype(BF16), tree_sum(vecs)
    with jax.named_scope("spread_plane"):
        vec, vec_rows = vector_rows(vec)
        piece = jnp.concatenate([piece, vec_rows])
        stack = [piece] + [over_plane(piece, s) for s in range(1, plane)]
    vec = tree_sum([vec] + [vector_sum(v[n:]) for v in stack[1:]])
    vec, vec_rows = vector_rows(vec)
    own = jnp.concatenate([v[:n] for v in stack] + [vec_rows])
    with jax.named_scope("spread_core"):
        got = over_core(own)
    line = pl.BlockSpec((1, width), lambda i, idx: (0, 0))
    share = pl.BlockSpec((1, ns), lambda i, idx: (0, 0))
    shared = [((1, width), F32, line)] * 3 + [((1, ns), F32, share)] * 3
    shared.append(((2, hid), F32, pl.BlockSpec((2, hid), lambda i, idx: (0, 0))))
    logs = [(nu_log[None], None), (theta_log[None], None)]
    if ns // plane % 16 == 0 and hid // plane % 16 == 0:
        whole = pl.BlockSpec((2, ns, width), lambda i, idx: (0, 0, 0))
        grad_in, grad_out_weight, grad_glu, *vectors = call(
            partial(finish, hid, ns, plane), 1,
            [(idx, None), (own, None), (got, None)] + logs,
            [((2, ns, width), F32, whole), ((2, ns, width), F32, whole), ((width, 2, hid), F32, pl.BlockSpec((width, 2, hid), lambda i, idx: (0, 0, 0)))] + shared,
            [((2, hid, width), F32)], 8, 0, 0,
        )
    else:
        vec = vec + vector_sum(got[plane * n :])
        vectors = call(partial(small_outputs, hid, ns), 1, [(idx, None), (vec, None)] + logs, shared, [], 2, 0, 0)
        pieces = [flip(v[: plane * n].reshape(plane, n, width), place) for v in (own, got)]
        total = flip(jnp.stack(pieces), core).astype(F32)
        nh, nr = hid // plane, ns // plane

        def part(start, size):
            return total[:, :, start : start + size].reshape(2, -1, width)

        grad_glu, grad_out, grad_in = part(0, nh).transpose(2, 0, 1), part(nh, nr), part(nh + nr, nr)
        grad_out_weight = jnp.stack([grad_out[0], -grad_out[1]])
    grad_ln_gain, grad_ln_bias, grad_skip, grad_nu, grad_theta, grad_gamma, grad_glu_bias = vectors
    return (
        y.reshape(block_input.shape),
        gx.reshape(block_input.shape),
        grad_ln_gain[0],
        grad_ln_bias[0],
        grad_nu[0],
        grad_theta[0],
        grad_gamma[0],
        grad_in.transpose(2, 0, 1),
        grad_out_weight,
        grad_skip[0],
        grad_glu,
        grad_glu_bias,
    )


def solution(mesh):
    in_specs = (
        P("dp", "mp", None), P(), P(), P("mp"), P("mp"), P("mp"), P(None, None, "mp"), P(None, "mp", None), P(),
        P(None, None, "mp"), P(None, "mp"), P("dp", "mp", None),
    )
    out_specs = (
        P("dp", "mp", None), P("dp", "mp", None), P(), P(), P("mp"), P("mp"), P("mp"), P(None, None, "mp"),
        P(None, "mp", None), P(), P(None, None, "mp"), P(None, "mp"),
    )
    return jax.shard_map(on_device, mesh=mesh, in_specs=in_specs, out_specs=out_specs, check_vma=False)
```

```python
from functools import partial

import jax
import jax.numpy as jnp
from jax import lax
from jax.experimental import pallas as pl
from jax.experimental.pallas import tpu as pltpu
from jax.sharding import PartitionSpec as P

EPS = 1e-05
F32 = jnp.float32
BF16 = jnp.bfloat16
CHUNKS = 16
STEP_ROWS = 512
BLOCK = 256
PARAM_ROWS = 16
MIB = 1024 * 1024
INV_SQRT2 = 0.7071067811865476
INV_SQRT_2PI = 0.3989422804014327


def nt(a, b):
    return lax.dot_general(a, b, (((1,), (1,)), ((), ())), preferred_element_type=F32)


def nn(a, b):
    return lax.dot_general(a, b, (((1,), (0,)), ((), ())), preferred_element_type=F32)


def tn(a, b):
    return lax.dot_general(a, b, (((0,), (0,)), ((), ())), preferred_element_type=F32)


def cmul(ar, ai, br, bi):
    return ar * br - ai * bi, ar * bi + ai * br


def cpower(re, im, log2):
    for _ in range(log2):
        re, im = cmul(re, im, re, im)
    return re, im


def log2_of(n):
    return n.bit_length() - 1


def block_rows(step, block):
    if isinstance(step, int):
        return slice(block * BLOCK, (block + 1) * BLOCK)
    return pl.ds(pl.multiple_of(step * STEP_ROWS + block * BLOCK, BLOCK), BLOCK)


def tile_rows(step, start):
    if isinstance(step, int):
        return slice(step * STEP_ROWS + start, step * STEP_ROWS + start + 16)
    return pl.ds(pl.multiple_of(step * STEP_ROWS + start, 16), 16)


def alternate(first, second):
    i = j = 0
    while i < len(first) or j < len(second):
        if j >= len(second) or (i < len(first) and i * len(second) <= j * len(first)):
            first[i]()
            i += 1
        else:
            second[j]()
            j += 1


def run(pieces):
    for piece in pieces:
        piece()


def product_nt(out, left, right, size=256):
    def piece(n):
        out[:, n : n + size] = nt(left(), right[n : n + size, :])

    return [partial(piece, n) for n in range(0, right.shape[0], size)]


def product_nn(out, left, right, size=256):
    def piece(n):
        out[:, n : n + size] = nn(left(), right[:, n : n + size])

    return [partial(piece, n) for n in range(0, right.shape[1], size)]


def product_tn(total, left, right, size=256):
    def piece(n):
        total[n : n + size, :] += tn(left(slice(n, n + size)), right())

    return [partial(piece, n) for n in range(0, total.shape[0], size)]


def assemble(dst, own, other, first, rows, me, core, slots, negate_second):
    for slot in range(slots):
        for part in range(2):
            mine = own[me ^ slot, first : first + rows, :]
            theirs = other[me ^ slot, first : first + rows, :]
            value = jnp.where(core == part, mine, theirs)
            start = (part * slots + slot) * rows
            dst[start : start + rows, :] = -value if negate_second and part == 1 else value


def prepare(idx, x_ref, gain_ref, bias_ref, xhat_ref, norm_ref, rstd_ref):
    step = pl.program_id(0)
    width = x_ref.shape[2]
    per = x_ref.shape[1]
    gain, bias = gain_ref[...], bias_ref[...]
    for k in range(0, per, 8):
        rows = jnp.swapaxes(x_ref[:, k : k + 8, :], 0, 1).reshape(8 * CHUNKS, width)
        for r in range(0, 8 * CHUNKS, 16):
            place = tile_rows(step, k * CHUNKS + r)
            part = rows[r : r + 16]
            mean = jnp.mean(part, -1, keepdims=True)
            cen = part - mean
            var = jnp.mean(cen * cen, -1, keepdims=True)
            rstd = lax.rsqrt(var + EPS)
            xhat = cen * rstd
            xhat_ref[place, :] = xhat
            rstd_ref[place, :] = jnp.broadcast_to(rstd, (16, 128))
            norm_ref[place, :] = (xhat * gain + bias).astype(BF16)


def lower(idx, cot_ref, cotlow_ref):
    step = pl.program_id(0)
    width = cot_ref.shape[2]
    for k in range(0, cot_ref.shape[1], 8):
        rows = jnp.swapaxes(cot_ref[:, k : k + 8, :], 0, 1).reshape(8 * CHUNKS, width)
        place = pl.ds(pl.multiple_of(step * STEP_ROWS + k * CHUNKS, 128), 8 * CHUNKS)
        cotlow_ref[place, :] = rows.astype(BF16)


def first_scan(
    chunk, mp, idx, norm_ref, own_ref, other_ref, glu_bias_ref,
    src_ref, wt_ref, par_ref, ends_ref, last_ref, h_ref, drive_a, drive_b,
):
    step = 0
    width = norm_ref.shape[1]
    states = width // 2
    ns = states // mp

    me, core = idx[0], idx[1]
    assemble(wt_ref, own_ref, other_ref, 0, ns, me, core, mp, False)
    total = own_ref[0, ns : ns + PARAM_ROWS, :].astype(F32)
    for s in range(1, mp):
        total = total + own_ref[s, ns : ns + PARAM_ROWS, :].astype(F32)
    decay = total[0:1] + total[2:3] + total[4:5]
    gamma = jnp.exp(total[1:2] + total[3:4] + total[5:6])
    radius = jnp.exp(-jnp.exp(decay[:, :states]))
    turn = jnp.exp(decay[:, states:])
    re, im = radius * jnp.cos(turn), radius * jnp.sin(turn)
    lre, lim = cpower(re, im, log2_of(chunk))
    tre, tim = cpower(lre, lim, log2_of(CHUNKS))
    par_ref[0:1, :] = jnp.concatenate([re, im], 1)
    par_ref[1:2, :] = gamma
    par_ref[2:3, :] = jnp.concatenate([lre, lim], 1)
    par_ref[3:8, :] = jnp.zeros((5, width), F32)
    pre, pim = jnp.ones_like(tre), jnp.zeros_like(tim)
    for s in range(mp):
        par_ref[8 + s : 9 + s, :] = jnp.concatenate([pre, pim], 1)
        pre, pim = cmul(pre, pim, tre, tim)

    gam = par_ref[1:2, :]
    lre, lim = par_ref[0:1, :states], par_ref[0:1, states:]
    h = [jnp.zeros((CHUNKS, states), F32)] * 2

    def drive_pieces(b, drive):
        return product_nt(drive, lambda: norm_ref[block_rows(step, b), :], wt_ref)

    def scan_piece(b, drive, r):
        hre, him = h
        src = drive[r : r + CHUNKS, :] * gam
        src_ref[tile_rows(step, b * BLOCK + r), :] = src
        h[0] = src[:, :states] + lre * hre - lim * him
        h[1] = src[:, states:] + lre * him + lim * hre

    def scan_pieces(b, drive):
        return [partial(scan_piece, b, drive, r) for r in range(0, BLOCK, CHUNKS)]

    blocks = norm_ref.shape[0] // BLOCK
    drives = (drive_a, drive_b)
    run(drive_pieces(0, drive_a))
    for b in range(blocks):
        more = drive_pieces(b + 1, drives[(b + 1) % 2]) if b + 1 < blocks else []
        alternate(more, scan_pieces(b, drives[b % 2]))
    h_ref[:, :states], h_ref[:, states:] = h
    ends_ref[...] = h_ref[...]
    pre, pim = par_ref[2:3, :states], par_ref[2:3, states:]
    re, im = h_ref[0:1, :states], h_ref[0:1, states:]
    for c in range(1, CHUNKS):
        mre, mim = cmul(pre, pim, re, im)
        re, im = mre + h_ref[c : c + 1, :states], mim + h_ref[c : c + 1, states:]
    last_ref[...] = jnp.zeros_like(last_ref)
    last_ref[0:1, :] = jnp.concatenate([re, im], 1)
    hid = glu_bias_ref.shape[1]
    biases = glu_bias_ref[...].astype(F32)
    for j in range(mp):
        last_ref[1:3, j * hid : (j + 1) * hid] = jnp.where(me == j, biases, 0.0)


def gelu_parts(v):
    cdf = 0.5 * (1.0 + lax.erf(v * INV_SQRT2))
    pdf = jnp.exp(-0.5 * v * v) * INV_SQRT_2PI
    return v * cdf, cdf + v * pdf


def readout(mp, idx, xhat_ref, src_ref, par_ref, ends_ref, gain_ref, bias_ref, skip_ref, own_ref, other_ref, *rest):
    others, mine = rest[: mp - 1], rest[mp - 1]
    (state_ref, act_ref, slope_ref, wc_ref, rows_ref, h_ref, low_a, low_b, mix_a, mix_b) = rest[mp:]
    step = 0
    width = xhat_ref.shape[1]
    states = width // 2
    me, core = idx[0], idx[1]

    assemble(wc_ref, own_ref, other_ref, 0, states // mp, me, core, mp, True)
    total = mine[...]
    for other in others:
        total = total + other[...]
    rows_ref[...] = total
    re = jnp.zeros((1, states), F32)
    im = jnp.zeros((1, states), F32)
    for s in range(1, mp):
        j = me ^ s
        power = jnp.maximum(me - 1 - j, 0)
        row = par_ref[pl.ds(8 + power, 1), :]
        sre, sim = cmul(row[:, :states], row[:, states:], others[s - 1][0:1, :states], others[s - 1][0:1, states:])
        keep = (j < me).astype(F32)
        re, im = re + keep * sre, im + keep * sim
    lre, lim = par_ref[2:3, :states], par_ref[2:3, states:]
    for c in range(CHUNKS):
        h_ref[c : c + 1, :states] = re
        h_ref[c : c + 1, states:] = im
        mre, mim = cmul(lre, lim, re, im)
        re, im = mre + ends_ref[c : c + 1, :states], mim + ends_ref[c : c + 1, states:]

    lre, lim = par_ref[0:1, :states], par_ref[0:1, states:]
    h = [h_ref[:, :states], h_ref[:, states:]]

    def scan_piece(b, low, r):
        hre, him = h
        rows = tile_rows(step, b * BLOCK + r)
        hre, him = (
            src_ref[rows, :states] + lre * hre - lim * him,
            src_ref[rows, states:] + lre * him + lim * hre,
        )
        low[r : r + CHUNKS, :states] = hre.astype(BF16)
        low[r : r + CHUNKS, states:] = him.astype(BF16)
        state_ref[rows, :] = low[r : r + CHUNKS, :]
        h[0], h[1] = hre, him

    def gelu_piece(b, mix, r):
        rows = tile_rows(step, b * BLOCK + r)
        for c in range(0, width, 128):
            cols = slice(c, c + 128)
            normed = xhat_ref[rows, cols] * gain_ref[:, cols] + bias_ref[:, cols]
            lru = mix[r : r + 16, cols] + skip_ref[:, cols] * normed
            act, slope = gelu_parts(lru)
            act_ref[rows, cols] = act.astype(BF16)
            slope_ref[rows, cols] = slope

    def scans(b, low):
        return [partial(scan_piece, b, low, r) for r in range(0, BLOCK, CHUNKS)]

    def mixes(low, mix):
        return product_nn(mix, lambda: low[...], wc_ref)

    def gelus(b, mix):
        return [partial(gelu_piece, b, mix, r) for r in range(0, BLOCK, 16)]

    blocks = src_ref.shape[0] // BLOCK
    lows, mix_refs = (low_a, low_b), (mix_a, mix_b)
    run(scans(0, low_a))
    for b in range(blocks):
        other = scans(b + 1, lows[(b + 1) % 2]) if b + 1 < blocks else []
        other = (gelus(b - 1, mix_refs[(b - 1) % 2]) if b else []) + other
        alternate(mixes(lows[b % 2], mix_refs[b % 2]), other)
    run(gelus(blocks - 1, mix_refs[(blocks - 1) % 2]))


def gating(mp, idx, cotlow_ref, act_ref, rows_ref, own_ref, other_ref,
           br_ref, gpre_ref, wg_ref, vec_ref, pre_a, pre_b):
    width = act_ref.shape[1]
    core = idx[1]
    assemble(wg_ref, own_ref, other_ref, width // 2 // mp, width // mp, idx[0], core, mp, False)
    vec_ref[...] = jnp.zeros_like(vec_ref)
    blocks = act_ref.shape[0] // BLOCK
    buffers = (pre_a, pre_b)

    def pre_pieces(b):
        return product_nt(buffers[b % 2], lambda: act_ref[b * BLOCK : (b + 1) * BLOCK, :], wg_ref) if b < blocks else []

    sums = {}

    def gate_piece(b, start, c):
        pre = buffers[b % 2]
        cols = slice(c, c + 128)
        gate_cols = slice(width + c, width + c + 128)
        for r in range(start, start + 64, 16):
            rows = slice(b * BLOCK + r, b * BLOCK + r + 16)
            value = pre[r : r + 16, cols] + rows_ref[1:2, cols]
            gate = pre[r : r + 16, gate_cols] + rows_ref[2:3, cols]
            sig = 0.5 * jnp.tanh(0.5 * gate) + 0.5
            branch = value * sig
            br_ref[rows, cols] = branch.astype(BF16)
            g = cotlow_ref[rows, cols].astype(F32)
            g_value = g * sig
            g_gate = g * branch * (1.0 - sig)
            gpre_ref[rows, cols] = g_value.astype(BF16)
            gpre_ref[rows, gate_cols] = g_gate.astype(BF16)
            for key, part in ((("value", c), g_value), (("gate", c), g_gate)):
                sums[key] = sums[key] + part if key in sums else part

    def gate_pieces(b):
        return [partial(gate_piece, b, start, c) for start in range(0, BLOCK, 64) for c in range(0, width, 128)]

    run(pre_pieces(0))
    for b in range(blocks):
        alternate(pre_pieces(b + 1), gate_pieces(b))
        for c in range(0, width, 128):
            vec_ref[1:2, c : c + 128] += jnp.sum(sums.pop(("value", c)), 0, keepdims=True)
            vec_ref[2:3, c : c + 128] += jnp.sum(sums.pop(("gate", c)), 0, keepdims=True)


def weight_products(idx, gpre_ref, act_ref, state_ref, gmix_ref, keep_ref, send_ref):
    core = idx[1]

    def product(left_ref, right_ref, first):
        columns = left_ref.shape[1]
        size = columns // 2
        for n in range(0, columns, 256):
            total = tn(left_ref[:, n : n + 256], right_ref[...])
            here = slice(first + n % size, first + n % size + 256)

            @pl.when(core == n // size)
            def _():
                keep_ref[here, :] = total

            @pl.when(core != n // size)
            def _():
                send_ref[here, :] = total.astype(BF16)

    product(gpre_ref, act_ref, 0)
    product(state_ref, gmix_ref, gpre_ref.shape[1] // 2)


def unmix(idx, gpre_ref, slope_ref, norm_ref, wg_ref, wc_ref, par_ref,
          gmix_ref, gs_ref, adj_ref, first_ref, vec_ref, ga_a, ga_b, gmix_a, gmix_b, gs_a, gs_b):
    step = 0
    width = norm_ref.shape[1]
    states = width // 2
    core = idx[1]

    vec_ref[...] = jnp.zeros_like(vec_ref)
    sums = {}

    def act_pieces(b, ga):
        return product_nn(ga, lambda: gpre_ref[block_rows(step, b), :], wg_ref)

    def lru_piece(b, ga, gmix, r):
        rows = tile_rows(step, b * BLOCK + r)
        for c in range(0, width, 128):
            cols = slice(c, c + 128)
            g_lru = ga[r : r + 16, cols] * slope_ref[rows, cols]
            low = g_lru.astype(BF16)
            gmix[r : r + 16, cols] = low
            gmix_ref[rows, cols] = low
            part = g_lru * norm_ref[rows, cols].astype(F32)
            sums[c] = sums[c] + part if c in sums else part

    def lru_pieces(b, ga, gmix):
        return [partial(lru_piece, b, ga, gmix, r) for r in range(0, BLOCK, 16)]

    def mix_pieces(b, gs, gmix):
        return product_nt(gs, lambda: gmix[...], wc_ref)

    lre, lim = par_ref[0:1, :states], par_ref[0:1, states:]
    power = [jnp.ones((8, states), F32), jnp.zeros((8, states), F32)]
    are = [jnp.zeros((8, states), F32) for _ in range(0, CHUNKS, 8)]
    aim = [jnp.zeros((8, states), F32) for _ in range(0, CHUNKS, 8)]

    def end_piece(b, gs, r):
        pre, pim = power
        for n, c in enumerate(range(0, CHUNKS, 8)):
            gre, gim = gs[r + c : r + c + 8, :states], gs[r + c : r + c + 8, states:]
            mre, mim = cmul(pre, pim, gre, gim)
            are[n], aim[n] = are[n] + mre, aim[n] + mim
        gs_ref[tile_rows(step, b * BLOCK + r), :] = gs[r : r + CHUNKS, :]
        power[0], power[1] = pre * lre + pim * lim, pim * lre - pre * lim

    def end_pieces(b, gs):
        return [partial(end_piece, b, gs, r) for r in range(0, BLOCK, CHUNKS)]

    blocks = gpre_ref.shape[0] // BLOCK
    gas, gmixes, gss = (ga_a, ga_b), (gmix_a, gmix_b), (gs_a, gs_b)
    run(act_pieces(0, ga_a))
    for b in range(blocks + 2):
        products = act_pieces(b + 1, gas[(b + 1) % 2]) if b + 1 < blocks else []
        products += mix_pieces(b - 1, gss[(b - 1) % 2], gmixes[(b - 1) % 2]) if 0 <= b - 1 < blocks else []
        other = lru_pieces(b, gas[b % 2], gmixes[b % 2]) if b < blocks else []
        other += end_pieces(b - 2, gss[b % 2]) if b >= 2 else []
        alternate(products, other)
    for c in range(0, width, 128):
        vec_ref[0:1, c : c + 128] += jnp.sum(sums[c], 0, keepdims=True)
    for n, c in enumerate(range(0, CHUNKS, 8)):
        adj_ref[c : c + 8, :states] = are[n]
        adj_ref[c : c + 8, states:] = aim[n]
    lre, lim = par_ref[2:3, :states], -par_ref[2:3, states:]
    last = CHUNKS - 1
    re, im = adj_ref[last : last + 1, :states], adj_ref[last : last + 1, states:]
    for c in range(CHUNKS - 2, -1, -1):
        mre, mim = cmul(lre, lim, re, im)
        re, im = mre + adj_ref[c : c + 1, :states], mim + adj_ref[c : c + 1, states:]
    first_ref[...] = jnp.broadcast_to(jnp.concatenate([re, im], 1), first_ref.shape)


def adjoint_scan(mp, idx, gs_ref, state_ref, src_ref, norm_ref, par_ref, adj_ref, *rest):
    others = rest[: mp - 1]
    (gdrive_ref, keep_ref, send_ref, vec_ref, acc_ref, h_ref, gdrive_a, gdrive_b) = rest[mp - 1 :]
    step = 0
    width = gs_ref.shape[1]
    states = width // 2
    me, core = idx[0], idx[1]

    re = jnp.zeros((1, states), F32)
    im = jnp.zeros((1, states), F32)
    for s in range(1, mp):
        j = me ^ s
        power = jnp.maximum(j - me - 1, 0)
        row = par_ref[pl.ds(8 + power, 1), :]
        sre, sim = cmul(row[:, :states], -row[:, states:], others[s - 1][0:1, :states], others[s - 1][0:1, states:])
        keep = (j > me).astype(F32)
        re, im = re + keep * sre, im + keep * sim
    lre, lim = par_ref[2:3, :states], -par_ref[2:3, states:]
    for c in range(CHUNKS - 1, -1, -1):
        h_ref[c : c + 1, :states] = re
        h_ref[c : c + 1, states:] = im
        mre, mim = cmul(lre, lim, re, im)
        re, im = mre + adj_ref[c : c + 1, :states], mim + adj_ref[c : c + 1, states:]
    acc_ref[...] = jnp.zeros_like(acc_ref)

    lre, lim = par_ref[0:1, :states], par_ref[0:1, states:]
    gam = par_ref[1:2, :states]
    h = [h_ref[:, :states], h_ref[:, states:]]
    sums = [jnp.zeros((CHUNKS, states), F32)] * 3

    def scan_piece(b, gdrive, r):
        hre, him = h
        rows = tile_rows(step, b * BLOCK + r)
        tre, tim = state_ref[rows, :states].astype(F32), state_ref[rows, states:].astype(F32)
        sums[0] = sums[0] + (hre * tre + him * tim)
        sums[1] = sums[1] + (him * tre - hre * tim)
        hre, him = (
            gs_ref[rows, :states] + lre * hre + lim * him,
            gs_ref[rows, states:] + lre * him - lim * hre,
        )
        sums[2] = sums[2] + (hre * src_ref[rows, :states] + him * src_ref[rows, states:])
        gdrive[r : r + CHUNKS, :states] = (hre * gam).astype(BF16)
        gdrive[r : r + CHUNKS, states:] = (him * gam).astype(BF16)
        gdrive_ref[rows, :] = gdrive[r : r + CHUNKS, :]
        h[0], h[1] = hre, him

    def scans(b, gdrive):
        return [partial(scan_piece, b, gdrive, r) for r in range(BLOCK - CHUNKS, -1, -CHUNKS)]

    def weight_pieces(b, gdrive):
        return product_tn(acc_ref, lambda cols: gdrive[:, cols], lambda: norm_ref[block_rows(step, b), :])

    last = gs_ref.shape[0] // BLOCK - 1
    buffers = (gdrive_a, gdrive_b)
    run(scans(last, buffers[last % 2]))
    for b in range(last - 1, -1, -1):
        alternate(weight_pieces(b + 1, buffers[(b + 1) % 2]), scans(b, buffers[b % 2]))
    run(weight_pieces(0, buffers[0]))
    keep_ref[...] = acc_ref[pl.ds(core * states, states), :]
    send_ref[...] = acc_ref[pl.ds((1 - core) * states, states), :].astype(BF16)
    sre, sim, sgam = [jnp.sum(v, 0, keepdims=True) for v in sums]
    vec_ref[0:1, :] = jnp.concatenate([sre, sim], 1)
    vec_ref[1:2, :] = jnp.concatenate([sgam, jnp.zeros((1, states), F32)], 1)
    vec_ref[2:8, :] = jnp.zeros((6, width), F32)


def norm_back(idx, cot_ref, gdrive_ref, wt_ref, gmix_ref, xhat_ref, rstd_ref, gain_ref, skip_ref, x_ref, br_ref,
              vec_skip_ref, vec_glu_ref, vec_lam_ref, gx_ref, y_ref, parts_ref, send_ref, gn_a, gn_b, dx_ref, vec_ref):
    step = pl.program_id(0)
    width = cot_ref.shape[2]
    per = STEP_ROWS // CHUNKS

    @pl.when(step == 0)
    def _():
        vec_ref[...] = jnp.zeros_like(vec_ref)

    def normed_pieces(block, gn):
        rows = pl.ds(pl.multiple_of(block * BLOCK, BLOCK), BLOCK)
        return product_nn(gn, lambda: gdrive_ref[rows, :], wt_ref)

    @pl.when(step == 0)
    def _():
        run(normed_pieces(0, gn_a))

    sums = [jnp.zeros((16, width), F32), jnp.zeros((16, width), F32)]

    def norm_piece(b, gn, r):
        rows = tile_rows(step, b * BLOCK + r)
        xhat = xhat_ref[rows, :]
        g = gn[r : r + 16, :] + skip_ref[...] * gmix_ref[rows, :].astype(F32)
        sums[0] = sums[0] + g * xhat
        sums[1] = sums[1] + g
        gh = g * gain_ref[...]
        first = jnp.mean(gh, -1, keepdims=True)
        second = jnp.mean(gh * xhat, -1, keepdims=True)
        rstd = jnp.concatenate([rstd_ref[rows, :]] * (width // 128), 1)
        dx_ref[b * BLOCK + r : b * BLOCK + r + 16, :] = rstd * (gh - first - xhat * second)

    def norm_pieces(b, gn):
        return [partial(norm_piece, b, gn, r) for r in range(0, BLOCK, 16)]

    def output_piece(k):
        rows = dx_ref[k * CHUNKS : (k + 8) * CHUNKS, :].reshape(8, CHUNKS, width)
        place = pl.ds(pl.multiple_of(step * per + k, 8), 8)
        gx_ref[:, k : k + 8, :] = cot_ref[:, place, :] + jnp.swapaxes(rows, 0, 1)

    def branch_piece(k):
        here = pl.ds(pl.multiple_of(step * STEP_ROWS + k * CHUNKS, 128), 8 * CHUNKS)
        rows = br_ref[here, :].astype(F32).reshape(8, CHUNKS, width)
        y_ref[:, k : k + 8, :] = x_ref[:, k : k + 8, :] + jnp.swapaxes(rows, 0, 1)

    after = jnp.minimum(2 * step + 2, gdrive_ref.shape[0] // BLOCK - 1)
    outputs = [partial(output_piece, k) for k in range(0, per, 8)]
    branches = [partial(branch_piece, k) for k in range(0, per, 8)]
    alternate(normed_pieces(2 * step + 1, gn_b), branches + norm_pieces(0, gn_a))
    alternate(normed_pieces(after, gn_a), outputs[: len(outputs) // 2] + norm_pieces(1, gn_b) + outputs[len(outputs) // 2 :])
    vec_ref[0:1, :] += jnp.sum(sums[0], 0, keepdims=True)
    vec_ref[1:2, :] += jnp.sum(sums[1], 0, keepdims=True)

    @pl.when(step == pl.num_programs(0) - 1)
    def _():
        rows = [vec_skip_ref[0:1, :], vec_glu_ref[1:3, :], vec_ref[0:2, :], vec_lam_ref[0:2, :], jnp.zeros((1, width), F32)]
        vec = jnp.concatenate(rows, 0)
        high = vec.astype(BF16)
        low = (vec - high.astype(F32)).astype(BF16)
        parts_ref[...] = high.astype(F32) + low.astype(F32)
        send_ref[...] = jnp.concatenate([high.astype(F32), low.astype(F32)], 0).astype(BF16)


def pack_rows(idx, *refs):
    *parts, out = refs
    for i, part in enumerate(parts):
        out[i] = part[...]


def split_pieces(slots, count, hid, ns, idx, keep_ref, got_ref, in_keep_ref, in_got_ref, own_ref, *sends):
    place = idx[2]
    parts = ((keep_ref, got_ref, 0, hid), (keep_ref, got_ref, slots * hid, ns), (in_keep_ref, in_got_ref, 0, ns))
    height = (hid + 2 * ns) // count
    for slot in range(slots):
        for s in range(count):
            low = slot * height
            for keep, got, base, size in parts:
                rows = size // count
                start = pl.multiple_of(base + slot * size + (place ^ s) * rows, rows)
                piece = keep[pl.ds(start, rows), :] + got[pl.ds(start, rows), :].astype(F32)
                if s == 0:
                    own_ref[low : low + rows, :] = piece
                else:
                    sends[s - 1][low : low + rows, :] = piece.astype(BF16)
                low += rows


def finish(hid, ns, count, idx, own_ref, got_ref, nu_ref, theta_ref, in_ref, out_ref, glu_ref, *rest):
    *rest, rows_ref = rest
    core, place = idx[1], idx[2]
    height = (hid + 2 * ns) // count
    for part in range(2):
        for i in range(count):
            here = pl.ds(pl.multiple_of((i ^ place) * height, 16), height)
            rows = jnp.where(core == part, own_ref[here, :], got_ref[here, :]).astype(F32)
            low = 0
            for ref, size in ((rows_ref, hid // count), (out_ref, ns // count), (in_ref, ns // count)):
                value = rows[low : low + size]
                ref[part, i * size : (i + 1) * size, :] = -value if ref is out_ref and part == 1 else value
                low += size
        glu_ref[:, part, :] = rows_ref[part].T
    first = count * height
    both = [ref[first : first + 16, :].astype(F32) for ref in (own_ref, got_ref)]
    vec = (both[0][:8] + both[0][8:]) + (both[1][:8] + both[1][8:])
    vector_outputs(hid, ns, idx, vec, nu_ref, theta_ref, *rest)


def vector_outputs(hid, ns, idx, vec, nu_ref, theta_ref, gain_ref, bias_ref, skip_ref, nu_out, theta_out, gamma_out, glu_ref):
    me = idx[0]
    width = vec.shape[1]
    states = width // 2
    skip_ref[...] = vec[0:1, :]
    gain_ref[...] = vec[3:4, :]
    bias_ref[...] = vec[4:5, :]

    def share(rows, start, size, count):
        total = jnp.zeros((rows.shape[0], size), F32)
        for j in range(count):
            total = total + jnp.where(me == j, rows[:, start + j * size : start + (j + 1) * size], 0.0)
        return total

    glu_ref[...] = share(vec[1:3, :], 0, hid, width // hid)
    re = share(vec[5:6, :], 0, ns, states // ns)
    im = share(vec[5:6, :], states, ns, states // ns)
    gamma_out[...] = share(vec[6:7, :], 0, ns, states // ns)
    speed, turn = jnp.exp(nu_ref[...]), jnp.exp(theta_ref[...])
    radius = jnp.exp(-speed)
    cos, sin = radius * jnp.cos(turn), radius * jnp.sin(turn)
    nu_out[...] = -speed * (cos * re + sin * im)
    theta_out[...] = turn * (cos * im - sin * re)


def small_outputs(hid, ns, idx, vec_ref, *rest):
    vector_outputs(hid, ns, idx, vec_ref[...], *rest)


def call(kernel, steps, ins, outs, scratch, mib, flops, moved, in_place=None, first=False):
    def in_hbm(array, block):
        return array if block is None or (array.size < 65536 and not first) else pltpu.with_memory_space_constraint(array, pltpu.HBM)

    def spec(block):
        return pl.BlockSpec(memory_space=pltpu.VMEM) if block is None else block

    return pl.pallas_call(
        kernel,
        grid_spec=pltpu.PrefetchScalarGridSpec(
            num_scalar_prefetch=1,
            grid=(steps,),
            in_specs=[spec(block) for _, block in ins[1:]],
            out_specs=[spec(block) for _, _, block in outs],
            scratch_shapes=[pltpu.VMEM(*s) for s in scratch],
        ),
        out_shape=[jax.ShapeDtypeStruct(s, t) if block is None else pltpu.HBM(s, t) for s, t, block in outs],
        input_output_aliases=in_place or {},
        compiler_params=pltpu.CompilerParams(vmem_limit_bytes=mib * MIB),
        cost_estimate=pl.CostEstimate(flops=flops, bytes_accessed=moved * MIB, transcendentals=0),
    )(*[in_hbm(a, block) for a, block in ins])


def xor_pairs(n, s):
    return [(i, i ^ s) for i in range(n)]


def from_each(value, axis, n):
    return [value] + [lax.ppermute(value, axis, xor_pairs(n, s)) for s in range(1, n)]


def tree_sum(parts):
    parts = list(parts)
    while len(parts) > 1:
        parts = [parts[i] + parts[i + 1] for i in range(0, len(parts), 2)]
    return parts[0]


def high_low(v):
    high = lax.reduce_precision(v, 8, 7)
    return high, lax.reduce_precision(v - high, 8, 7)


def vector_rows(v):
    high, low = high_low(v)
    return high + low, jnp.concatenate([high, low]).astype(BF16)


def vector_sum(rows):
    n = rows.shape[0] // 2
    return rows[:n].astype(F32) + rows[n:].astype(F32)


def flip(stack, position):
    n = stack.shape[0]
    for b in range(log2_of(n)):
        pairs = stack.reshape((n >> (b + 1), 2, 1 << b) + stack.shape[1:])
        pairs = jnp.where((position >> b) & 1 == 1, pairs[:, ::-1], pairs)
        stack = pairs.reshape(stack.shape)
    return stack


def on_device(
    block_input, ln_gain, ln_bias, nu_log, theta_log, gamma_log, in_weight, out_weight, skip, glu_weight, glu_bias,
    out_cotangent,
):
    mp = lax.axis_size("mp")
    dp = lax.axis_size("dp")
    plane = dp // 2
    me = lax.axis_index("mp")
    dpi = lax.axis_index("dp")
    core = dpi & 1
    place = dpi >> 1
    idx = jnp.stack([me, core, place]).astype(jnp.int32)
    tokens, width = block_input.shape[1:]
    ns = nu_log.shape[0]
    states = ns * mp
    hid = glu_weight.shape[2]
    chunk = tokens // CHUNKS
    per = STEP_ROWS // CHUNKS
    steps = tokens // STEP_ROWS
    x = block_input.reshape(CHUNKS, chunk, width)
    cot = out_cotangent.reshape(CHUNKS, chunk, width)
    gain, bias, skp = ln_gain[None], ln_bias[None], skip[None]

    def over_core(v):
        return lax.ppermute(v, "dp", xor_pairs(dp, 1))

    def over_plane(v, s):
        return lax.ppermute(v, "dp", xor_pairs(dp, 2 * s))

    def over_mp(v, s):
        return lax.ppermute(v, "mp", xor_pairs(mp, s))

    here = (jnp.arange(mp) == me).astype(F32)[:, None]

    def placed(v):
        return (here * v[None]).reshape(-1)

    def thirds(v):
        high, rest = high_low(v)
        return [high, rest, lax.reduce_precision(v - high - rest, 8, 7)]

    first_rows = [placed(nu_log), placed(gamma_log)], [placed(theta_log), placed(gamma_log)]
    first_rows = jnp.concatenate([jnp.stack(v) for v in first_rows], 1)
    first_rows = lax.optimization_barrier(first_rows)
    params = jnp.concatenate(thirds(first_rows)).astype(BF16)
    params = jnp.pad(params, ((0, PARAM_ROWS - params.shape[0]), (0, 0)))

    def gathered(value, name):
        with jax.named_scope(name):
            return [value] + [over_mp(value, s) for s in range(1, mp)]

    def packed(parts, *earlier):
        value = parts[0]
        parts = lax.optimization_barrier(tuple(parts) + earlier)[: len(parts)]
        shape = (mp,) + value.shape
        return call(pack_rows, 1, [(idx, None)] + [(p, None) for p in parts], [(shape, value.dtype, None)], [], 1, 0, 0)[0]

    def tied(value, *earlier):
        return lax.optimization_barrier((value,) + earlier)[0]

    in_part = lax.dynamic_index_in_dim(in_weight, core, 1, keepdims=False).T
    out_part = lax.dynamic_index_in_dim(out_weight, core, 0, keepdims=False)
    glu_part = lax.dynamic_index_in_dim(glu_weight, core, 1, keepdims=False).T
    in_send = jnp.concatenate([in_part, params])
    both_part = jnp.concatenate([out_part, glu_part])
    x = tied(x, in_send, both_part)
    in_parts = gathered(in_send, "gather_in")

    chunked = pl.BlockSpec((CHUNKS, per, width), lambda i, idx: (0, i, 0))
    vector = pl.BlockSpec((1, width), lambda i, idx: (0, 0))
    rowed = pl.BlockSpec((STEP_ROWS, width), lambda i, idx: (i, 0))
    big = (tokens, width)
    npar = 8 + mp
    product = 2 * tokens * width * width
    small = ((8, width), F32, None)

    def scratch(*kinds):
        return [((rows, cols), kind) for rows, cols, kind in kinds]

    xhat, norm, rstd = call(
        prepare, steps,
        [(idx, None), (x, chunked), (gain, vector), (bias, vector)],
        [(big, F32, None), (big, BF16, None), ((tokens, 128), F32, None)],
        [], 6, product, 12, None, True,
    )
    in_parts = list(lax.optimization_barrier(tuple(in_parts) + (norm,))[:-1])
    both_own = gathered(tied(both_part, *in_parts[1:]), "gather_out_glu")
    in_own = packed(in_parts, norm)
    in_other = over_core(in_own)
    (cotlow,) = call(lower, steps, [(idx, None), (tied(cot, in_own), chunked)], [(big, BF16, None)], [], 5, 0, 8)
    norm = tied(norm, cotlow)
    src, wt, par, ends, last = call(
        partial(first_scan, chunk, mp), 1,
        [(idx, None), (norm, None), (in_own, None), (in_other, None), (glu_bias, None)],
        [(big, F32, None), ((width, width), BF16, None), ((npar, width), F32, None), ((CHUNKS, width), F32, None), small],
        scratch((CHUNKS, width, F32), (BLOCK, width, F32), (BLOCK, width, F32)), 5, product, 8,
    )
    with jax.named_scope("carry"):
        lasts = [over_mp(last, s) for s in range(1, mp)]
    both_own = packed(both_own, *lasts)
    both_other = over_core(both_own)
    state, act, slope, wc, bias_rows = call(
        partial(readout, mp), 1,
        [(idx, None), (xhat, None), (src, None), (par, None), (ends, None), (gain, vector), (bias, vector), (skp, vector),
         (both_own, None), (both_other, None)] + [(v, None) for v in lasts + [last]],
        [(big, BF16, None), (big, BF16, None), (big, F32, None), ((width, width), BF16, None), small],
        scratch((CHUNKS, width, F32), (BLOCK, width, BF16), (BLOCK, width, BF16), (BLOCK, width, F32), (BLOCK, width, F32)), 8, product, 8,
    )
    branch, gpre, wg, vec_glu = call(
        partial(gating, mp), 1,
        [(idx, None), (cotlow, None), (act, None), (bias_rows, None), (both_own, None), (both_other, None)],
        [(big, BF16, None), ((tokens, 2 * width), BF16, None), ((2 * width, width), BF16, None), small],
        scratch((BLOCK, 2 * width, F32), (BLOCK, 2 * width, F32)),
        10, 2 * product, 8,
    )
    gmix, gs, adj, first, vec_skip = call(
        unmix, 1,
        [(idx, None), (gpre, None), (slope, None), (norm, None), (wg, None), (wc, None), (par, None)],
        [(big, BF16, None), (big, F32, None), ((CHUNKS, width), F32, None), small, small],
        scratch((BLOCK, width, F32), (BLOCK, width, F32), (BLOCK, width, BF16),
                (BLOCK, width, BF16), (BLOCK, width, F32), (BLOCK, width, F32)),
        10, 4 * product, 8,
    )
    with jax.named_scope("carry_back"):
        firsts = [over_mp(first, s) for s in range(1, mp)]
    early_rows = mp * (hid + ns)
    sums = [((early_rows, width), F32, None), ((early_rows, width), BF16, None)]
    keep, send = call(
        weight_products, 1,
        [(idx, None), (tied(gpre, first), None), (act, None), (state, None), (gmix, None)],
        sums, [], 12, 0, 0,
    )
    firsts[0] = tied(firsts[0], send)
    with jax.named_scope("sum_early_core"):
        got = over_core(tied(send, *firsts))
    gdrive, in_keep, in_send, vec_lam = call(
        partial(adjoint_scan, mp), 1,
        [(idx, None), (gs, None), (state, None), (src, None), (norm, None), (par, None),
         (adj, None)] + [(v, None) for v in firsts],
        [(big, BF16, None), ((states, width), F32, None), ((states, width), BF16, None), small],
        scratch((width, width, F32), (CHUNKS, width, F32), (BLOCK, width, BF16),
                (BLOCK, width, BF16)), 8, product, 8,
    )
    with jax.named_scope("sum_in_core"):
        in_got = over_core(in_send)
    got = tied(got, gdrive)
    height = mp * (hid + 2 * ns) // plane
    if ns // plane % 16 == 0 and hid // plane % 16 == 0:
        own_piece, *sends = call(
            partial(split_pieces, mp, plane, hid, ns), 1,
            [(idx, None), (keep, None), (got, None), (in_keep, None), (in_got, None)],
            [((height, width), F32, None)] + [((height, width), BF16, None)] * (plane - 1), [], 4, 0, 0,
        )
    else:
        both = keep + got.astype(F32)
        both = [both[: mp * hid], both[mp * hid :], in_keep + in_got.astype(F32)]
        both = jnp.concatenate([v.reshape(mp, plane, -1, width) for v in both], 2).swapaxes(0, 1)
        sends = [lax.dynamic_index_in_dim(both, place ^ s, 0, keepdims=False) for s in range(plane)]
        sends = [v.reshape(-1, width) for v in sends]
        own_piece, sends = sends[0], [v.astype(BF16) for v in sends[1:]]
    with jax.named_scope("sum_plane"):
        pieces = [over_plane(v, s + 1) for s, v in enumerate(sends)]
    gx, y, vec, vec_rows = call(
        norm_back, steps,
        [(idx, None), (cot, None), (tied(gdrive, own_piece), None), (wt, None), (gmix, None), (xhat, None), (rstd, None),
         (gain, vector), (skp, vector), (x, chunked), (branch, None), (vec_skip, None), (vec_glu, None),
         (vec_lam, None)],
        [((CHUNKS, chunk, width), F32, chunked), ((CHUNKS, chunk, width), F32, chunked), small, ((16, width), BF16, None)],
        scratch((BLOCK, width, F32), (BLOCK, width, F32), (STEP_ROWS, width, F32), (8, width, F32)), 18, product, 8,
    )
    pieces[0], own_piece, nu_log, theta_log, me, core, place = lax.optimization_barrier(
        (pieces[0], own_piece, nu_log, theta_log, me, core, place, vec)
    )[:7]
    rows = tree_sum([own_piece] + [p.astype(F32) for p in pieces]).reshape(mp, -1, width)
    with jax.named_scope("sum_mp"):
        got, vecs = [lax.dynamic_index_in_dim(rows, me, 0, keepdims=False)], [vec]
        n = got[0].shape[0]
        for s in range(1, mp):
            send = lax.dynamic_index_in_dim(rows, me ^ s, 0, keepdims=False).astype(BF16)
            buffer = over_mp(jnp.concatenate([send, vec_rows]), s)
            got.append(buffer[:n].astype(F32))
            vecs.append(vector_sum(buffer[n:]))
    piece, vec = tree_sum(got).astype(BF16), tree_sum(vecs)
    with jax.named_scope("spread_plane"):
        vec, vec_rows = vector_rows(vec)
        piece = jnp.concatenate([piece, vec_rows])
        stack = [piece] + [over_plane(piece, s) for s in range(1, plane)]
    vec = tree_sum([vec] + [vector_sum(v[n:]) for v in stack[1:]])
    vec, vec_rows = vector_rows(vec)
    own = jnp.concatenate([v[:n] for v in stack] + [vec_rows])
    with jax.named_scope("spread_core"):
        got = over_core(own)
    line = pl.BlockSpec((1, width), lambda i, idx: (0, 0))
    share = pl.BlockSpec((1, ns), lambda i, idx: (0, 0))
    shared = [((1, width), F32, line)] * 3 + [((1, ns), F32, share)] * 3
    shared.append(((2, hid), F32, pl.BlockSpec((2, hid), lambda i, idx: (0, 0))))
    logs = [(nu_log[None], None), (theta_log[None], None)]
    if ns // plane % 16 == 0 and hid // plane % 16 == 0:
        whole = pl.BlockSpec((2, ns, width), lambda i, idx: (0, 0, 0))
        grad_in, grad_out_weight, grad_glu, *vectors = call(
            partial(finish, hid, ns, plane), 1,
            [(idx, None), (own, None), (got, None)] + logs,
            [((2, ns, width), F32, whole), ((2, ns, width), F32, whole), ((width, 2, hid), F32, pl.BlockSpec((width, 2, hid), lambda i, idx: (0, 0, 0)))] + shared,
            [((2, hid, width), F32)], 8, 0, 0,
        )
    else:
        vec = vec + vector_sum(got[plane * n :])
        vectors = call(partial(small_outputs, hid, ns), 1, [(idx, None), (vec, None)] + logs, shared, [], 2, 0, 0)
        pieces = [flip(v[: plane * n].reshape(plane, n, width), place) for v in (own, got)]
        total = flip(jnp.stack(pieces), core).astype(F32)
        nh, nr = hid // plane, ns // plane

        def part(start, size):
            return total[:, :, start : start + size].reshape(2, -1, width)

        grad_glu, grad_out, grad_in = part(0, nh).transpose(2, 0, 1), part(nh, nr), part(nh + nr, nr)
        grad_out_weight = jnp.stack([grad_out[0], -grad_out[1]])
    grad_ln_gain, grad_ln_bias, grad_skip, grad_nu, grad_theta, grad_gamma, grad_glu_bias = vectors
    return (
        y.reshape(block_input.shape),
        gx.reshape(block_input.shape),
        grad_ln_gain[0],
        grad_ln_bias[0],
        grad_nu[0],
        grad_theta[0],
        grad_gamma[0],
        grad_in.transpose(2, 0, 1),
        grad_out_weight,
        grad_skip[0],
        grad_glu,
        grad_glu_bias,
    )


def solution(mesh):
    in_specs = (
        P("dp", "mp", None), P(), P(), P("mp"), P("mp"), P("mp"), P(None, None, "mp"), P(None, "mp", None), P(),
        P(None, None, "mp"), P(None, "mp"), P("dp", "mp", None),
    )
    out_specs = (
        P("dp", "mp", None), P("dp", "mp", None), P(), P(), P("mp"), P("mp"), P("mp"), P(None, None, "mp"),
        P(None, "mp", None), P(), P(None, None, "mp"), P(None, "mp"),
    )
    return jax.shard_map(on_device, mesh=mesh, in_specs=in_specs, out_specs=out_specs, check_vma=False)
```
